32 devices in a mesh: lat: 4 (over z), lon: 8 (over y, x, core).
Axes of the slice: x: 2, y: 2, z: 4, core: 2. Of those that a mesh axis runs over, the one named last changes fastest.
Arguments:
- patches: bfloat16 [6144, 1536], P(('lat', 'lon')), may hold values from -6 to 6
- requests: int32 [4, 4096], P('lat', 'lon'), may hold values from 0 to 191, as said below
- footprint: int32 [256, 64], P('lat', 'lon'), may hold values from -1 to 511, as said below
- weight_index: int32 [256, 64], P('lat', 'lon'), may hold values from 0 to 15
- composite_weights: float32 [16], replicated, may hold values from 0.1 to 1
- labels: int32 [256, 1024], P('lat', 'lon'), may hold values from 0 to 10
- conv1_weight: bfloat16 [9, 64, 12], replicated, may hold values from -0.625 to 0.625
- conv2_weight: bfloat16 [9, 64, 64], replicated, may hold values from -0.25 to 0.25
- head_weight: bfloat16 [11, 64], replicated, may hold values from -0.75 to 0.75
Outputs:
- skip_features: bfloat16 [64, 256, 1024], P(None, 'lat', 'lon')
- grad_conv1: float32 [9, 64, 12], replicated
- grad_conv2: float32 [9, 64, 64], replicated
- grad_head: float32 [11, 64], replicated
- loss: float32 [], replicated
The draws below stay inside these ranges and needn't reach their ends.
Inputs may be any that keep to these rules, and one draw needn't show every extreme that they name: `requests`: every entry is a row offset into the store of the device at the same lat index and lon index b. `footprint`: an entry that is not -1 is b*64 + p, position p of the bucket that the tile takes from lon index b. Slot 0 is never -1. In one tile no two entries are equal, and in some tiles every position of every bucket is named.
All inputs are finite; a program needn't handle non-finite values.
Results may differ from the reference program's by a relative error of at most 0.0055.
Values may be sent and summed in bfloat16 or wider, within the bound.
No kernel may reach another device: no remote copies, remote signals or barrier semaphores. Data moves between devices by JAX's collectives and lax.ppermute only.
A program may use at most 64 MiB of HBM per device.

```python
import math
import jax
import jax.numpy as jnp
from jax import lax

TILE_ROWS = 64
PATCH_PX = 128
BANDS = 12
FEAT = 64
NCLASS = 11
SLOTS = 8
TAPS = 9
QUALITY = 16
STORE_DEV = 192
BUCKET = 64
IMG_ROWS = 256
IMG_COLS = 1024
N_LAT = 4
N_LON = 8


def routing_plan(key):
    tile_count = N_LAT * N_LON
    keys = [jax.random.fold_in(key, 101 + number) for number in range(6)]
    draw_level = jax.random.randint(keys[0], (tile_count,), 0, 65)
    scene_count = 1 + (SLOTS - 1) * draw_level * (draw_level + 64) // (2 * 64 * 64)
    tile_ids = jnp.arange(tile_count, dtype=jnp.int32)
    forced = tile_ids % N_LON == tile_ids // N_LON % N_LON
    scene_count = jnp.where(forced, SLOTS, scene_count)
    lon_ids = jnp.arange(N_LON, dtype=jnp.int32)
    scores = jax.random.randint(keys[1], (tile_count, N_LON), 0, 1 << 20) * N_LON + lon_ids[None, :]
    owners = jnp.argsort(scores, axis=1).astype(jnp.int32)
    slot_ids = jnp.arange(SLOTS, dtype=jnp.int32)
    row_ids = jnp.arange(TILE_ROWS, dtype=jnp.int32)
    starts = jax.random.randint(keys[3], (tile_count, SLOTS), 0, TILE_ROWS // 5 + 1)
    starts = jnp.where(forced[:, None] | (slot_ids[None, :] == 0), 0, starts)
    order = slot_ids[None, :] * TILE_ROWS + row_ids[:, None]
    run_index = order // BUCKET
    position = order % BUCKET
    owner_of = owners[:, run_index]
    in_use = (slot_ids[None, None, :] < scene_count[:, None, None]) & (row_ids[None, :, None] >= starts[:, None, :])
    foot_value = jnp.where(in_use, owner_of * BUCKET + position[None], -1)
    footprint = foot_value.reshape(N_LAT, N_LON, TILE_ROWS, SLOTS).transpose(0, 2, 1, 3).reshape(N_LAT * TILE_ROWS, N_LON * SLOTS)
    shifts = jax.random.randint(keys[2], (tile_count, N_LON), 0, BUCKET)
    bases = jax.random.randint(keys[4], (tile_count, N_LON), 0, STORE_DEV - BUCKET + 1)
    bases = jnp.where(forced[:, None] & (lon_ids[None, :] == 0), STORE_DEV - BUCKET, bases)
    bases = jnp.where(forced[:, None] & (lon_ids[None, :] == 1), 0, bases)
    bucket_ids = jnp.arange(BUCKET, dtype=jnp.int32)
    requests = bases[:, :, None] + (bucket_ids[None, None, :] + shifts[:, :, None]) % BUCKET
    return (footprint.astype(jnp.int32), requests.reshape(N_LAT, N_LON * N_LON * BUCKET).astype(jnp.int32))


def draw_requests(key, part):
    return routing_plan(key)[1]


def draw_footprint(key, part):
    return routing_plan(key)[0]


def touch_ends(entries, stream_key, least, top_value):
    index_at = [jax.random.randint(jax.random.fold_in(stream_key, axis), (), 0, length) for axis, length in enumerate(entries.shape)]
    widest = entries.shape.index(max(entries.shape))
    neighbour = index_at[:widest] + [(index_at[widest] + 1) % entries.shape[widest]] + index_at[widest + 1:]
    return entries.at[tuple(index_at)].set(least).at[tuple(neighbour)].set(top_value)


def shard_levels(own_key, extent, cuts, low, largest):
    def one(dim, parts):
        heights = jax.random.uniform(jax.random.fold_in(jax.random.fold_in(own_key, 6), dim), (parts,), jnp.float32, low / len(cuts), largest / len(cuts))
        return jnp.repeat(jnp.exp(heights), extent[dim] // parts).reshape((-1,) + (1,) * (len(extent) - dim - 1))

    factor_of = one(*cuts[0])
    for cut in cuts[1:]:
        factor_of = factor_of * one(*cut)
    return factor_of


def noise(rng, shape, spread, reach, shards=(), kind=jnp.bfloat16):
    drawn = spread * jax.random.normal(rng, shape, jnp.float32)
    if shards:
        drawn = drawn * shard_levels(rng, shape, shards, -0.22, 0.18)
    return jnp.clip(drawn, -reach, reach).astype(kind)


def setup_inputs(seed: int = 0) -> dict:
    seeds = jax.random.split(jax.random.key(seed), 10)
    patches = noise(seeds[0], (N_LAT * N_LON * STORE_DEV, BANDS * PATCH_PX), 1.0, 6.0, ((0, 32),))
    requests = draw_requests(jax.random.fold_in(seeds[9], 71), 0)
    footprint = draw_footprint(jax.random.fold_in(seeds[9], 71), 0)
    weight_index = touch_ends(jax.random.randint(seeds[3], (IMG_ROWS, N_LON * SLOTS), 0, QUALITY), jax.random.fold_in(seeds[3], 1), 0, QUALITY - 1).astype(jnp.int32)
    composite_weights = jnp.clip(jnp.exp(jax.random.uniform(seeds[4], (QUALITY,), jnp.float32, math.log(0.1), math.log(1.0))), 0.1, 1.0)
    labels = touch_ends(jax.random.randint(seeds[5], (IMG_ROWS, IMG_COLS), 0, NCLASS), jax.random.fold_in(seeds[5], 1), 0, NCLASS - 1).astype(jnp.int32)
    conv1_weight = noise(seeds[6], (TAPS, FEAT, BANDS), (TAPS * BANDS) ** -0.5, 0.625)
    conv2_weight = noise(seeds[7], (TAPS, FEAT, FEAT), (TAPS * FEAT) ** -0.5, 0.25)
    head_weight = noise(seeds[8], (NCLASS, FEAT), FEAT ** -0.5, 0.75)
    return {"patches": patches, "requests": requests, "footprint": footprint, "weight_index": weight_index, "composite_weights": composite_weights, "labels": labels, "conv1_weight": conv1_weight, "conv2_weight": conv2_weight, "head_weight": head_weight}


def silu_slope(pre_value):
    sigmoid_value = jax.nn.sigmoid(pre_value)
    return sigmoid_value * (1.0 + pre_value * (1.0 - sigmoid_value))

def conv_forward(padded, weight, out_rows, out_cols):
    channels = padded.shape[0]
    result = jnp.zeros((weight.shape[1], out_rows * out_cols), jnp.float32)
    for tap_index in range(TAPS):
        tap_row, tap_col = (tap_index // 3, tap_index % 3)
        window = padded[:, tap_row:tap_row + out_rows, tap_col:tap_col + out_cols].reshape(channels, out_rows * out_cols)
        result = result + jnp.dot(weight[tap_index], window, preferred_element_type=jnp.float32)
    return result.reshape(weight.shape[1], out_rows, out_cols)

def conv_adjoint(padded, weight, out_rows, out_cols):
    channels = padded.shape[0]
    result = jnp.zeros((weight.shape[2], out_rows * out_cols), jnp.float32)
    for tap_index in range(TAPS):
        tap_row, tap_col = (2 - tap_index // 3, 2 - tap_index % 3)
        window = padded[:, tap_row:tap_row + out_rows, tap_col:tap_col + out_cols].reshape(channels, out_rows * out_cols)
        result = result + lax.dot_general(weight[tap_index], window, (((0,), (0,)), ((), ())), preferred_element_type=jnp.float32)
    return result.reshape(weight.shape[2], out_rows, out_cols)

def weight_grad(slope, padded, out_rows, out_cols):
    channels = padded.shape[0]
    slope_flat = slope.reshape(slope.shape[0], out_rows * out_cols)
    grads = []
    for tap_index in range(TAPS):
        tap_row, tap_col = (tap_index // 3, tap_index % 3)
        window = padded[:, tap_row:tap_row + out_rows, tap_col:tap_col + out_cols].reshape(channels, out_rows * out_cols)
        grads.append(lax.dot_general(slope_flat, window, (((1,), (1,)), ((), ())), preferred_element_type=jnp.float32))
    return jnp.stack(grads)

def reference(patches, requests, footprint, weight_index, composite_weights, labels, conv1_weight, conv2_weight, head_weight):
    row_width = BANDS * PATCH_PX
    slot_lon = jnp.arange(N_LON * SLOTS, dtype=jnp.int32) // SLOTS

    def composite_strip(inputs):
        strip_index, foot_rows, level_rows, asked_rows = inputs
        entry_index = jnp.maximum(foot_rows, 0)
        source = entry_index // BUCKET
        offset = asked_rows[((slot_lon[None, :] * N_LON + source) * BUCKET + entry_index % BUCKET).astype(jnp.int32)]
        global_row = ((strip_index * N_LON + source) * STORE_DEV + offset).astype(jnp.int32)
        gathered = patches[global_row.reshape(-1)].reshape(TILE_ROWS, N_LON, SLOTS, row_width)
        slot_scale = jnp.where(foot_rows >= 0, composite_weights[level_rows], 0.0).reshape(TILE_ROWS, N_LON, SLOTS)
        blended = lax.optimization_barrier(jnp.sum(slot_scale[..., None] * gathered.astype(jnp.float32), axis=2))
        blended = blended / lax.optimization_barrier(jnp.sum(slot_scale, axis=2))[..., None]
        blended = blended.astype(jnp.bfloat16).reshape(TILE_ROWS, N_LON, BANDS, PATCH_PX)
        return blended.transpose(2, 0, 1, 3).reshape(BANDS, TILE_ROWS, IMG_COLS)
    strips = lax.map(composite_strip, (jnp.arange(N_LAT, dtype=jnp.int32), footprint.reshape(N_LAT, TILE_ROWS, N_LON * SLOTS), weight_index.reshape(N_LAT, TILE_ROWS, N_LON * SLOTS), requests))
    composite = strips.transpose(1, 0, 2, 3).reshape(BANDS, IMG_ROWS, IMG_COLS)
    band_pad = jnp.pad(composite, ((0, 0), (1, 1), (1, 1)))
    pre_one = conv_forward(band_pad, conv1_weight, IMG_ROWS, IMG_COLS)
    hidden_one = jax.nn.silu(pre_one).astype(jnp.bfloat16)
    hidden_pad = jnp.pad(hidden_one, ((0, 0), (1, 1), (1, 1)))
    pre_two = conv_forward(hidden_pad, conv2_weight, IMG_ROWS, IMG_COLS)
    skip_features = jax.nn.silu(pre_two).astype(jnp.bfloat16)
    skip_flat = skip_features.reshape(FEAT, IMG_ROWS * IMG_COLS)
    logits = jnp.dot(head_weight, skip_flat, preferred_element_type=jnp.float32)
    log_total = jnp.log(lax.optimization_barrier(jnp.sum(jnp.exp(logits), axis=0)))
    onehot = labels.reshape(-1)[None, :] == jnp.arange(NCLASS, dtype=jnp.int32)[:, None]
    loss_sum = jnp.sum(log_total - lax.optimization_barrier(jnp.sum(jnp.where(onehot, logits, 0.0), axis=0)))
    class_error = (jnp.exp(logits - log_total[None, :]) - onehot.astype(jnp.float32)).astype(jnp.bfloat16)
    grad_head = lax.dot_general(class_error, skip_flat, (((1,), (1,)), ((), ())), preferred_element_type=jnp.float32)
    back_two = lax.dot_general(head_weight, class_error, (((0,), (0,)), ((), ())), preferred_element_type=jnp.float32)
    slope_two = (back_two.reshape(FEAT, IMG_ROWS, IMG_COLS) * silu_slope(pre_two)).astype(jnp.bfloat16)
    grad_two = weight_grad(slope_two, hidden_pad, IMG_ROWS, IMG_COLS)
    slope_pad = jnp.pad(slope_two, ((0, 0), (1, 1), (1, 1)))
    back_one = conv_adjoint(slope_pad, conv2_weight, IMG_ROWS, IMG_COLS)
    slope_one = (back_one * silu_slope(pre_one)).astype(jnp.bfloat16)
    grad_one = weight_grad(slope_one, band_pad, IMG_ROWS, IMG_COLS)
    pixel_count = IMG_ROWS * IMG_COLS
    return (skip_features, grad_one / pixel_count, grad_two / pixel_count, grad_head / pixel_count, loss_sum / pixel_count)
```

```python
import functools

import jax
import jax.numpy as jnp
from jax import lax
from jax.experimental import pallas as pl
from jax.experimental.pallas import tpu as pltpu
from jax.sharding import PartitionSpec as P

BF16 = jnp.bfloat16
F32 = jnp.float32
GROUP = 16
VMEM_LIMIT = 40 * 1024 * 1024


def dot(left, right):
    return lax.dot_general(left, right, (((1,), (0,)), ((), ())), preferred_element_type=F32)


def dot_nt(left, right):
    return lax.dot_general(left, right, (((1,), (1,)), ((), ())), preferred_element_type=F32)


def iota(shape, dim):
    return lax.broadcasted_iota(jnp.int32, shape, dim)


def call(kernel, out_shape, scratch=(), **kwargs):
    return pl.pallas_call(
        kernel,
        out_shape=out_shape,
        scratch_shapes=list(scratch),
        compiler_params=pltpu.CompilerParams(vmem_limit_bytes=VMEM_LIMIT),
        **kwargs,
    )


def struct(shape, dtype):
    return jax.ShapeDtypeStruct(shape, dtype)


def plan_kernel(requests, footprint, weight_index, levels, labels, out):
    rows, slots = footprint.shape
    patch_cols = labels.shape[1]
    foot = footprint[...]
    level_of = weight_index[...]
    weight = jnp.zeros((rows, slots), F32)
    for level in range(levels.shape[0]):
        weight = jnp.where(level_of == level, levels[level], weight)
    weight = jnp.where(foot >= 0, weight, 0.0)
    weight = weight / jnp.sum(weight, axis=1, keepdims=True)
    foot = foot.astype(F32)
    out[...] = jnp.zeros_like(out)
    for group in range(rows // 8):
        base = group * 2 * slots
        out[0:8, base : base + slots] = foot[group * 8 : group * 8 + 8]
        out[0:8, base + slots : base + 2 * slots] = weight[group * 8 : group * 8 + 8]
    asked = requests[...].astype(F32)
    for part in range(requests.shape[1] // 128):
        out[8 + part : 9 + part, :] = asked[:, part * 128 : (part + 1) * 128]
    lane = iota((8, patch_cols), 1)
    side = iota((8, patch_cols), 0)
    pick = ((side == 0) & (lane == 0)) | ((side == 1) & (lane == patch_cols - 1))
    edges = dot_nt(jnp.where(pick, 1.0, 0.0).astype(BF16), labels[...].astype(F32).astype(BF16))
    out[12:13, 0:rows] = edges[0:1]
    out[12:13, rows : 2 * rows] = edges[1:2]


def partial_kernel(tile_rows, slots, bucket, bands, me_ref, plans, own, mate, *refs):
    count = plans.shape[0]
    store, row_width = own.shape
    patch_cols = row_width // bands
    chips = count // 2
    outs, (stored, edge, spread) = refs[:chips], refs[chips:]
    me = me_ref[0]
    chip, core = me // 2, me % 2
    stored[pl.ds(pl.multiple_of(core * store, 64), store), :] = own[...]
    stored[pl.ds(pl.multiple_of((1 - core) * store, 64), store), :] = mate[...]

    wanted = [patch_cols - 3, patch_cols - 2, patch_cols - 1, 0, 1, 2]
    row_id = iota((6 * GROUP, row_width), 0)
    lane_id = iota((6 * GROUP, row_width), 1)
    column = row_id // GROUP
    column_lane = jnp.where(column < 3, column + (patch_cols - 3), column - 3)
    band = row_id % GROUP
    pick = (lane_id == band * patch_cols + column_lane) & (band < bands)
    edge[...] = dot_nt(jnp.where(pick, 1.0, 0.0).astype(BF16), stored[...]).astype(BF16)

    zero_tile = jnp.zeros(spread.shape[1:], spread.dtype)
    spread[0] = zero_tile
    spread[count + 1] = zero_tile
    pair = 2 * bucket
    place = iota((8, pair), 1) + chip * pair
    target = place.astype(F32)
    store_row = iota((2 * store, pair), 0)
    store_base = jnp.where(iota((2 * store, pair), 1) >= bucket, store, 0)

    def one_tile(tile, carry):
        groups = []
        for group in range(tile_rows // 8):
            base = group * 2 * slots
            total = jnp.zeros((8, pair), F32)
            for slot in range(slots):
                entry = plans[tile, 0:8, base + slot : base + slot + 1]
                weight = plans[tile, 0:8, base + slots + slot : base + slots + slot + 1]
                total = total + jnp.where(entry == target, weight, 0.0)
            groups.append(total)
        at_place = jnp.concatenate(groups, axis=0)
        if pair == 128:
            asked = plans[tile, pl.ds(8 + chip, 1), :]
        else:
            start = chip * pair
            asked = plans[tile, pl.ds(8 + start // 128, 1), :]
            asked = pltpu.roll(jnp.broadcast_to(asked, (8, 128)), (128 - start % 128) % 128, 1)[0:1, 0:pair]
        hit = store_row == asked.astype(jnp.int32) + store_base
        hit = jnp.where(hit, 1.0, 0.0).astype(BF16)
        high = at_place.astype(BF16)
        low = (at_place - high.astype(F32)).astype(BF16)
        both = dot_nt(jnp.concatenate([high, low], axis=0), hit)
        over_rows = both[:tile_rows] + both[tile_rows:]
        high = over_rows.astype(BF16)
        low = (over_rows - high.astype(F32)).astype(BF16)
        spread[tile + 1, 0:tile_rows] = high
        spread[tile + 1, tile_rows : 2 * tile_rows] = low
        return carry

    lax.fori_loop(0, count, one_tile, 0, unroll=2)

    for move in range(chips):
        tile = 2 * jnp.bitwise_xor(chip, move) + core
        weights = spread[tile + 1]
        for start in range(0, row_width, 512):
            stop = min(start + 512, row_width)
            both = dot(weights, stored[:, start:stop])
            outs[move][:, start:stop] = (both[:tile_rows] + both[tile_rows:]).astype(BF16)
        left = dot_nt(edge[0 : 3 * GROUP], spread[tile])
        right = dot_nt(edge[3 * GROUP : 6 * GROUP], spread[tile + 2])
        tail = outs[move]
        tail[:, row_width:] = jnp.zeros((tile_rows, tail.shape[1] - row_width), BF16)
        tail[0 : 3 * GROUP, row_width : row_width + tile_rows] = (
            left[:, :tile_rows] + left[:, tile_rows:]
        ).astype(BF16)
        tail[0 : 3 * GROUP, row_width + tile_rows : row_width + 2 * tile_rows] = (
            right[:, :tile_rows] + right[:, tile_rows:]
        ).astype(BF16)


def composite_kernel(bands, me_ref, plans, labels, *refs):
    count = plans.shape[0]
    tile_rows, patch_cols = labels.shape
    chips = count // 2
    parts = refs[:chips]
    main, strips, upper, lower, bank, side, bundle = refs[chips:]
    row_width = bands * patch_cols
    me = me_ref[0]
    for band in range(bands):
        columns = slice(band * patch_cols, (band + 1) * patch_cols)
        total = parts[0][:, columns].astype(F32)
        for part in parts[1:]:
            total = total + part[:, columns].astype(F32)
        bank[band * tile_rows : (band + 1) * tile_rows, :] = total
    bank[bands * tile_rows : (bands + 1) * tile_rows, :] = labels[...].astype(F32)
    bank[(bands + 1) * tile_rows : GROUP * tile_rows, :] = jnp.zeros(
        ((GROUP - bands - 1) * tile_rows, patch_cols), F32
    )
    for row in range(tile_rows):
        main[:, row * patch_cols : (row + 1) * patch_cols] = bank[
            pl.ds(row, GROUP, stride=tile_rows), :
        ].astype(BF16)

    far = parts[0][0 : 3 * GROUP, row_width : row_width + 2 * tile_rows].astype(F32)
    for part in parts[1:]:
        far = far + part[0 : 3 * GROUP, row_width : row_width + 2 * tile_rows].astype(F32)
    side[...] = jnp.zeros_like(side)
    side[0 : 3 * GROUP, 3 : 3 + tile_rows] = far[:, :tile_rows]
    side[7 * GROUP : 10 * GROUP, 3 : 3 + tile_rows] = far[:, tile_rows:]
    before = plans[jnp.maximum(me - 1, 0), 12:13, tile_rows : 2 * tile_rows]
    after = plans[jnp.minimum(me + 1, count - 1), 12:13, 0:tile_rows]
    side[2 * GROUP + bands : 2 * GROUP + bands + 1, 3 : 3 + tile_rows] = before
    side[7 * GROUP + bands : 7 * GROUP + bands + 1, 3 : 3 + tile_rows] = after
    row_id = iota((4 * GROUP, patch_cols), 0)
    lane_id = iota((4 * GROUP, patch_cols), 1)
    near = jnp.zeros((4 * GROUP, tile_rows), F32)
    column = row_id // GROUP
    column_lane = jnp.where(column < 2, column, column + (patch_cols - 4))
    for band in range(bands):
        pick = (row_id % GROUP == band) & (lane_id == column_lane)
        tile = bank[band * tile_rows : (band + 1) * tile_rows, :].astype(BF16)
        near = near + dot_nt(jnp.where(pick, 1.0, 0.0).astype(BF16), tile)
    side[3 * GROUP : 7 * GROUP, 3 : 3 + tile_rows] = near
    strips[...] = side[...].astype(BF16)

    for target, start in ((upper, 0), (lower, tile_rows - 3)):
        target[:, 0 : 3 * patch_cols] = main[:, start * patch_cols : (start + 3) * patch_cols]
        bundle[...] = jnp.zeros_like(bundle)
        for column in range(10):
            bundle[:, column * 3 : column * 3 + 3] = side[
                column * GROUP : (column + 1) * GROUP, 3 + start : 6 + start
            ]
        target[:, 3 * patch_cols :] = bundle[...].astype(BF16)


def weights_kernel(conv1, conv2, head, one_main, one_strip, two_main, two_strip, two_back, head_pad, head_turn, wide, tall):
    bands = conv1.shape[2]
    feat = conv2.shape[1]
    classes = head.shape[0]
    for target, order in ((one_main, False), (one_strip, True)):
        wide[...] = jnp.zeros_like(wide)
        for tap in range(9):
            source = (tap % 3) * 3 + tap // 3 if order else tap
            wide[:, tap * GROUP : tap * GROUP + bands] = conv1[source].astype(F32)
        target[...] = wide[:, 0 : 9 * GROUP].astype(BF16)
    for target, order in ((two_main, 0), (two_strip, 1), (two_back, 2)):
        for tap in range(9):
            source = ((tap % 3) * 3 + tap // 3) if order == 1 else (8 - tap if order == 2 else tap)
            block = conv2[source].astype(F32)
            wide[:, tap * feat : (tap + 1) * feat] = jnp.transpose(block) if order == 2 else block
        target[...] = wide[...].astype(BF16)
    tall[...] = jnp.zeros_like(tall)
    tall[0:classes, 0:feat] = head[...].astype(F32)
    padded = tall[...]
    head_pad[...] = padded[0:GROUP, 0:feat].astype(BF16)
    head_turn[...] = jnp.transpose(padded)[0:feat, 0:GROUP].astype(BF16)


def sigmoid(value):
    return 0.5 * jnp.tanh(0.5 * value) + 0.5


def head_stage(pre, label, mask, head_pad, head_turn, classes):
    gate = sigmoid(pre)
    soft = pre * gate
    skip = soft.astype(BF16)
    logits = dot(head_pad, skip)
    rank = iota(logits.shape, 0)
    real = rank < classes
    total = jnp.sum(jnp.where(real, jnp.exp(logits), 0.0), axis=0, keepdims=True)
    log_total = jnp.log(total)
    chosen = rank == label
    error = jnp.where(real, jnp.exp(logits - log_total) - jnp.where(chosen, 1.0, 0.0), 0.0)
    error = error.astype(BF16)
    loss = log_total - jnp.sum(jnp.where(chosen, logits, 0.0), axis=0, keepdims=True)
    back = dot(head_turn, error)
    slope = back * (gate + soft * (1.0 - gate))
    if mask is not None:
        slope = jnp.where(mask, slope, 0.0)
    return skip, error, slope, loss


def network_kernel(
    bands, classes, rows, cols, lat_count, lon_count, step,
    place, main, strips, above, below,
    one_main, one_strip, two_main, two_strip, two_back, head_pad, head_turn,
    skip_out, keep_out, send_out,
    band_rows, band_side, hidden_rows, slope_one_rate, slope_rows, sums,
):
    feat = two_main.shape[0]
    lat, lon = place[0], place[1]
    ext = rows + 6

    def span(row, count=1):
        return pl.ds(pl.multiple_of(row * cols, 128), count * cols)

    band_side[...] = strips[...].astype(F32)
    up_tail = above[:, 3 * cols :].astype(F32)
    down_tail = below[:, 3 * cols :].astype(F32)
    for column in range(10):
        at = slice(column * GROUP, (column + 1) * GROUP)
        band_side[at, 0:3] = up_tail[:, column * 3 : column * 3 + 3]
        band_side[at, 3 + rows : 6 + rows] = down_tail[:, column * 3 : column * 3 + 3]

    def turned(value):
        return jnp.concatenate(
            [pltpu.roll(value, 1, 1), value, pltpu.roll(value, value.shape[1] - 1, 1)], axis=0
        ).astype(BF16)

    lane_row = iota((1, 128), 1) - 3
    row_inside = (lat * rows + lane_row >= 0) & (lat * rows + lane_row < lat_count * rows)
    row_inside = row_inside & (lane_row >= -3) & (lane_row < rows + 3)
    has_left, has_right = lon > 0, lon < lon_count - 1
    side_taps = [turned(band_side[c * GROUP : (c + 1) * GROUP, :]) for c in range(10)]
    hidden_side = []
    for first in (0, 1, 2, 5, 6, 7):
        pre = dot(one_strip[...], jnp.concatenate(side_taps[first : first + 3], axis=0))
        inside = row_inside
        if first in (0, 1):
            inside = inside & has_left
        if first in (6, 7):
            inside = inside & has_right
        hidden_side.append(jnp.where(inside, pre * sigmoid(pre), 0.0).astype(BF16).astype(F32))
    hidden_taps = [turned(value) for value in hidden_side]
    slope_side = []
    for first, label_column, has in ((0, 2, has_left), (3, 7, has_right)):
        pre = dot(two_strip[...], jnp.concatenate(hidden_taps[first : first + 3], axis=0))
        at = label_column * GROUP + bands
        label = band_side[at : at + 1, :].astype(jnp.int32)
        slope = head_stage(pre, label, row_inside & has, head_pad[...], head_turn[...], classes)[2]
        slope_side.append(slope.astype(BF16).astype(F32))

    lane = iota((1, cols), 1)

    def put_shifted(target, value, row, count, left_side, right_side, size):
        target[size : 2 * size, span(row, count)] = value.astype(BF16)
        for i in range(count):
            tile = value[:, i * cols : (i + 1) * cols]
            turn = lax.rem(128 - (row + i), 128)
            left = pltpu.roll(left_side, turn, 1)
            right = pltpu.roll(right_side, lax.rem(turn + cols - 1, 128), 1)
            at_left = jnp.where(lane == 0, left, pltpu.roll(tile, 1, 1))
            at_right = jnp.where(lane == cols - 1, right, pltpu.roll(tile, cols - 1, 1))
            target[0:size, span(row + i)] = at_left.astype(BF16)
            target[2 * size : 3 * size, span(row + i)] = at_right.astype(BF16)

    def around(ref, row, count):
        return jnp.concatenate([ref[:, span(row + u, count)] for u in (-1, 0, 1)], axis=0)

    band_left = band_side[2 * GROUP : 3 * GROUP, :]
    band_right = band_side[7 * GROUP : 8 * GROUP, :]
    put_shifted(band_rows, above[:, 0 : 3 * cols].astype(F32), 0, 3, band_left, band_right, GROUP)
    put_shifted(band_rows, below[:, 0 : 3 * cols].astype(F32), rows + 3, 3, band_left, band_right, GROUP)

    def band_step(i, carry):
        row = i * step
        put_shifted(band_rows, main[:, span(row, step)].astype(F32), row + 3, step, band_left, band_right, GROUP)
        return carry

    lax.fori_loop(0, rows // step, band_step, 0)

    hidden_left, hidden_right = hidden_side[1], hidden_side[4]

    def hidden_chunk(row, count, mask, keep):
        pre = dot(one_main[...], around(band_rows, row, count))
        gate = sigmoid(pre)
        soft = pre * gate
        if keep:
            slope_one_rate[:, span(row, count)] = gate + soft * (1.0 - gate)
        if mask is not None:
            soft = jnp.where(mask, soft, 0.0)
        put_shifted(hidden_rows, soft.astype(BF16).astype(F32), row, count, hidden_left, hidden_right, feat)

    top_inside, bottom_inside = lat > 0, lat < lat_count - 1
    hidden_chunk(1, 2, top_inside, False)
    hidden_chunk(rows + 3, 2, bottom_inside, False)

    def hidden_step(i, carry):
        hidden_chunk(i * step + 3, step, None, True)
        return carry

    lax.fori_loop(0, rows // step, hidden_step, 0)

    slope_left, slope_right = slope_side

    def label_of(row, count):
        return band_rows[GROUP + bands : GROUP + bands + 1, span(row, count)].astype(F32).astype(jnp.int32)

    for row, mask in ((2, top_inside), (rows + 3, bottom_inside)):
        pre = dot(two_main[...], around(hidden_rows, row, 1))
        slope = head_stage(pre, label_of(row, 1), mask, head_pad[...], head_turn[...], classes)[2]
        put_shifted(slope_rows, slope.astype(BF16).astype(F32), row, 1, slope_left, slope_right, feat)

    def slope_step(i, carry):
        grad_two, grad_head, loss_sum = carry
        row = i * step + 3
        near = around(hidden_rows, row, step)
        pre = dot(two_main[...], near)
        skip, error, slope, loss = head_stage(
            pre, label_of(row, step), None, head_pad[...], head_turn[...], classes
        )
        skip_out[:, span(row - 3, step)] = skip
        slope = slope.astype(BF16)
        grad_two = grad_two + dot_nt(slope, near)
        grad_head = grad_head + dot_nt(skip, error)
        put_shifted(slope_rows, slope.astype(F32), row, step, slope_left, slope_right, feat)
        return grad_two, grad_head, loss_sum + loss

    grad_two, grad_head, loss_sum = lax.fori_loop(
        0,
        rows // step,
        slope_step,
        (
            jnp.zeros((feat, 9 * feat), F32),
            jnp.zeros((feat, GROUP), F32),
            jnp.zeros((1, step * cols), F32),
        ),
    )

    def back_step(i, grad_one):
        row = i * step + 3
        back = dot(two_back[...], around(slope_rows, row, step))
        slope = (back * slope_one_rate[:, span(row, step)]).astype(BF16)
        return grad_one + dot_nt(slope, around(band_rows, row, step))

    grad_one = lax.fori_loop(0, rows // step, back_step, jnp.zeros((feat, 9 * GROUP), F32))

    sums[...] = jnp.zeros_like(sums)
    sums[:, 0 : 9 * feat] = grad_two
    sums[:, 9 * feat : 9 * feat + 9 * GROUP] = grad_one
    at = 9 * feat + 9 * GROUP
    sums[:, at : at + GROUP] = grad_head
    sums[0:1, at + GROUP : at + GROUP + 1] = jnp.sum(loss_sum, axis=1, keepdims=True)
    half = feat // 2
    core = lon % 2
    keep_out[...] = sums[pl.ds(pl.multiple_of(core * half, 8), half), :]
    send_out[...] = sums[pl.ds(pl.multiple_of((1 - core) * half, 8), half), :]


def finish_kernel(pixels, me_ref, own, mate, grad_one, grad_two, grad_head, loss, sums):
    half = own.shape[0]
    feat = 2 * half
    bands = grad_one.shape[2]
    classes = grad_head.shape[0]
    core = me_ref[0] % 2
    scale = 1.0 / pixels
    sums[pl.ds(pl.multiple_of(core * half, 8), half), :] = own[...]
    sums[pl.ds(pl.multiple_of((1 - core) * half, 8), half), :] = mate[...]
    for tap in range(9):
        grad_two[tap] = sums[:, tap * feat : (tap + 1) * feat] * scale
        at = 9 * feat + tap * GROUP
        grad_one[tap] = sums[:, at : at + bands] * scale
    at = 9 * feat + 9 * GROUP
    turned = jnp.transpose(sums[:, at : at + GROUP])
    grad_head[...] = turned[0:classes] * scale
    loss[...] = sums[0:1, at + GROUP : at + GROUP + 1] * scale


def tree_sum(values):
    values = list(values)
    while len(values) > 1:
        values = [values[i] + values[i + 1] for i in range(0, len(values), 2)]
    return values[0]


def body(
    patches,
    requests,
    footprint,
    weight_index,
    composite_weights,
    labels,
    conv1_weight,
    conv2_weight,
    head_weight,
):
    lon_count = lax.axis_size("lon")
    lat_count = lax.axis_size("lat")
    chips = lon_count // 2
    rows, slots = footprint.shape
    cols = labels.shape[1]
    store, row_width = patches.shape
    bands = row_width // cols
    bucket = requests.shape[1] // lon_count
    feat = conv2_weight.shape[1]
    classes = head_weight.shape[0]
    vmem = pl.BlockSpec(memory_space=pltpu.VMEM)
    smem = pl.BlockSpec(memory_space=pltpu.SMEM)

    lon = lax.axis_index("lon")
    place = jnp.stack([lax.axis_index("lat"), lon]).astype(jnp.int32)
    me = lon.astype(jnp.int32).reshape(1)

    def by_lon(value, move):
        return lax.ppermute(value, "lon", [(i, i ^ move) for i in range(lon_count)])

    mate_patches = by_lon(patches, 1)
    plan = call(
        plan_kernel,
        struct((16, 128), F32),
        in_specs=[vmem, vmem, vmem, smem, vmem],
    )(requests, footprint, weight_index, composite_weights, labels)
    plans = lax.all_to_all(
        jnp.broadcast_to(plan[None], (lon_count,) + plan.shape), "lon", split_axis=0, concat_axis=0, tiled=True
    )
    wide = row_width + 2 * rows
    parts = call(
        functools.partial(partial_kernel, rows, slots, bucket, bands),
        [struct((rows, wide), BF16)] * chips,
        [
            pltpu.VMEM((2 * store, row_width), BF16),
            pltpu.VMEM((6 * GROUP, 2 * store), BF16),
            pltpu.VMEM((lon_count + 2, 2 * rows, 2 * store), BF16),
        ],
        in_specs=[smem, vmem, vmem, vmem],
    )(me, plans, patches, mate_patches)
    parts = [parts[0]] + [by_lon(parts[move], 2 * move) for move in range(1, chips)]
    main, strips, upper, lower = call(
        functools.partial(composite_kernel, bands),
        [
            struct((GROUP, rows * cols), BF16),
            struct((10 * GROUP, 128), BF16),
            struct((GROUP, 3 * cols + 128), BF16),
            struct((GROUP, 3 * cols + 128), BF16),
        ],
        [
            pltpu.VMEM((GROUP * rows, cols), F32),
            pltpu.VMEM((10 * GROUP, 128), F32),
            pltpu.VMEM((GROUP, 128), F32),
        ],
        in_specs=[smem] + [vmem] * (2 + chips),
    )(me, plans, labels, *parts)
    below = lax.ppermute(upper, "lat", [(i + 1, i) for i in range(lat_count - 1)])
    above = lax.ppermute(lower, "lat", [(i, i + 1) for i in range(lat_count - 1)])

    weights = call(
        weights_kernel,
        [
            struct((feat, 9 * GROUP), BF16),
            struct((feat, 9 * GROUP), BF16),
            struct((feat, 9 * feat), BF16),
            struct((feat, 9 * feat), BF16),
            struct((feat, 9 * feat), BF16),
            struct((GROUP, feat), BF16),
            struct((feat, GROUP), BF16),
        ],
        [pltpu.VMEM((feat, 9 * feat), F32), pltpu.VMEM((128, 128), F32)],
    )(conv1_weight, conv2_weight, head_weight)

    sum_width = -(-(9 * feat + 9 * GROUP + GROUP + 1) // 128) * 128
    ext = rows + 6
    half = feat // 2
    skip, keep, send = call(
        functools.partial(network_kernel, bands, classes, rows, cols, lat_count, lon_count, 4),
        [
            struct((feat, rows * cols), BF16),
            struct((half, sum_width), F32),
            struct((half, sum_width), F32),
        ],
        [
            pltpu.VMEM((3 * GROUP, ext * cols), BF16),
            pltpu.VMEM((10 * GROUP, 128), F32),
            pltpu.VMEM((3 * feat, ext * cols), BF16),
            pltpu.VMEM((feat, ext * cols), F32),
            pltpu.VMEM((3 * feat, ext * cols), BF16),
            pltpu.VMEM((feat, sum_width), F32),
        ],
        in_specs=[smem] + [vmem] * 11,
    )(place, main, strips, above, below, *weights)

    total = keep + by_lon(send, 1)
    total = tree_sum([total] + [by_lon(total, 2 * move) for move in range(1, chips)])
    total = tree_sum(
        [total]
        + [
            lax.ppermute(total, "lat", [(i, i ^ move) for i in range(lat_count)])
            for move in range(1, lat_count)
        ]
    )
    other = by_lon(total, 1)
    pixels = rows * cols * lat_count * lon_count
    grad_one, grad_two, grad_head, loss = call(
        functools.partial(finish_kernel, pixels),
        [
            struct((9, feat, bands), F32),
            struct((9, feat, feat), F32),
            struct((classes, feat), F32),
            struct((1, 1), F32),
        ],
        [pltpu.VMEM((feat, sum_width), F32)],
        in_specs=[smem, vmem, vmem],
    )(me, total, other)
    return skip.reshape(feat, rows, cols), grad_one, grad_two, grad_head, loss.reshape(())


def solution(mesh):
    placed = (
        P(("lat", "lon"), None),
        P("lat", "lon"),
        P("lat", "lon"),
        P("lat", "lon"),
        P(),
        P("lat", "lon"),
        P(),
        P(),
        P(),
    )
    return jax.shard_map(
        body,
        mesh=mesh,
        in_specs=placed,
        out_specs=(P(None, "lat", "lon"), P(), P(), P(), P()),
        check_vma=False,
    )
```

```python
import functools

import jax
import jax.numpy as jnp
from jax import lax
from jax.experimental import pallas as pl
from jax.experimental.pallas import tpu as pltpu
from jax.sharding import PartitionSpec as P

BF16 = jnp.bfloat16
F32 = jnp.float32
GROUP = 16
VMEM_LIMIT = 40 * 1024 * 1024


def dot(left, right):
    return lax.dot_general(left, right, (((1,), (0,)), ((), ())), preferred_element_type=F32)


def dot_nt(left, right):
    return lax.dot_general(left, right, (((1,), (1,)), ((), ())), preferred_element_type=F32)


def iota(shape, dim):
    return lax.broadcasted_iota(jnp.int32, shape, dim)


def call(kernel, out_shape, scratch=(), **kwargs):
    return pl.pallas_call(
        kernel,
        out_shape=out_shape,
        scratch_shapes=list(scratch),
        compiler_params=pltpu.CompilerParams(vmem_limit_bytes=VMEM_LIMIT),
        **kwargs,
    )


def struct(shape, dtype):
    return jax.ShapeDtypeStruct(shape, dtype)


def plan_kernel(requests, footprint, weight_index, levels, labels, out):
    slots, rows = footprint.shape
    patch_cols = labels.shape[1]
    foot = footprint[...]
    level_of = weight_index[...]
    weight = jnp.zeros((slots, rows), F32)
    for level in range(levels.shape[0]):
        weight = jnp.where(level_of == level, levels[level], weight)
    weight = jnp.where(foot >= 0, weight, 0.0)
    weight = weight / jnp.sum(weight, axis=0, keepdims=True)
    turned = jnp.transpose(jnp.concatenate([foot.astype(F32), weight], axis=0))
    groups = [turned[group * 8 : group * 8 + 8] for group in range(rows // 8)]
    asked = requests[...].astype(F32)
    asked = [asked[:, part * 128 : (part + 1) * 128] for part in range(requests.shape[1] // 128)]
    lane = iota((8, patch_cols), 1)
    side = iota((8, patch_cols), 0)
    pick = ((side == 0) & (lane == 0)) | ((side == 1) & (lane == patch_cols - 1))
    edges = dot_nt(jnp.where(pick, 1.0, 0.0).astype(BF16), labels[...].astype(F32).astype(BF16))
    edges = jnp.concatenate([edges[0:1], edges[1:2]], axis=1)
    lower = jnp.concatenate(asked + [edges, jnp.zeros((7 - len(asked), 128), F32)], axis=0)
    whole = jnp.concatenate([jnp.concatenate(groups, axis=1), lower], axis=0)
    for target in range(out.shape[0]):
        out[target] = whole


def store_kernel(bands, me_ref, own, mate, stored, edge):
    store, row_width = own.shape
    patch_cols = row_width // bands
    core = me_ref[0] % 2
    stored[pl.ds(pl.multiple_of(core * store, 64), store), :] = own[...]
    stored[pl.ds(pl.multiple_of((1 - core) * store, 64), store), :] = mate[...]
    row_id = iota((6 * GROUP, patch_cols), 0)
    lane_id = iota((6 * GROUP, patch_cols), 1)
    column = row_id // GROUP
    column_lane = jnp.where(column < 3, column + (patch_cols - 3), column - 3)
    at_column = lane_id == column_lane
    total = jnp.zeros(edge.shape, F32)
    for band in range(bands):
        pick = jnp.where(at_column & (row_id % GROUP == band), 1.0, 0.0).astype(BF16)
        total = total + dot_nt(pick, stored[:, band * patch_cols : (band + 1) * patch_cols])
    edge[...] = total.astype(BF16)


def spread_kernel(tile_rows, slots, bucket, store, me_ref, plans, spread):
    count = plans.shape[0]
    chip = me_ref[0] // 2
    zero_tile = jnp.zeros(spread.shape[1:], spread.dtype)
    spread[0] = zero_tile
    spread[count + 1] = zero_tile
    pair = 2 * bucket
    target = (iota((8, pair), 1) + chip * pair).astype(F32)
    store_row = iota((2 * store, pair), 0)
    store_base = jnp.where(iota((2 * store, pair), 1) >= bucket, store, 0)
    relative = (store_row - store_base).astype(F32)
    for tile in range(count):
        groups = []
        for group in range(tile_rows // 8):
            base = group * 2 * slots
            total = jnp.zeros((8, pair), F32)
            for slot in range(slots):
                entry = plans[tile, 0:8, base + slot : base + slot + 1]
                weight = plans[tile, 0:8, base + slots + slot : base + slots + slot + 1]
                total = total + jnp.where(entry == target, weight, 0.0)
            groups.append(total)
        at_place = jnp.concatenate(groups, axis=0)
        if pair == 128:
            asked = plans[tile, pl.ds(8 + chip, 1), :]
        else:
            start = chip * pair
            asked = plans[tile, pl.ds(8 + start // 128, 1), :]
            asked = pltpu.roll(jnp.broadcast_to(asked, (8, 128)), (128 - start % 128) % 128, 1)[0:1, 0:pair]
        hit = jnp.where(relative == asked, 1.0, 0.0).astype(BF16)
        high = at_place.astype(BF16)
        low = (at_place - high.astype(F32)).astype(BF16)
        both = dot_nt(jnp.concatenate([high, low], axis=0), hit)
        over_rows = both[:tile_rows] + both[tile_rows:]
        high = over_rows.astype(BF16)
        low = (over_rows - high.astype(F32)).astype(BF16)
        spread[tile + 1, 0:tile_rows] = high
        spread[tile + 1, tile_rows : 2 * tile_rows] = low


def part_kernel(move, me_ref, spread, stored, edge, out):
    tile_rows = out.shape[0]
    row_width = stored.shape[1]
    me = me_ref[0]
    tile = 2 * jnp.bitwise_xor(me // 2, move) + me % 2
    weights = spread[tile + 1]
    for start in range(0, row_width, 512):
        stop = min(start + 512, row_width)
        both = dot(weights, stored[:, start:stop])
        out[:, start:stop] = (both[:tile_rows] + both[tile_rows:]).astype(BF16)
    left = dot_nt(edge[0 : 3 * GROUP], spread[tile])
    right = dot_nt(edge[3 * GROUP : 6 * GROUP], spread[tile + 2])
    sides = jnp.concatenate(
        [left[:, :tile_rows] + left[:, tile_rows:], right[:, :tile_rows] + right[:, tile_rows:]], axis=1
    )
    out[0 : 3 * GROUP, row_width:] = sides.astype(BF16)
    out[3 * GROUP :, row_width:] = jnp.zeros((tile_rows - 3 * GROUP, 2 * tile_rows), BF16)


def composite_kernel(bands, me_ref, plans, labels, *refs):
    count = plans.shape[0]
    tile_rows, patch_cols = labels.shape
    chips = count // 2
    parts = refs[:chips]
    main, strips, upper, lower, bank, side, bundle = refs[chips:]
    row_width = bands * patch_cols
    me = me_ref[0]
    for band in range(bands):
        columns = slice(band * patch_cols, (band + 1) * patch_cols)
        total = parts[0][:, columns].astype(F32)
        for part in parts[1:]:
            total = total + part[:, columns].astype(F32)
        bank[band * tile_rows : (band + 1) * tile_rows, :] = total
    bank[bands * tile_rows : (bands + 1) * tile_rows, :] = labels[...].astype(F32)
    bank[(bands + 1) * tile_rows : GROUP * tile_rows, :] = jnp.zeros(
        ((GROUP - bands - 1) * tile_rows, patch_cols), F32
    )
    for row in range(tile_rows):
        main[:, row * patch_cols : (row + 1) * patch_cols] = bank[
            pl.ds(row, GROUP, stride=tile_rows), :
        ].astype(BF16)

    far = parts[0][0 : 3 * GROUP, row_width : row_width + 2 * tile_rows].astype(F32)
    for part in parts[1:]:
        far = far + part[0 : 3 * GROUP, row_width : row_width + 2 * tile_rows].astype(F32)
    side[...] = jnp.zeros_like(side)
    side[0 : 3 * GROUP, 3 : 3 + tile_rows] = far[:, :tile_rows]
    side[7 * GROUP : 10 * GROUP, 3 : 3 + tile_rows] = far[:, tile_rows:]
    before = plans[jnp.maximum(me - 1, 0), 12:13, tile_rows : 2 * tile_rows]
    after = plans[jnp.minimum(me + 1, count - 1), 12:13, 0:tile_rows]
    side[2 * GROUP + bands : 2 * GROUP + bands + 1, 3 : 3 + tile_rows] = before
    side[7 * GROUP + bands : 7 * GROUP + bands + 1, 3 : 3 + tile_rows] = after
    row_id = iota((4 * GROUP, patch_cols), 0)
    lane_id = iota((4 * GROUP, patch_cols), 1)
    near = jnp.zeros((4 * GROUP, tile_rows), F32)
    column = row_id // GROUP
    column_lane = jnp.where(column < 2, column, column + (patch_cols - 4))
    for band in range(bands):
        pick = (row_id % GROUP == band) & (lane_id == column_lane)
        tile = bank[band * tile_rows : (band + 1) * tile_rows, :].astype(BF16)
        near = near + dot_nt(jnp.where(pick, 1.0, 0.0).astype(BF16), tile)
    side[3 * GROUP : 7 * GROUP, 3 : 3 + tile_rows] = near
    strips[...] = side[...].astype(BF16)

    for target, start in ((upper, 0), (lower, tile_rows - 3)):
        target[:, 0 : 3 * patch_cols] = main[:, start * patch_cols : (start + 3) * patch_cols]
        bundle[...] = jnp.zeros_like(bundle)
        for column in range(10):
            bundle[:, column * 3 : column * 3 + 3] = side[
                column * GROUP : (column + 1) * GROUP, 3 + start : 6 + start
            ]
        target[:, 3 * patch_cols :] = bundle[...].astype(BF16)


def weights_kernel(conv1, conv2, head, one_main, one_strip, two_main, two_back, head_pad, head_turn, wide, tall):
    bands = conv1.shape[1]
    feat = conv2.shape[1]
    classes = head.shape[0]
    wide[...] = jnp.zeros_like(wide)
    for tap in range(9):
        wide[tap * GROUP : tap * GROUP + bands, :] = conv1[tap].astype(F32)
    one_main[...] = jnp.transpose(wide[...]).astype(BF16)
    for tap in range(9):
        wide[tap * GROUP : tap * GROUP + bands, :] = conv1[(tap % 3) * 3 + tap // 3].astype(F32)
    one_strip[...] = jnp.transpose(wide[...]).astype(BF16)
    for row in range(3):
        at = slice(row * feat, (row + 1) * feat)
        two_main[at, :] = jnp.concatenate([conv2[row * 3 + col] for col in range(3)], axis=1)
        turned = jnp.concatenate([conv2[8 - (row * 3 + col)].astype(F32) for col in range(3)], axis=0)
        two_back[at, :] = jnp.transpose(turned).astype(BF16)
    tall[...] = jnp.zeros_like(tall)
    tall[0:classes, 0:feat] = head[...].astype(F32)
    padded = tall[...]
    head_pad[...] = padded[0:GROUP, 0:feat].astype(BF16)
    head_turn[...] = jnp.transpose(padded)[0:feat, 0:GROUP].astype(BF16)


def sigmoid(value):
    return 0.5 * jnp.tanh(0.5 * value) + 0.5


def head_stage(pre, label, mask, head_pad, head_turn, classes):
    gate = sigmoid(pre)
    soft = pre * gate
    skip = soft.astype(BF16)
    logits = dot(head_pad, skip)
    rank = iota(logits.shape, 0)
    real = rank < classes
    total = jnp.sum(jnp.where(real, jnp.exp(logits), 0.0), axis=0, keepdims=True)
    log_total = jnp.log(total)
    chosen = rank == label
    error = jnp.where(real, jnp.exp(logits - log_total) - jnp.where(chosen, 1.0, 0.0), 0.0)
    error = error.astype(BF16)
    loss = log_total - jnp.sum(jnp.where(chosen, logits, 0.0), axis=0, keepdims=True)
    back = dot(head_turn, error)
    slope = back * (gate + soft * (1.0 - gate))
    if mask is not None:
        slope = jnp.where(mask, slope, 0.0)
    return skip, error, slope.astype(BF16), loss


def span(row, count, cols):
    return slice(row * cols, (row + count) * cols)


def put_shifted(target, value, row, count, left_side, right_side, size, cols):
    lane = iota((1, cols), 1)
    target[size : 2 * size, span(row, count, cols)] = value
    for i in range(count):
        tile = value[:, i * cols : (i + 1) * cols]
        turn = (128 - (row + i)) % 128
        left = pltpu.roll(left_side, turn, 1)
        right = pltpu.roll(right_side, (turn + cols - 1) % 128, 1)
        target[0:size, span(row + i, 1, cols)] = jnp.where(lane == 0, left, pltpu.roll(tile, 1, 1))
        target[2 * size : 3 * size, span(row + i, 1, cols)] = jnp.where(
            lane == cols - 1, right, pltpu.roll(tile, cols - 1, 1)
        )


def above_below(ref, row, count, cols):
    return jnp.concatenate([ref[:, span(row + u, count, cols)] for u in (-1, 0, 1)], axis=0)


def below_above(ref, row, count, cols):
    return jnp.concatenate([ref[:, span(row - u, count, cols)] for u in (-1, 0, 1)], axis=0)


def conv_rows(weight, ref, row, count, cols):
    feat = weight.shape[0] // 3
    near = dot(weight[...], ref[:, span(row - 1, count + 2, cols)])
    return (
        near[0:feat, span(0, count, cols)]
        + near[feat : 2 * feat, span(1, count, cols)]
        + near[2 * feat :, span(2, count, cols)]
    )


def turned_rows(value):
    return jnp.concatenate(
        [pltpu.roll(value, 1, 1), value, pltpu.roll(value, value.shape[1] - 1, 1)], axis=0
    ).astype(BF16)


def strip_inside(place, rows, lat_count, lon_count):
    lat, lon = place[0], place[1]
    lane_row = iota((1, 128), 1) - 3
    inside = (lat * rows + lane_row >= 0) & (lat * rows + lane_row < lat_count * rows)
    inside = inside & (lane_row < rows + 3)
    return inside, inside & (lon > 0), inside & (lon < lon_count - 1)


def strip_hidden(side, one_strip, insides, firsts):
    inside, left_inside, right_inside = insides
    taps = {}
    hidden = []
    for first in firsts:
        for column in range(first, first + 3):
            if column not in taps:
                taps[column] = turned_rows(side[column * GROUP : (column + 1) * GROUP, :])
        pre = dot(one_strip[...], jnp.concatenate([taps[first + i] for i in range(3)], axis=0))
        mask = left_inside if first in (0, 1) else right_inside if first in (6, 7) else inside
        hidden.append(jnp.where(mask, pre * sigmoid(pre), 0.0).astype(BF16))
    return hidden


def hidden_chunk(one_main, band_rows, hidden_rows, rate, row, count, mask, sides, cols):
    pre = dot(one_main[...], above_below(band_rows, row, count, cols))
    gate = sigmoid(pre)
    soft = pre * gate
    if rate is not None:
        rate[:, span(row - 3, count, cols)] = gate + soft * (1.0 - gate)
    if mask is not None:
        soft = jnp.where(mask, soft, 0.0)
    put_shifted(hidden_rows, soft.astype(BF16), row, count, *sides, pre.shape[0], cols)


def inner_kernel(rows, cols, lat_count, lon_count, step, place, main, strips, one_main, one_strip, band_rows, hidden_rows, rate, side):
    side[...] = strips[...].astype(F32)
    hidden_left, hidden_right = strip_hidden(
        side, one_strip, strip_inside(place, rows, lat_count, lon_count), (1, 6)
    )
    band_sides = (strips[2 * GROUP : 3 * GROUP, :], strips[7 * GROUP : 8 * GROUP, :])
    for row in range(0, rows, step):
        put_shifted(band_rows, main[:, span(row, step, cols)], row + 3, step, *band_sides, GROUP, cols)
    for row in range(4, rows + 2, step):
        count = min(step, rows + 2 - row)
        hidden_chunk(one_main, band_rows, hidden_rows, rate, row, count, None, (hidden_left, hidden_right), cols)


def outer_kernel(
    bands, classes, rows, cols, lat_count, lon_count, step,
    place, strips, above, below, band_in, hidden_in, rate_in,
    one_main, one_strip, two_main, two_back, head_pad, head_turn,
    skip_out, keep_out, send_out,
    band_rows, side, hidden_rows, rate, slope_rows, slope_own, sums,
):
    feat = head_turn.shape[0]
    lat, lon = place[0], place[1]
    band_rows[:, span(3, rows, cols)] = band_in[:, span(3, rows, cols)]
    hidden_rows[:, span(4, rows - 2, cols)] = hidden_in[:, span(4, rows - 2, cols)]
    rate[:, span(1, rows - 2, cols)] = rate_in[:, span(1, rows - 2, cols)]

    side[...] = strips[...].astype(F32)
    up_tail = above[:, 3 * cols :].astype(F32)
    down_tail = below[:, 3 * cols :].astype(F32)
    for column in range(10):
        at = slice(column * GROUP, (column + 1) * GROUP)
        side[at, 0:3] = up_tail[:, column * 3 : column * 3 + 3]
        side[at, 3 + rows : 6 + rows] = down_tail[:, column * 3 : column * 3 + 3]

    insides = strip_inside(place, rows, lat_count, lon_count)
    hidden_side = strip_hidden(side, one_strip, insides, (0, 1, 2, 5, 6, 7))
    hidden_taps = [turned_rows(value.astype(F32)) for value in hidden_side]
    slope_side = []
    for first, label_column, inside in ((0, 2, insides[1]), (3, 7, insides[2])):
        pre = None
        for col in range(3):
            weight = jnp.concatenate(
                [two_main[u * feat : (u + 1) * feat, col * feat : (col + 1) * feat] for u in range(3)], axis=1
            )
            term = dot(weight, hidden_taps[first + col])
            pre = term if pre is None else pre + term
        at = label_column * GROUP + bands
        label = side[at : at + 1, :].astype(jnp.int32)
        slope_side.append(head_stage(pre, label, inside, head_pad[...], head_turn[...], classes)[2])

    band_sides = (
        side[2 * GROUP : 3 * GROUP, :].astype(BF16),
        side[7 * GROUP : 8 * GROUP, :].astype(BF16),
    )
    put_shifted(band_rows, above[:, 0 : 3 * cols], 0, 3, *band_sides, GROUP, cols)
    put_shifted(band_rows, below[:, 0 : 3 * cols], rows + 3, 3, *band_sides, GROUP, cols)

    top_inside, bottom_inside = lat > 0, lat < lat_count - 1
    hidden_sides = (hidden_side[1], hidden_side[4])
    hidden_chunk(one_main, band_rows, hidden_rows, None, 1, 2, top_inside, hidden_sides, cols)
    hidden_chunk(one_main, band_rows, hidden_rows, rate, 3, 1, None, hidden_sides, cols)
    hidden_chunk(one_main, band_rows, hidden_rows, rate, rows + 2, 1, None, hidden_sides, cols)
    hidden_chunk(one_main, band_rows, hidden_rows, None, rows + 3, 2, bottom_inside, hidden_sides, cols)

    def label_of(row, count):
        return band_rows[GROUP + bands : GROUP + bands + 1, span(row, count, cols)].astype(F32).astype(jnp.int32)

    for row, mask in ((2, top_inside), (rows + 3, bottom_inside)):
        pre = conv_rows(two_main, hidden_rows, row, 1, cols)
        slope = head_stage(pre, label_of(row, 1), mask, head_pad[...], head_turn[...], classes)[2]
        put_shifted(slope_rows, slope, row, 1, *slope_side, feat, cols)

    for row in (1, rows + 3):
        slope_own[:, span(row, 2, cols)] = jnp.zeros((feat, 2 * cols), BF16)
    grad_head = jnp.zeros((feat, GROUP), F32)
    loss_sum = jnp.zeros((1, 1), F32)
    for row in range(3, rows + 3, step):
        pre = conv_rows(two_main, hidden_rows, row, step, cols)
        skip, error, slope, loss = head_stage(
            pre, label_of(row, step), None, head_pad[...], head_turn[...], classes
        )
        skip_out[:, span(row - 3, step, cols)] = skip
        slope_own[:, span(row, step, cols)] = slope
        grad_head = grad_head + dot_nt(skip, error)
        put_shifted(slope_rows, slope, row, step, *slope_side, feat, cols)
        loss_sum = loss_sum + jnp.sum(loss, axis=1, keepdims=True)

    def grad_of(slope_ref, value_ref):
        total = None
        for row in range(2, rows + 4, 11):
            count = min(11, rows + 4 - row)
            term = dot_nt(below_above(slope_ref, row, count, cols), value_ref[:, span(row, count, cols)])
            total = term if total is None else total + term
        return total

    sums[...] = jnp.zeros_like(sums)
    sums[:, 0 : 3 * feat] = grad_of(slope_own, hidden_rows)
    for row in range(3, rows + 3, step):
        back = conv_rows(two_back, slope_rows, row, step, cols)
        slope_own[:, span(row, step, cols)] = (back * rate[:, span(row - 3, step, cols)]).astype(BF16)
    sums[:, 3 * feat : 3 * feat + 3 * GROUP] = grad_of(slope_own, band_rows)
    at = 3 * feat + 3 * GROUP
    sums[0:feat, at : at + GROUP] = grad_head
    sums[feat : feat + 1, at : at + 1] = loss_sum
    half = 3 * feat // 2
    core = lon % 2
    keep_out[...] = sums[pl.ds(pl.multiple_of(core * half, 8), half), :]
    send_out[...] = sums[pl.ds(pl.multiple_of((1 - core) * half, 8), half), :]


def finish_kernel(pixels, me_ref, own, mate, grad_one, grad_two, grad_head, loss, sums):
    half = own.shape[0]
    feat = grad_two.shape[1]
    bands = grad_one.shape[1]
    classes = grad_head.shape[0]
    core = me_ref[0] % 2
    scale = 1.0 / pixels
    sums[pl.ds(pl.multiple_of(core * half, 8), half), :] = own[...] * scale
    sums[pl.ds(pl.multiple_of((1 - core) * half, 8), half), :] = mate[...] * scale
    at = 3 * feat
    turned = jnp.transpose(sums[:, at : at + 3 * GROUP + GROUP])
    for tap in range(9):
        u, v = tap // 3, tap % 3
        grad_two[tap] = sums[u * feat : (u + 1) * feat, v * feat : (v + 1) * feat]
        grad_one[tap] = turned[v * GROUP : v * GROUP + bands, u * feat : (u + 1) * feat]
    grad_head[...] = turned[3 * GROUP : 3 * GROUP + classes, 0:feat]
    loss[...] = turned[3 * GROUP : 3 * GROUP + 1, feat : feat + 1]


def tree_sum(values):
    values = list(values)
    while len(values) > 1:
        values = [values[i] + values[i + 1] for i in range(0, len(values), 2)]
    return values[0]


def body(
    patches,
    requests,
    footprint,
    weight_index,
    composite_weights,
    labels,
    conv1_weight,
    conv2_weight,
    head_weight,
):
    lon_count = lax.axis_size("lon")
    lat_count = lax.axis_size("lat")
    chips = lon_count // 2
    rows, slots = footprint.shape
    cols = labels.shape[1]
    store, row_width = patches.shape
    bands = row_width // cols
    bucket = requests.shape[1] // lon_count
    feat = conv2_weight.shape[1]
    classes = head_weight.shape[0]
    vmem = pl.BlockSpec(memory_space=pltpu.VMEM)
    smem = pl.BlockSpec(memory_space=pltpu.SMEM)

    lon = lax.axis_index("lon")
    place = jnp.stack([lax.axis_index("lat"), lon]).astype(jnp.int32)
    me = lon.astype(jnp.int32).reshape(1)

    def by_lon(value, move):
        return lax.ppermute(value, "lon", [(i, i ^ move) for i in range(lon_count)])

    mate_patches = by_lon(patches, 1)
    plan = call(
        plan_kernel,
        struct((lon_count, 16, 128), F32),
        in_specs=[vmem, vmem, vmem, smem, vmem],
    )(requests, footprint.T, weight_index.T, composite_weights, labels)
    plans = lax.all_to_all(plan, "lon", split_axis=0, concat_axis=0, tiled=True)
    stored, edge = call(
        functools.partial(store_kernel, bands),
        [struct((2 * store, row_width), BF16), struct((6 * GROUP, 2 * store), BF16)],
        in_specs=[smem, vmem, vmem],
    )(me, patches, mate_patches)
    spread = call(
        functools.partial(spread_kernel, rows, slots, bucket, store),
        struct((lon_count + 2, 2 * rows, 2 * store), BF16),
        in_specs=[smem, vmem],
    )(me, plans)
    parts = []
    for move in range(chips - 1, -1, -1):
        part = call(
            functools.partial(part_kernel, move),
            struct((rows, row_width + 2 * rows), BF16),
            in_specs=[smem, vmem, vmem, vmem],
        )(me, spread, stored, edge)
        parts.append(by_lon(part, 2 * move) if move else part)
    main, strips, upper, lower = call(
        functools.partial(composite_kernel, bands),
        [
            struct((GROUP, rows * cols), BF16),
            struct((10 * GROUP, 128), BF16),
            struct((GROUP, 3 * cols + 128), BF16),
            struct((GROUP, 3 * cols + 128), BF16),
        ],
        [
            pltpu.VMEM((GROUP * rows, cols), F32),
            pltpu.VMEM((10 * GROUP, 128), F32),
            pltpu.VMEM((GROUP, 128), F32),
        ],
        in_specs=[smem] + [vmem] * (2 + chips),
    )(me, plans, labels, *parts)
    below = lax.ppermute(upper, "lat", [(i + 1, i) for i in range(lat_count - 1)])
    above = lax.ppermute(lower, "lat", [(i, i + 1) for i in range(lat_count - 1)])

    one_main, one_strip, two_main, two_back, head_pad, head_turn = call(
        weights_kernel,
        [
            struct((feat, 9 * GROUP), BF16),
            struct((feat, 9 * GROUP), BF16),
            struct((3 * feat, 3 * feat), BF16),
            struct((3 * feat, 3 * feat), BF16),
            struct((GROUP, feat), BF16),
            struct((feat, GROUP), BF16),
        ],
        [pltpu.VMEM((9 * GROUP, feat), F32), pltpu.VMEM((128, 128), F32)],
    )(conv1_weight.transpose(0, 2, 1), conv2_weight, head_weight)

    ext = rows + 6
    step = 16
    band_rows, hidden_rows, rate = call(
        functools.partial(inner_kernel, rows, cols, lat_count, lon_count, step),
        [
            struct((3 * GROUP, ext * cols), BF16),
            struct((3 * feat, ext * cols), BF16),
            struct((feat, rows * cols), F32),
        ],
        [pltpu.VMEM((10 * GROUP, 128), F32)],
        in_specs=[smem] + [vmem] * 4,
        cost_estimate=pl.CostEstimate(flops=10**8, bytes_accessed=10**7, transcendentals=0),
    )(place, main, strips, one_main, one_strip)
    half = 3 * feat // 2
    sum_width = 3 * feat + 4 * GROUP
    skip, keep, send = call(
        functools.partial(outer_kernel, bands, classes, rows, cols, lat_count, lon_count, step),
        [
            struct((feat, rows * cols), BF16),
            struct((half, sum_width), F32),
            struct((half, sum_width), F32),
        ],
        [
            pltpu.VMEM((3 * GROUP, ext * cols), BF16),
            pltpu.VMEM((10 * GROUP, 128), F32),
            pltpu.VMEM((3 * feat, ext * cols), BF16),
            pltpu.VMEM((feat, rows * cols), F32),
            pltpu.VMEM((3 * feat, ext * cols), BF16),
            pltpu.VMEM((feat, ext * cols), BF16),
            pltpu.VMEM((3 * feat, sum_width), F32),
        ],
        in_specs=[smem] + [vmem] * 12,
    )(
        place, strips, above, below, band_rows, hidden_rows, rate,
        one_main, one_strip, two_main, two_back, head_pad, head_turn,
    )

    total = keep + by_lon(send, 1)
    total = tree_sum([total] + [by_lon(total, 2 * move) for move in range(1, chips)])
    sent = total.astype(BF16)
    total = tree_sum(
        [sent.astype(F32)]
        + [
            lax.ppermute(sent, "lat", [(i, i ^ move) for i in range(lat_count)]).astype(F32)
            for move in range(1, lat_count)
        ]
    )
    other = by_lon(total, 1)
    pixels = rows * cols * lat_count * lon_count
    grad_one, grad_two, grad_head, loss = call(
        functools.partial(finish_kernel, pixels),
        [
            struct((9, bands, feat), F32),
            struct((9, feat, feat), F32),
            struct((classes, feat), F32),
            struct((1, 1), F32),
        ],
        [pltpu.VMEM((3 * feat, sum_width), F32)],
        in_specs=[smem, vmem, vmem],
    )(me, total, other)
    return skip.reshape(feat, rows, cols), grad_one.transpose(0, 2, 1), grad_two, grad_head, loss.reshape(())


def solution(mesh):
    placed = (
        P(("lat", "lon"), None),
        P("lat", "lon"),
        P("lat", "lon"),
        P("lat", "lon"),
        P(),
        P("lat", "lon"),
        P(),
        P(),
        P(),
    )
    return jax.shard_map(
        body,
        mesh=mesh,
        in_specs=placed,
        out_specs=(P(None, "lat", "lon"), P(), P(), P(), P()),
        check_vma=False,
    )
```

```python
import functools

import jax
import jax.numpy as jnp
from jax import lax
from jax.experimental import pallas as pl
from jax.experimental.pallas import tpu as pltpu
from jax.sharding import PartitionSpec as P

BF16 = jnp.bfloat16
F32 = jnp.float32
GROUP = 16
VMEM_LIMIT = 28 * 1024 * 1024


def dot(left, right):
    return lax.dot_general(left, right, (((1,), (0,)), ((), ())), preferred_element_type=F32)


def dot_nt(left, right):
    return lax.dot_general(left, right, (((1,), (1,)), ((), ())), preferred_element_type=F32)


def iota(shape, dim):
    return lax.broadcasted_iota(jnp.int32, shape, dim)


def call(kernel, out_shape, scratch=(), vmem_limit=VMEM_LIMIT, **kwargs):
    return pl.pallas_call(
        kernel,
        out_shape=out_shape,
        scratch_shapes=list(scratch),
        compiler_params=pltpu.CompilerParams(vmem_limit_bytes=vmem_limit),
        **kwargs,
    )


def struct(shape, dtype):
    return jax.ShapeDtypeStruct(shape, dtype)


def plan_kernel(
    store, requests_hbm, footprint_hbm, weight_index_hbm, levels_hbm, labels_hbm, out, labels_out,
    requests, footprint, weight_index, levels, labels, sems,
):
    copies = [
        pltpu.make_async_copy(source, target, sems.at[i])
        for i, (source, target) in enumerate(
            (
                (footprint_hbm, footprint),
                (requests_hbm, requests),
                (weight_index_hbm, weight_index),
                (levels_hbm, levels),
                (labels_hbm, labels),
            )
        )
    ]
    for copy in copies:
        copy.start()
    for copy in copies:
        copy.wait()
    slots, rows = footprint.shape
    patch_cols = labels.shape[1]
    count = out.shape[0]
    bucket = requests.shape[1] // count
    foot = footprint[...]
    level_of = weight_index[...]
    weight = jnp.zeros((slots, rows), F32)
    for level in range(levels.shape[0]):
        weight = jnp.where(level_of == level, levels[level], weight)
    weight = jnp.where(foot >= 0, weight, 0.0)
    weight = weight / jnp.sum(weight, axis=0, keepdims=True)
    flat = jnp.concatenate([foot[slot : slot + 1] for slot in range(slots)], axis=1)
    owner = jnp.right_shift(flat, bucket.bit_length() - 1)
    place = jnp.bitwise_and(flat, bucket - 1)
    at_place = jnp.where(iota((bucket, slots * rows), 0) == place, 1.0, 0.0).astype(BF16)
    asked = requests[...].astype(F32)
    asked = jnp.concatenate([asked[:, i * bucket : (i + 1) * bucket] for i in range(count)], axis=0)
    offset = dot(asked.astype(BF16), at_place)
    offset = jnp.sum(jnp.where(iota(offset.shape, 0) == owner, offset, 0.0), axis=0, keepdims=True)
    entry = offset + (owner * store).astype(F32)
    entry = jnp.concatenate([entry[:, slot * rows : (slot + 1) * rows] for slot in range(slots)], axis=0)
    turned = jnp.transpose(jnp.concatenate([entry, weight], axis=0))
    groups = jnp.concatenate([turned[group * 8 : group * 8 + 8] for group in range(rows // 8)], axis=1)
    lane = iota((8, patch_cols), 1)
    side = iota((8, patch_cols), 0)
    pick = ((side == 0) & (lane == 0)) | ((side == 1) & (lane == patch_cols - 1))
    label = labels[...].astype(F32)
    labels_out[...] = label
    edges = dot_nt(jnp.where(pick, 1.0, 0.0).astype(BF16), label.astype(BF16))
    edges = jnp.concatenate([edges, jnp.concatenate([edges[1:2], edges[0:7]], axis=0)], axis=1)
    for target in range(count):
        out[target, 0:8, :] = groups
        out[target, 8:16, :] = edges


def store_kernel(bands, me_ref, own, mate, stored, edge):
    store, row_width = own.shape
    patch_cols = row_width // bands
    core = me_ref[0] % 2
    stored[pl.ds(pl.multiple_of(core * store, 64), store), :] = own[...]
    stored[pl.ds(pl.multiple_of((1 - core) * store, 64), store), :] = mate[...]
    row_id = iota((6 * GROUP, patch_cols), 0)
    lane_id = iota((6 * GROUP, patch_cols), 1)
    column = row_id // GROUP
    column_lane = jnp.where(column < 3, column + (patch_cols - 3), column - 3)
    at_column = lane_id == column_lane
    total = jnp.zeros(edge.shape, F32)
    for band in range(bands):
        pick = jnp.where(at_column & (row_id % GROUP == band), 1.0, 0.0).astype(BF16)
        total = total + dot_nt(pick, stored[:, band * patch_cols : (band + 1) * patch_cols])
    edge[...] = total.astype(BF16)


def part_kernel(moves, slots, me_ref, plans, stored, edge, *refs):
    outs, weights = refs[:-1], refs[-1]
    count = plans.shape[0]
    tile_rows = outs[0].shape[0]
    held, row_width = stored.shape
    me = me_ref[0]
    column = iota((8, held), 1).astype(F32) + (me // 2 * held).astype(F32)

    def put_weights(index, at):
        there = (index >= 0) & (index < count)
        entries = plans[jnp.clip(index, 0, count - 1), 0:8, :]
        for group in range(tile_rows // 8):
            base = group * 2 * slots
            total = jnp.zeros((8, held), F32)
            for slot in range(slots):
                entry = entries[:, base + slot : base + slot + 1]
                weight = entries[:, base + slots + slot : base + slots + slot + 1]
                total = total + jnp.where(entry == column, weight, 0.0)
            total = jnp.where(there, total, 0.0)
            high = total.astype(BF16).astype(F32)
            weights[at, group * 8 : group * 8 + 8, :] = high
            weights[at, tile_rows + group * 8 : tile_rows + group * 8 + 8, :] = total - high

    if len(moves) > 1:
        for index in range(-1, count + 1):
            put_weights(index, index + 1)
    for move, out in zip(moves, outs, strict=True):
        tile = 2 * jnp.bitwise_xor(me // 2, move) + me % 2
        if len(moves) > 1:
            at = tile + 1
        else:
            at = 1
            for i in range(3):
                put_weights(tile - 1 + i, i)
        row_weights = weights[at].astype(BF16)
        for start in range(0, row_width, 512):
            stop = min(start + 512, row_width)
            both = dot(row_weights, stored[:, start:stop])
            out[:, start:stop] = (both[:tile_rows] + both[tile_rows:]).astype(out.dtype)
        left = dot_nt(edge[0 : 3 * GROUP], weights[at - 1].astype(BF16))
        right = dot_nt(edge[3 * GROUP : 6 * GROUP], weights[at + 1].astype(BF16))
        sides = jnp.concatenate(
            [left[:, :tile_rows] + left[:, tile_rows:], right[:, :tile_rows] + right[:, tile_rows:]], axis=1
        )
        out[0 : 3 * GROUP, row_width:] = sides.astype(out.dtype)
        out[3 * GROUP :, row_width:] = jnp.zeros((tile_rows - 3 * GROUP, 2 * tile_rows), out.dtype)


def composite_kernel(bands, me_ref, plans, labels, *refs):
    count = plans.shape[0]
    tile_rows, patch_cols = labels.shape
    chips = count // 2
    parts = refs[:chips]
    main, strips, upper, lower, bank, side, bundle = refs[chips:]
    row_width = bands * patch_cols
    me = me_ref[0]
    for band in range(bands):
        columns = slice(band * patch_cols, (band + 1) * patch_cols)
        total = parts[0][:, columns].astype(F32)
        for part in parts[1:]:
            total = total + part[:, columns].astype(F32)
        bank[band * tile_rows : (band + 1) * tile_rows, :] = total
    bank[bands * tile_rows : (bands + 1) * tile_rows, :] = labels[...]
    bank[(bands + 1) * tile_rows : GROUP * tile_rows, :] = jnp.zeros(
        ((GROUP - bands - 1) * tile_rows, patch_cols), F32
    )
    for row in range(tile_rows):
        main[:, row * patch_cols : (row + 1) * patch_cols] = bank[
            pl.ds(row, GROUP, stride=tile_rows), :
        ].astype(BF16)

    far = parts[0][0 : 3 * GROUP, row_width : row_width + 2 * tile_rows].astype(F32)
    for part in parts[1:]:
        far = far + part[0 : 3 * GROUP, row_width : row_width + 2 * tile_rows].astype(F32)
    side[...] = jnp.zeros_like(side)
    side[0 : 3 * GROUP, 3 : 3 + tile_rows] = far[:, :tile_rows]
    side[7 * GROUP : 10 * GROUP, 3 : 3 + tile_rows] = far[:, tile_rows:]
    before = plans[jnp.maximum(me - 1, 0), 8:9, tile_rows : 2 * tile_rows]
    after = plans[jnp.minimum(me + 1, count - 1), 8:9, 0:tile_rows]
    side[2 * GROUP + bands : 2 * GROUP + bands + 1, 3 : 3 + tile_rows] = before
    side[7 * GROUP + bands : 7 * GROUP + bands + 1, 3 : 3 + tile_rows] = after
    row_id = iota((4 * GROUP, patch_cols), 0)
    lane_id = iota((4 * GROUP, patch_cols), 1)
    near = jnp.zeros((4 * GROUP, tile_rows), F32)
    column = row_id // GROUP
    column_lane = jnp.where(column < 2, column, column + (patch_cols - 4))
    for band in range(bands):
        pick = (row_id % GROUP == band) & (lane_id == column_lane)
        tile = bank[band * tile_rows : (band + 1) * tile_rows, :].astype(BF16)
        near = near + dot_nt(jnp.where(pick, 1.0, 0.0).astype(BF16), tile)
    side[3 * GROUP : 7 * GROUP, 3 : 3 + tile_rows] = near
    strips[...] = side[...].astype(BF16)

    for target, start in ((upper, 0), (lower, tile_rows - 3)):
        target[:, 0 : 3 * patch_cols] = main[:, start * patch_cols : (start + 3) * patch_cols]
        bundle[...] = jnp.zeros_like(bundle)
        for column in range(10):
            bundle[:, column * 3 : column * 3 + 3] = side[
                column * GROUP : (column + 1) * GROUP, 3 + start : 6 + start
            ]
        target[:, 3 * patch_cols :] = bundle[...].astype(BF16)


def weights_kernel(conv1, conv2, head, one_main, one_strip, two_main, two_back, head_pad, head_turn, wide, tall):
    bands = conv1.shape[1]
    feat = conv2.shape[1]
    classes = head.shape[0]
    wide[...] = jnp.zeros_like(wide)
    for tap in range(9):
        wide[tap * GROUP : tap * GROUP + bands, :] = conv1[tap].astype(F32)
    one_main[...] = jnp.transpose(wide[...]).astype(BF16)
    for tap in range(9):
        wide[tap * GROUP : tap * GROUP + bands, :] = conv1[(tap % 3) * 3 + tap // 3].astype(F32)
    one_strip[...] = jnp.transpose(wide[...]).astype(BF16)
    for row in range(3):
        at = slice(row * feat, (row + 1) * feat)
        two_main[at, :] = jnp.concatenate([conv2[row * 3 + col] for col in range(3)], axis=1)
        turned = jnp.concatenate([conv2[8 - (row * 3 + col)].astype(F32) for col in range(3)], axis=0)
        two_back[at, :] = jnp.transpose(turned).astype(BF16)
    tall[...] = jnp.zeros_like(tall)
    tall[0:classes, 0:feat] = head[...].astype(F32)
    padded = tall[...]
    head_pad[...] = padded[0:GROUP, 0:feat].astype(BF16)
    head_turn[...] = jnp.transpose(padded)[0:feat, 0:GROUP].astype(BF16)


def sigmoid(value):
    return 0.5 * jnp.tanh(0.5 * value) + 0.5


def head_stage(pre, label, mask, head_pad, head_turn, classes):
    gate = sigmoid(pre)
    soft = pre * gate
    skip = soft.astype(BF16)
    logits = dot(head_pad, skip)
    rank = iota(logits.shape, 0)
    real = rank < classes
    total = jnp.sum(jnp.where(real, jnp.exp(logits), 0.0), axis=0, keepdims=True)
    log_total = jnp.log(total)
    chosen = rank == label
    error = jnp.where(real, jnp.exp(logits - log_total) - jnp.where(chosen, 1.0, 0.0), 0.0)
    error = error.astype(BF16)
    loss = log_total - jnp.sum(jnp.where(chosen, logits, 0.0), axis=0, keepdims=True)
    back = dot(head_turn, error)
    slope = back * (gate + soft * (1.0 - gate))
    if mask is not None:
        slope = jnp.where(mask, slope, 0.0)
    return skip, error, slope.astype(BF16), loss


def span(row, count, cols):
    return slice(row * cols, (row + count) * cols)


def put_shifted(target, value, row, count, left_side, right_side, size, cols):
    lane = iota((1, cols), 1)
    target[size : 2 * size, span(row, count, cols)] = value
    for i in range(count):
        tile = value[:, i * cols : (i + 1) * cols]
        turn = (128 - (row + i)) % 128
        left = pltpu.roll(left_side, turn, 1)
        right = pltpu.roll(right_side, (turn + cols - 1) % 128, 1)
        target[0:size, span(row + i, 1, cols)] = jnp.where(lane == 0, left, pltpu.roll(tile, 1, 1))
        target[2 * size : 3 * size, span(row + i, 1, cols)] = jnp.where(
            lane == cols - 1, right, pltpu.roll(tile, cols - 1, 1)
        )


def above_below(ref, row, count, cols):
    return jnp.concatenate([ref[:, span(row + u, count, cols)] for u in (-1, 0, 1)], axis=0)


def below_above(ref, row, count, cols):
    return jnp.concatenate([ref[:, span(row - u, count, cols)] for u in (-1, 0, 1)], axis=0)


def conv_rows(weight, ref, row, count, cols):
    feat = weight.shape[0] // 3
    near = dot(weight[...], ref[:, span(row - 1, count + 2, cols)])
    return (
        near[0:feat, span(0, count, cols)]
        + near[feat : 2 * feat, span(1, count, cols)]
        + near[2 * feat :, span(2, count, cols)]
    )


def turned_rows(value):
    return jnp.concatenate(
        [pltpu.roll(value, 1, 1), value, pltpu.roll(value, value.shape[1] - 1, 1)], axis=0
    ).astype(BF16)


def strip_inside(place, rows, lat_count, lon_count):
    lat, lon = place[0], place[1]
    lane_row = iota((1, 128), 1) - 3
    inside = (lat * rows + lane_row >= 0) & (lat * rows + lane_row < lat_count * rows)
    inside = inside & (lane_row < rows + 3)
    return inside, inside & (lon > 0), inside & (lon < lon_count - 1)


def strip_hidden(side, one_strip, insides, firsts):
    inside, left_inside, right_inside = insides
    taps = {}
    hidden = []
    for first in firsts:
        for column in range(first, first + 3):
            if column not in taps:
                taps[column] = turned_rows(side[column * GROUP : (column + 1) * GROUP, :])
        pre = dot(one_strip[...], jnp.concatenate([taps[first + i] for i in range(3)], axis=0))
        mask = left_inside if first in (0, 1) else right_inside if first in (6, 7) else inside
        hidden.append(jnp.where(mask, pre * sigmoid(pre), 0.0).astype(BF16))
    return hidden


def hidden_chunk(one_main, band_rows, hidden_rows, rate, row, count, mask, sides, cols):
    pre = dot(one_main[...], above_below(band_rows, row, count, cols))
    gate = sigmoid(pre)
    soft = pre * gate
    if rate is not None:
        rate[:, span(row - 3, count, cols)] = gate + soft * (1.0 - gate)
    if mask is not None:
        soft = jnp.where(mask, soft, 0.0)
    put_shifted(hidden_rows, soft.astype(BF16), row, count, *sides, pre.shape[0], cols)


def inner_kernel(rows, cols, lat_count, lon_count, step, place, main, strips, one_main, one_strip, band_rows, hidden_rows, rate, side):
    side[...] = strips[...].astype(F32)
    hidden_left, hidden_right = strip_hidden(
        side, one_strip, strip_inside(place, rows, lat_count, lon_count), (1, 6)
    )
    band_sides = (strips[2 * GROUP : 3 * GROUP, :], strips[7 * GROUP : 8 * GROUP, :])
    for row in range(0, rows, step):
        put_shifted(band_rows, main[:, span(row, step, cols)], row + 3, step, *band_sides, GROUP, cols)
    for row in range(4, rows + 2, step):
        count = min(step, rows + 2 - row)
        hidden_chunk(one_main, band_rows, hidden_rows, rate, row, count, None, (hidden_left, hidden_right), cols)


def outer_kernel(
    bands, classes, rows, cols, lat_count, lon_count, step,
    place, strips, above, below, band_in, hidden_in, rate_in,
    one_main, one_strip, two_main, two_back, head_pad, head_turn,
    skip_out, keep_out, send_out,
    band_rows, side, hidden_rows, rate, slope_rows, slope_own, sums,
):
    feat = head_turn.shape[0]
    lat, lon = place[0], place[1]
    band_rows[:, span(3, rows, cols)] = band_in[:, span(3, rows, cols)]
    hidden_rows[:, span(4, rows - 2, cols)] = hidden_in[:, span(4, rows - 2, cols)]
    rate[:, span(1, rows - 2, cols)] = rate_in[:, span(1, rows - 2, cols)]

    side[...] = strips[...].astype(F32)
    up_tail = above[:, 3 * cols :].astype(F32)
    down_tail = below[:, 3 * cols :].astype(F32)
    for column in range(10):
        at = slice(column * GROUP, (column + 1) * GROUP)
        side[at, 0:3] = up_tail[:, column * 3 : column * 3 + 3]
        side[at, 3 + rows : 6 + rows] = down_tail[:, column * 3 : column * 3 + 3]

    insides = strip_inside(place, rows, lat_count, lon_count)
    hidden_side = strip_hidden(side, one_strip, insides, (0, 1, 2, 5, 6, 7))
    hidden_taps = [turned_rows(value.astype(F32)) for value in hidden_side]
    slope_side = []
    for first, label_column, inside in ((0, 2, insides[1]), (3, 7, insides[2])):
        pre = None
        for col in range(3):
            weight = jnp.concatenate(
                [two_main[u * feat : (u + 1) * feat, col * feat : (col + 1) * feat] for u in range(3)], axis=1
            )
            term = dot(weight, hidden_taps[first + col])
            pre = term if pre is None else pre + term
        at = label_column * GROUP + bands
        label = side[at : at + 1, :].astype(jnp.int32)
        slope_side.append(head_stage(pre, label, inside, head_pad[...], head_turn[...], classes)[2])

    band_sides = (
        side[2 * GROUP : 3 * GROUP, :].astype(BF16),
        side[7 * GROUP : 8 * GROUP, :].astype(BF16),
    )
    put_shifted(band_rows, above[:, 0 : 3 * cols], 0, 3, *band_sides, GROUP, cols)
    put_shifted(band_rows, below[:, 0 : 3 * cols], rows + 3, 3, *band_sides, GROUP, cols)

    top_inside, bottom_inside = lat > 0, lat < lat_count - 1
    hidden_sides = (hidden_side[1], hidden_side[4])
    hidden_chunk(one_main, band_rows, hidden_rows, None, 1, 2, top_inside, hidden_sides, cols)
    hidden_chunk(one_main, band_rows, hidden_rows, rate, 3, 1, None, hidden_sides, cols)
    hidden_chunk(one_main, band_rows, hidden_rows, rate, rows + 2, 1, None, hidden_sides, cols)
    hidden_chunk(one_main, band_rows, hidden_rows, None, rows + 3, 2, bottom_inside, hidden_sides, cols)

    def label_of(row, count):
        return band_rows[GROUP + bands : GROUP + bands + 1, span(row, count, cols)].astype(F32).astype(jnp.int32)

    for row, mask in ((2, top_inside), (rows + 3, bottom_inside)):
        pre = conv_rows(two_main, hidden_rows, row, 1, cols)
        slope = head_stage(pre, label_of(row, 1), mask, head_pad[...], head_turn[...], classes)[2]
        put_shifted(slope_rows, slope, row, 1, *slope_side, feat, cols)

    for row in (1, rows + 3):
        slope_own[:, span(row, 2, cols)] = jnp.zeros((feat, 2 * cols), BF16)
    grad_head = jnp.zeros((feat, GROUP), F32)
    loss_sum = jnp.zeros((1, 1), F32)
    for row in range(3, rows + 3, step):
        pre = conv_rows(two_main, hidden_rows, row, step, cols)
        skip, error, slope, loss = head_stage(
            pre, label_of(row, step), None, head_pad[...], head_turn[...], classes
        )
        skip_out[:, span(row - 3, step, cols)] = skip
        slope_own[:, span(row, step, cols)] = slope
        grad_head = grad_head + dot_nt(skip, error)
        put_shifted(slope_rows, slope, row, step, *slope_side, feat, cols)
        loss_sum = loss_sum + jnp.sum(loss, axis=1, keepdims=True)

    def grad_of(slope_ref, value_ref):
        total = None
        for row in range(2, rows + 4, 11):
            count = min(11, rows + 4 - row)
            term = dot_nt(below_above(slope_ref, row, count, cols), value_ref[:, span(row, count, cols)])
            total = term if total is None else total + term
        return total

    sums[...] = jnp.zeros_like(sums)
    sums[:, 0 : 3 * feat] = grad_of(slope_own, hidden_rows)
    for row in range(3, rows + 3, step):
        back = conv_rows(two_back, slope_rows, row, step, cols)
        slope_own[:, span(row, step, cols)] = (back * rate[:, span(row - 3, step, cols)]).astype(BF16)
    sums[:, 3 * feat : 3 * feat + 3 * GROUP] = grad_of(slope_own, band_rows)
    at = 3 * feat + 3 * GROUP
    sums[0:feat, at : at + GROUP] = grad_head
    sums[feat : feat + 1, at : at + 1] = loss_sum
    half = 3 * feat // 2
    core = lon % 2
    keep_out[...] = sums[pl.ds(pl.multiple_of(core * half, 8), half), :]
    send_out[...] = sums[pl.ds(pl.multiple_of((1 - core) * half, 8), half), :]


def finish_kernel(pixels, me_ref, own, mate, grad_one, grad_two, grad_head, loss, sums):
    half = own.shape[0]
    feat = grad_two.shape[1]
    bands = grad_one.shape[1]
    classes = grad_head.shape[0]
    core = me_ref[0] % 2
    scale = 1.0 / pixels
    sums[pl.ds(pl.multiple_of(core * half, 8), half), :] = own[...] * scale
    sums[pl.ds(pl.multiple_of((1 - core) * half, 8), half), :] = mate[...] * scale
    at = 3 * feat
    turned = jnp.transpose(sums[:, at : at + 3 * GROUP + GROUP])
    for tap in range(9):
        u, v = tap // 3, tap % 3
        grad_two[tap] = sums[u * feat : (u + 1) * feat, v * feat : (v + 1) * feat]
        grad_one[tap] = turned[v * GROUP : v * GROUP + bands, u * feat : (u + 1) * feat]
    grad_head[...] = turned[3 * GROUP : 3 * GROUP + classes, 0:feat]
    loss[...] = turned[3 * GROUP : 3 * GROUP + 1, feat : feat + 1]


def tree_sum(values):
    values = list(values)
    while len(values) > 1:
        values = [values[i] + values[i + 1] for i in range(0, len(values), 2)]
    return values[0]


def body(
    patches,
    requests,
    footprint,
    weight_index,
    composite_weights,
    labels,
    conv1_weight,
    conv2_weight,
    head_weight,
):
    lon_count = lax.axis_size("lon")
    lat_count = lax.axis_size("lat")
    chips = lon_count // 2
    rows, slots = footprint.shape
    cols = labels.shape[1]
    store, row_width = patches.shape
    bands = row_width // cols
    bucket = requests.shape[1] // lon_count
    feat = conv2_weight.shape[1]
    classes = head_weight.shape[0]
    vmem = pl.BlockSpec(memory_space=pltpu.VMEM)
    smem = pl.BlockSpec(memory_space=pltpu.SMEM)

    lon = lax.axis_index("lon")
    place = jnp.stack([lax.axis_index("lat"), lon]).astype(jnp.int32)
    me = lon.astype(jnp.int32).reshape(1)

    def by_lon(value, move):
        return lax.ppermute(value, "lon", [(i, i ^ move) for i in range(lon_count)])

    hbm = pl.BlockSpec(memory_space=pltpu.HBM)
    plan, tile_labels = call(
        functools.partial(plan_kernel, store),
        [struct((lon_count, 16, 128), F32), struct((rows, cols), F32)],
        [
            pltpu.VMEM(requests.shape, jnp.int32),
            pltpu.VMEM((slots, rows), jnp.int32),
            pltpu.VMEM((slots, rows), jnp.int32),
            pltpu.SMEM(composite_weights.shape, F32),
            pltpu.VMEM(labels.shape, jnp.int32),
            pltpu.SemaphoreType.DMA((5,)),
        ],
        vmem_limit=63 * 1024 * 1024,
        in_specs=[hbm] * 5,
    )(requests, footprint.T, weight_index.T, composite_weights, labels)
    plan, patches = lax.optimization_barrier((plan, patches))
    mate_patches = by_lon(patches, 1)
    plans = lax.all_to_all(plan, "lon", split_axis=0, concat_axis=0, tiled=True)
    stored, edge = call(
        functools.partial(store_kernel, bands),
        [struct((2 * store, row_width), BF16), struct((6 * GROUP, 2 * store), BF16)],
        in_specs=[smem, vmem, vmem],
        cost_estimate=pl.CostEstimate(flops=10**9, bytes_accessed=10**7, transcendentals=0),
    )(me, patches, mate_patches)
    plans, stored, edge = lax.optimization_barrier((plans, stored, edge))
    moves = list(range(chips - 1, 0, -1))
    parts = []
    for some in (moves, [0]):
        parts += call(
            functools.partial(part_kernel, some, slots),
            [struct((rows, row_width + 2 * rows), BF16 if move else F32) for move in some],
            [pltpu.VMEM((lon_count + 2 if len(some) > 1 else 3, 2 * rows, 2 * store), F32)],
            in_specs=[smem, vmem, vmem, vmem],
            cost_estimate=pl.CostEstimate(flops=10**9, bytes_accessed=10**7, transcendentals=0),
        )(me, plans, stored, edge)
    parts = [by_lon(part, 2 * move) for move, part in zip(moves, parts)] + parts[-1:]
    main, strips, upper, lower = call(
        functools.partial(composite_kernel, bands),
        [
            struct((GROUP, rows * cols), BF16),
            struct((10 * GROUP, 128), BF16),
            struct((GROUP, 3 * cols + 128), BF16),
            struct((GROUP, 3 * cols + 128), BF16),
        ],
        [
            pltpu.VMEM((GROUP * rows, cols), F32),
            pltpu.VMEM((10 * GROUP, 128), F32),
            pltpu.VMEM((GROUP, 128), F32),
        ],
        in_specs=[smem] + [vmem] * (2 + chips),
    )(me, plans, tile_labels, *parts)
    below = lax.ppermute(upper, "lat", [(i + 1, i) for i in range(lat_count - 1)])
    above = lax.ppermute(lower, "lat", [(i, i + 1) for i in range(lat_count - 1)])

    one_main, one_strip, two_main, two_back, head_pad, head_turn = call(
        weights_kernel,
        [
            struct((feat, 9 * GROUP), BF16),
            struct((feat, 9 * GROUP), BF16),
            struct((3 * feat, 3 * feat), BF16),
            struct((3 * feat, 3 * feat), BF16),
            struct((GROUP, feat), BF16),
            struct((feat, GROUP), BF16),
        ],
        [pltpu.VMEM((9 * GROUP, feat), F32), pltpu.VMEM((128, 128), F32)],
    )(conv1_weight.transpose(0, 2, 1), conv2_weight, head_weight)

    ext = rows + 6
    step = 16
    band_rows, hidden_rows, rate = call(
        functools.partial(inner_kernel, rows, cols, lat_count, lon_count, step),
        [
            struct((3 * GROUP, ext * cols), BF16),
            struct((3 * feat, ext * cols), BF16),
            struct((feat, rows * cols), F32),
        ],
        [pltpu.VMEM((10 * GROUP, 128), F32)],
        in_specs=[smem] + [vmem] * 4,
        cost_estimate=pl.CostEstimate(flops=10**8, bytes_accessed=10**7, transcendentals=0),
    )(place, main, strips, one_main, one_strip)
    half = 3 * feat // 2
    sum_width = 3 * feat + 4 * GROUP
    skip, keep, send = call(
        functools.partial(outer_kernel, bands, classes, rows, cols, lat_count, lon_count, step),
        [
            struct((feat, rows * cols), BF16),
            struct((half, sum_width), F32),
            struct((half, sum_width), F32),
        ],
        [
            pltpu.VMEM((3 * GROUP, ext * cols), BF16),
            pltpu.VMEM((10 * GROUP, 128), F32),
            pltpu.VMEM((3 * feat, ext * cols), BF16),
            pltpu.VMEM((feat, rows * cols), F32),
            pltpu.VMEM((3 * feat, ext * cols), BF16),
            pltpu.VMEM((feat, ext * cols), BF16),
            pltpu.VMEM((3 * feat, sum_width), F32),
        ],
        in_specs=[smem] + [vmem] * 12,
    )(
        place, strips, above, below, band_rows, hidden_rows, rate,
        one_main, one_strip, two_main, two_back, head_pad, head_turn,
    )

    total = keep + by_lon(send, 1)
    total = tree_sum([total] + [by_lon(total, 2 * move) for move in range(1, chips)])
    sent = total.astype(BF16)
    total = tree_sum(
        [sent.astype(F32)]
        + [
            lax.ppermute(sent, "lat", [(i, i ^ move) for i in range(lat_count)]).astype(F32)
            for move in range(1, lat_count)
        ]
    )
    other = by_lon(total, 1)
    pixels = rows * cols * lat_count * lon_count
    grad_one, grad_two, grad_head, loss = call(
        functools.partial(finish_kernel, pixels),
        [
            struct((9, bands, feat), F32),
            struct((9, feat, feat), F32),
            struct((classes, feat), F32),
            struct((1, 1), F32),
        ],
        [pltpu.VMEM((3 * feat, sum_width), F32)],
        in_specs=[smem, vmem, vmem],
    )(me, total, other)
    return skip.reshape(feat, rows, cols), grad_one.transpose(0, 2, 1), grad_two, grad_head, loss.reshape(())


def solution(mesh):
    placed = (
        P(("lat", "lon"), None),
        P("lat", "lon"),
        P("lat", "lon"),
        P("lat", "lon"),
        P(),
        P("lat", "lon"),
        P(),
        P(),
        P(),
    )
    return jax.shard_map(
        body,
        mesh=mesh,
        in_specs=placed,
        out_specs=(P(None, "lat", "lon"), P(), P(), P(), P()),
        check_vma=False,
    )
```

```python
import functools

import jax
import jax.numpy as jnp
from jax import lax
from jax.experimental import pallas as pl
from jax.experimental.pallas import tpu as pltpu
from jax.sharding import PartitionSpec as P

BF16 = jnp.bfloat16
F32 = jnp.float32
GROUP = 16
VMEM_LIMIT = 28 * 1024 * 1024


def dot(left, right):
    return lax.dot_general(left, right, (((1,), (0,)), ((), ())), preferred_element_type=F32)


def dot_nt(left, right):
    return lax.dot_general(left, right, (((1,), (1,)), ((), ())), preferred_element_type=F32)


def iota(shape, dim):
    return lax.broadcasted_iota(jnp.int32, shape, dim)


def call(kernel, out_shape, scratch=(), vmem_limit=VMEM_LIMIT, **kwargs):
    return pl.pallas_call(
        kernel,
        out_shape=out_shape,
        scratch_shapes=list(scratch),
        compiler_params=pltpu.CompilerParams(vmem_limit_bytes=vmem_limit),
        **kwargs,
    )


def struct(shape, dtype):
    return jax.ShapeDtypeStruct(shape, dtype)


def plan_kernel(
    store, requests_hbm, footprint_hbm, weight_index_hbm, levels_hbm, labels_hbm, out, labels_out,
    requests, footprint, weight_index, levels, labels, sems,
):
    copies = [
        pltpu.make_async_copy(source, target, sems.at[i])
        for i, (source, target) in enumerate(
            (
                (footprint_hbm, footprint),
                (requests_hbm, requests),
                (weight_index_hbm, weight_index),
                (levels_hbm, levels),
                (labels_hbm, labels),
            )
        )
    ]
    for copy in copies:
        copy.start()
    for copy in copies:
        copy.wait()
    slots, rows = footprint.shape
    patch_cols = labels.shape[1]
    count = out.shape[0]
    bucket = requests.shape[1] // count
    foot = footprint[...]
    level_of = weight_index[...]
    weight = jnp.zeros((slots, rows), F32)
    for level in range(levels.shape[0]):
        weight = jnp.where(level_of == level, levels[level], weight)
    weight = jnp.where(foot >= 0, weight, 0.0)
    weight = weight / jnp.sum(weight, axis=0, keepdims=True)
    flat = jnp.concatenate([foot[slot : slot + 1] for slot in range(slots)], axis=1)
    owner = jnp.right_shift(flat, bucket.bit_length() - 1)
    place = jnp.bitwise_and(flat, bucket - 1)
    at_place = jnp.where(iota((bucket, slots * rows), 0) == place, 1.0, 0.0).astype(BF16)
    asked = requests[...].astype(F32)
    asked = jnp.concatenate([asked[:, i * bucket : (i + 1) * bucket] for i in range(count)], axis=0)
    offset = dot(asked.astype(BF16), at_place)
    offset = jnp.sum(jnp.where(iota(offset.shape, 0) == owner, offset, 0.0), axis=0, keepdims=True)
    entry = offset + (owner * store).astype(F32)
    entry = jnp.concatenate([entry[:, slot * rows : (slot + 1) * rows] for slot in range(slots)], axis=0)
    lane = iota((8, patch_cols), 1)
    side = iota((8, patch_cols), 0)
    pick = ((side == 0) & (lane == 0)) | ((side == 1) & (lane == patch_cols - 1))
    label = labels[...].astype(F32)
    labels_out[...] = label
    edges = dot_nt(jnp.where(pick, 1.0, 0.0).astype(BF16), label.astype(BF16))
    entries = jnp.concatenate([entry, edges], axis=1)
    weights = jnp.concatenate([weight, jnp.zeros_like(weight)], axis=1)
    for target in range(count):
        out[target, 0:slots, :] = entries
        out[target, slots : 2 * slots, :] = weights


def store_kernel(bands, me_ref, own, mate, stored, edge):
    store, row_width = own.shape
    patch_cols = row_width // bands
    core = me_ref[0] % 2
    stored[pl.ds(pl.multiple_of(core * store, 64), store), :] = own[...]
    stored[pl.ds(pl.multiple_of((1 - core) * store, 64), store), :] = mate[...]
    row_id = iota((6 * GROUP, patch_cols), 0)
    lane_id = iota((6 * GROUP, patch_cols), 1)
    column = row_id // GROUP
    column_lane = jnp.where(column < 3, column + (patch_cols - 3), column - 3)
    at_column = lane_id == column_lane
    total = jnp.zeros(edge.shape, F32)
    for band in range(bands):
        pick = jnp.where(at_column & (row_id % GROUP == band), 1.0, 0.0).astype(BF16)
        total = total + dot_nt(pick, stored[:, band * patch_cols : (band + 1) * patch_cols])
    edge[...] = total.astype(BF16)


def put_weights(plans, chip, first, target):
    held, lanes = target.shape
    rows = lanes // 2
    slots = plans.shape[1] // 2
    both = jnp.concatenate([plans[2 * chip, :, 0:rows], plans[2 * chip + 1, :, 0:rows]], axis=1)
    entries, weights = both[0:slots] - first, both[slots:]
    for start in range(0, held, 64):
        stored_row = (iota((64, lanes), 0) + start).astype(F32)
        total = jnp.zeros((64, lanes), F32)
        for slot in range(slots):
            total = total + jnp.where(entries[slot : slot + 1] == stored_row, weights[slot : slot + 1], 0.0)
        target[start : start + 64, :] = total


def high_low(value):
    high = value.astype(BF16)
    return high, (value - high.astype(F32)).astype(BF16)


def part_kernel(moves, me_ref, plans, stored, edge, *refs):
    outs, (over, turned, sides) = refs[:-3], refs[-3:]
    chips = plans.shape[0] // 2
    rows = outs[0].shape[0]
    held, row_width = stored.shape
    me = me_ref[0]
    here, core = me // 2, me % 2
    first = (here * held).astype(F32)
    sides[0] = jnp.zeros(sides.shape[1:], F32)
    sides[chips + 1] = jnp.zeros(sides.shape[1:], F32)
    for chip in range(chips):
        put_weights(plans, chip, first, over.at[chip])
        high, low = high_low(over[chip])
        sides[chip + 1] = dot(edge[...], high) + dot(edge[...], low)
    for move, out in zip(moves, outs, strict=True):
        chip = jnp.bitwise_xor(here, move)
        turned[...] = jnp.transpose(over[chip])
        high, low = high_low(turned[pl.ds(pl.multiple_of(core * rows, 8), rows), :])
        both = jnp.concatenate([high, low], axis=0)
        for start in range(0, row_width, 512):
            stop = min(start + 512, row_width)
            product = dot(both, stored[:, start:stop])
            out[:, start:stop] = (product[:rows] + product[rows:]).astype(out.dtype)
        near, before, after = sides[chip + 1], sides[chip], sides[chip + 2]
        left = jnp.where(core == 1, near[0 : 3 * GROUP, 0:rows], before[0 : 3 * GROUP, rows:])
        right = jnp.where(core == 0, near[3 * GROUP :, rows:], after[3 * GROUP :, 0:rows])
        out[0 : 3 * GROUP, row_width:] = jnp.concatenate([left, right], axis=1).astype(out.dtype)
        out[3 * GROUP :, row_width:] = jnp.zeros((rows - 3 * GROUP, 2 * rows), out.dtype)


def composite_kernel(bands, me_ref, plans, labels, *refs):
    count = plans.shape[0]
    tile_rows, patch_cols = labels.shape
    chips = count // 2
    parts = refs[:chips]
    main, strips, upper, lower, bank, side, bundle = refs[chips:]
    row_width = bands * patch_cols
    me = me_ref[0]
    for band in range(bands):
        columns = slice(band * patch_cols, (band + 1) * patch_cols)
        total = parts[0][:, columns].astype(F32)
        for part in parts[1:]:
            total = total + part[:, columns].astype(F32)
        bank[band * tile_rows : (band + 1) * tile_rows, :] = total
    bank[bands * tile_rows : (bands + 1) * tile_rows, :] = labels[...]
    bank[(bands + 1) * tile_rows : GROUP * tile_rows, :] = jnp.zeros(
        ((GROUP - bands - 1) * tile_rows, patch_cols), F32
    )
    for row in range(tile_rows):
        main[:, row * patch_cols : (row + 1) * patch_cols] = bank[
            pl.ds(row, GROUP, stride=tile_rows), :
        ].astype(BF16)

    far = parts[0][0 : 3 * GROUP, row_width : row_width + 2 * tile_rows].astype(F32)
    for part in parts[1:]:
        far = far + part[0 : 3 * GROUP, row_width : row_width + 2 * tile_rows].astype(F32)
    side[...] = jnp.zeros_like(side)
    side[0 : 3 * GROUP, 3 : 3 + tile_rows] = far[:, :tile_rows]
    side[7 * GROUP : 10 * GROUP, 3 : 3 + tile_rows] = far[:, tile_rows:]
    before = plans[jnp.maximum(me - 1, 0), 1:2, tile_rows : 2 * tile_rows]
    after = plans[jnp.minimum(me + 1, count - 1), 0:1, tile_rows : 2 * tile_rows]
    side[2 * GROUP + bands : 2 * GROUP + bands + 1, 3 : 3 + tile_rows] = before
    side[7 * GROUP + bands : 7 * GROUP + bands + 1, 3 : 3 + tile_rows] = after
    row_id = iota((4 * GROUP, patch_cols), 0)
    lane_id = iota((4 * GROUP, patch_cols), 1)
    near = jnp.zeros((4 * GROUP, tile_rows), F32)
    column = row_id // GROUP
    column_lane = jnp.where(column < 2, column, column + (patch_cols - 4))
    for band in range(bands):
        pick = (row_id % GROUP == band) & (lane_id == column_lane)
        tile = bank[band * tile_rows : (band + 1) * tile_rows, :].astype(BF16)
        near = near + dot_nt(jnp.where(pick, 1.0, 0.0).astype(BF16), tile)
    side[3 * GROUP : 7 * GROUP, 3 : 3 + tile_rows] = near
    strips[...] = side[...].astype(BF16)

    for target, start in ((upper, 0), (lower, tile_rows - 3)):
        target[:, 0 : 3 * patch_cols] = main[:, start * patch_cols : (start + 3) * patch_cols]
        bundle[...] = jnp.zeros_like(bundle)
        for column in range(10):
            bundle[:, column * 3 : column * 3 + 3] = side[
                column * GROUP : (column + 1) * GROUP, 3 + start : 6 + start
            ]
        target[:, 3 * patch_cols :] = bundle[...].astype(BF16)


def weights_kernel(conv1, conv2, head, one_main, one_strip, two_main, two_back, head_pad, head_turn, wide, tall):
    bands = conv1.shape[1]
    feat = conv2.shape[1]
    classes = head.shape[0]
    wide[...] = jnp.zeros_like(wide)
    for tap in range(9):
        wide[tap * GROUP : tap * GROUP + bands, :] = conv1[tap].astype(F32)
    one_main[...] = jnp.transpose(wide[...]).astype(BF16)
    for tap in range(9):
        wide[tap * GROUP : tap * GROUP + bands, :] = conv1[(tap % 3) * 3 + tap // 3].astype(F32)
    one_strip[...] = jnp.transpose(wide[...]).astype(BF16)
    for row in range(3):
        at = slice(row * feat, (row + 1) * feat)
        two_main[at, :] = jnp.concatenate([conv2[row * 3 + col] for col in range(3)], axis=1)
        turned = jnp.concatenate([conv2[8 - (row * 3 + col)].astype(F32) for col in range(3)], axis=0)
        two_back[at, :] = jnp.transpose(turned).astype(BF16)
    tall[...] = jnp.zeros_like(tall)
    tall[0:classes, 0:feat] = head[...].astype(F32)
    padded = tall[...]
    head_pad[...] = padded[0:GROUP, 0:feat].astype(BF16)
    head_turn[...] = jnp.transpose(padded)[0:feat, 0:GROUP].astype(BF16)


def sigmoid(value):
    return 0.5 * jnp.tanh(0.5 * value) + 0.5


def head_stage(pre, label, mask, head_pad, head_turn, classes):
    gate = sigmoid(pre)
    soft = pre * gate
    skip = soft.astype(BF16)
    logits = dot(head_pad, skip)
    rank = iota(logits.shape, 0)
    real = rank < classes
    total = jnp.sum(jnp.where(real, jnp.exp(logits), 0.0), axis=0, keepdims=True)
    log_total = jnp.log(total)
    chosen = rank == label
    error = jnp.where(real, jnp.exp(logits - log_total) - jnp.where(chosen, 1.0, 0.0), 0.0)
    error = error.astype(BF16)
    loss = log_total - jnp.sum(jnp.where(chosen, logits, 0.0), axis=0, keepdims=True)
    back = dot(head_turn, error)
    slope = back * (gate + soft * (1.0 - gate))
    if mask is not None:
        slope = jnp.where(mask, slope, 0.0)
    return skip, error, slope.astype(BF16), loss


def span(row, count, cols):
    return slice(row * cols, (row + count) * cols)


def put_shifted(target, value, row, count, left_side, right_side, size, cols):
    lane = iota((1, cols), 1)
    target[size : 2 * size, span(row, count, cols)] = value
    for i in range(count):
        tile = value[:, i * cols : (i + 1) * cols]
        turn = (128 - (row + i)) % 128
        left = pltpu.roll(left_side, turn, 1)
        right = pltpu.roll(right_side, (turn + cols - 1) % 128, 1)
        target[0:size, span(row + i, 1, cols)] = jnp.where(lane == 0, left, pltpu.roll(tile, 1, 1))
        target[2 * size : 3 * size, span(row + i, 1, cols)] = jnp.where(
            lane == cols - 1, right, pltpu.roll(tile, cols - 1, 1)
        )


def above_below(ref, row, count, cols):
    return jnp.concatenate([ref[:, span(row + u, count, cols)] for u in (-1, 0, 1)], axis=0)


def below_above(ref, row, count, cols):
    return jnp.concatenate([ref[:, span(row - u, count, cols)] for u in (-1, 0, 1)], axis=0)


def conv_rows(weight, ref, row, count, cols):
    feat = weight.shape[0] // 3
    near = dot(weight[...], ref[:, span(row - 1, count + 2, cols)])
    return (
        near[0:feat, span(0, count, cols)]
        + near[feat : 2 * feat, span(1, count, cols)]
        + near[2 * feat :, span(2, count, cols)]
    )


def turned_rows(value):
    return jnp.concatenate(
        [pltpu.roll(value, 1, 1), value, pltpu.roll(value, value.shape[1] - 1, 1)], axis=0
    ).astype(BF16)


def strip_inside(place, rows, lat_count, lon_count):
    lat, lon = place[0], place[1]
    lane_row = iota((1, 128), 1) - 3
    inside = (lat * rows + lane_row >= 0) & (lat * rows + lane_row < lat_count * rows)
    inside = inside & (lane_row < rows + 3)
    return inside, inside & (lon > 0), inside & (lon < lon_count - 1)


def strip_hidden(side, one_strip, insides, firsts):
    inside, left_inside, right_inside = insides
    taps = {}
    for first in firsts:
        for column in range(first, first + 3):
            if column not in taps:
                taps[column] = turned_rows(side[column * GROUP : (column + 1) * GROUP, :])
    near = jnp.concatenate(
        [jnp.concatenate([taps[first + i] for first in firsts], axis=1) for i in range(3)], axis=0
    )
    pre = dot(one_strip[...], near)
    soft = pre * sigmoid(pre)
    hidden = []
    for i, first in enumerate(firsts):
        mask = left_inside if first in (0, 1) else right_inside if first in (6, 7) else inside
        hidden.append(jnp.where(mask, soft[:, i * 128 : (i + 1) * 128], 0.0))
    return hidden


def hidden_chunk(one_main, band_rows, hidden_rows, rate, row, count, mask, sides, cols):
    pre = dot(one_main[...], above_below(band_rows, row, count, cols))
    gate = sigmoid(pre)
    soft = pre * gate
    if rate is not None:
        rate[:, span(row - 3, count, cols)] = gate + soft * (1.0 - gate)
    if mask is not None:
        soft = jnp.where(mask, soft, 0.0)
    put_shifted(hidden_rows, soft.astype(BF16), row, count, *sides, pre.shape[0], cols)


def inner_kernel(rows, cols, lat_count, lon_count, step, place, main, strips, one_main, one_strip, band_rows, hidden_rows, rate, side):
    side[...] = strips[...].astype(F32)
    hidden_sides = [
        hidden.astype(BF16)
        for hidden in strip_hidden(side, one_strip, strip_inside(place, rows, lat_count, lon_count), (1, 6))
    ]
    band_sides = (strips[2 * GROUP : 3 * GROUP, :], strips[7 * GROUP : 8 * GROUP, :])
    for row in range(0, rows, step):
        put_shifted(band_rows, main[:, span(row, step, cols)], row + 3, step, *band_sides, GROUP, cols)
    for row in range(4, rows + 2, step):
        count = min(step, rows + 2 - row)
        hidden_chunk(one_main, band_rows, hidden_rows, rate, row, count, None, hidden_sides, cols)


def outer_kernel(
    bands, classes, rows, cols, lat_count, lon_count, step,
    place, strips, above, below, band_in, hidden_in, rate_in,
    one_main, one_strip, two_main, two_back, head_pad, head_turn,
    skip_out, keep_out, send_out,
    band_rows, side, hidden_rows, rate, slope_rows, slope_own, sums,
):
    feat = head_turn.shape[0]
    lat, lon = place[0], place[1]
    band_rows[:, span(3, rows, cols)] = band_in[:, span(3, rows, cols)]
    hidden_rows[:, span(4, rows - 2, cols)] = hidden_in[:, span(4, rows - 2, cols)]
    rate[:, span(1, rows - 2, cols)] = rate_in[:, span(1, rows - 2, cols)]

    side[...] = strips[...].astype(F32)
    up_tail = above[:, 3 * cols :].astype(F32)
    down_tail = below[:, 3 * cols :].astype(F32)
    for column in range(10):
        at = slice(column * GROUP, (column + 1) * GROUP)
        side[at, 0:3] = up_tail[:, column * 3 : column * 3 + 3]
        side[at, 3 + rows : 6 + rows] = down_tail[:, column * 3 : column * 3 + 3]

    insides = strip_inside(place, rows, lat_count, lon_count)
    hidden_side = strip_hidden(side, one_strip, insides, (0, 1, 2, 5, 6, 7))
    hidden_taps = [turned_rows(value) for value in hidden_side]
    strip_pre = None
    for col in range(3):
        weight = jnp.concatenate(
            [two_main[u * feat : (u + 1) * feat, col * feat : (col + 1) * feat] for u in range(3)], axis=1
        )
        term = dot(weight, jnp.concatenate([hidden_taps[col], hidden_taps[3 + col]], axis=1))
        strip_pre = term if strip_pre is None else strip_pre + term

    band_sides = (
        side[2 * GROUP : 3 * GROUP, :].astype(BF16),
        side[7 * GROUP : 8 * GROUP, :].astype(BF16),
    )
    put_shifted(band_rows, above[:, 0 : 3 * cols], 0, 3, *band_sides, GROUP, cols)
    put_shifted(band_rows, below[:, 0 : 3 * cols], rows + 3, 3, *band_sides, GROUP, cols)

    top_inside, bottom_inside = lat > 0, lat < lat_count - 1
    hidden_sides = (hidden_side[1].astype(BF16), hidden_side[4].astype(BF16))
    near = jnp.concatenate(
        [above_below(band_rows, 1, 3, cols), above_below(band_rows, rows + 2, 3, cols)], axis=1
    )
    pre = dot(one_main[...], near)
    gate = sigmoid(pre)
    soft = pre * gate
    ends = gate + soft * (1.0 - gate)
    rate[:, span(0, 1, cols)] = ends[:, span(2, 1, cols)]
    rate[:, span(rows - 1, 1, cols)] = ends[:, span(3, 1, cols)]
    lane = iota((1, 6 * cols), 1)
    soft = jnp.where(((lane >= 2 * cols) | top_inside) & ((lane < 4 * cols) | bottom_inside), soft, 0.0)
    soft = soft.astype(BF16)
    put_shifted(hidden_rows, soft[:, span(0, 3, cols)], 1, 3, *hidden_sides, feat, cols)
    put_shifted(hidden_rows, soft[:, span(3, 3, cols)], rows + 2, 3, *hidden_sides, feat, cols)

    def label_of(row, count):
        return band_rows[GROUP + bands : GROUP + bands + 1, span(row, count, cols)].astype(F32).astype(jnp.int32)

    pre = [conv_rows(two_main, hidden_rows, row, 1, cols) for row in (2, rows + 3)]
    label = [side[c * GROUP + bands : c * GROUP + bands + 1, :].astype(jnp.int32) for c in (2, 7)]
    label += [label_of(row, 1) for row in (2, rows + 3)]
    ones = jnp.ones((1, cols), jnp.int32)
    mask = [jnp.where(inside, 1, 0) for inside in insides[1:]]
    mask += [jnp.where(inside, ones, 0) for inside in (top_inside, bottom_inside)]
    slope = head_stage(
        jnp.concatenate([strip_pre] + pre, axis=1),
        jnp.concatenate(label, axis=1),
        jnp.concatenate(mask, axis=1) > 0,
        head_pad[...],
        head_turn[...],
        classes,
    )[2]
    slope_side = (slope[:, 0:128], slope[:, 128:256])
    put_shifted(slope_rows, slope[:, 256 : 256 + cols], 2, 1, *slope_side, feat, cols)
    put_shifted(slope_rows, slope[:, 256 + cols :], rows + 3, 1, *slope_side, feat, cols)

    for row in (1, rows + 3):
        slope_own[:, span(row, 2, cols)] = jnp.zeros((feat, 2 * cols), BF16)
    grad_head = jnp.zeros((feat, GROUP), F32)
    loss_sum = jnp.zeros((1, 1), F32)
    for row in range(3, rows + 3, step):
        pre = conv_rows(two_main, hidden_rows, row, step, cols)
        skip, error, slope, loss = head_stage(
            pre, label_of(row, step), None, head_pad[...], head_turn[...], classes
        )
        skip_out[:, span(row - 3, step, cols)] = skip
        slope_own[:, span(row, step, cols)] = slope
        grad_head = grad_head + dot_nt(skip, error)
        put_shifted(slope_rows, slope, row, step, *slope_side, feat, cols)
        loss_sum = loss_sum + jnp.sum(loss, axis=1, keepdims=True)

    def grad_of(product):
        total = None
        for row in range(2, rows + 4, 11):
            count = min(11, rows + 4 - row)
            term = product(below_above(slope_own, row, count, cols), span(row, count, cols))
            total = term if total is None else total + term
        return total

    sums[...] = jnp.zeros_like(sums)
    sums[:, 0 : 3 * feat] = grad_of(lambda slopes, at: dot_nt(slopes, hidden_rows[:, at]))
    for row in range(3, rows + 3, step):
        back = conv_rows(two_back, slope_rows, row, step, cols)
        slope_own[:, span(row, step, cols)] = (back * rate[:, span(row - 3, step, cols)]).astype(BF16)
    sums[:, 3 * feat : 3 * feat + 3 * GROUP] = grad_of(lambda slopes, at: dot_nt(slopes, band_rows[:, at]))
    at = 3 * feat + 3 * GROUP
    sums[0:feat, at : at + GROUP] = grad_head
    sums[feat : feat + 1, at : at + 1] = loss_sum
    half = 3 * feat // 2
    core = lon % 2
    keep_out[...] = sums[pl.ds(pl.multiple_of(core * half, 8), half), :]
    send_out[...] = sums[pl.ds(pl.multiple_of((1 - core) * half, 8), half), :]


def finish_kernel(pixels, me_ref, own, mate, grad_one, grad_two, grad_head, loss, sums):
    half = own.shape[0]
    feat = grad_two.shape[1]
    bands = grad_one.shape[1]
    classes = grad_head.shape[0]
    core = me_ref[0] % 2
    scale = 1.0 / pixels
    sums[pl.ds(pl.multiple_of(core * half, 8), half), :] = own[...] * scale
    sums[pl.ds(pl.multiple_of((1 - core) * half, 8), half), :] = mate[...] * scale
    at = 3 * feat
    turned = jnp.transpose(sums[:, at : at + 3 * GROUP + GROUP])
    for tap in range(9):
        u, v = tap // 3, tap % 3
        grad_two[tap] = sums[u * feat : (u + 1) * feat, v * feat : (v + 1) * feat]
        grad_one[tap] = turned[v * GROUP : v * GROUP + bands, u * feat : (u + 1) * feat]
    grad_head[...] = turned[3 * GROUP : 3 * GROUP + classes, 0:feat]
    loss_row = turned[3 * GROUP : 3 * GROUP + 1]
    loss[...] = loss_row[:, feat : feat + 1] + loss_row[:, feat + GROUP : feat + GROUP + 1]


def tree_sum(values):
    values = list(values)
    while len(values) > 1:
        values = [values[i + 1] + values[i] for i in range(0, len(values), 2)]
    return values[0]


def body(
    patches,
    requests,
    footprint,
    weight_index,
    composite_weights,
    labels,
    conv1_weight,
    conv2_weight,
    head_weight,
):
    lon_count = lax.axis_size("lon")
    lat_count = lax.axis_size("lat")
    chips = lon_count // 2
    rows, slots = footprint.shape
    cols = labels.shape[1]
    store, row_width = patches.shape
    bands = row_width // cols
    bucket = requests.shape[1] // lon_count
    feat = conv2_weight.shape[1]
    classes = head_weight.shape[0]
    vmem = pl.BlockSpec(memory_space=pltpu.VMEM)
    smem = pl.BlockSpec(memory_space=pltpu.SMEM)

    lon = lax.axis_index("lon")
    place = jnp.stack([lax.axis_index("lat"), lon]).astype(jnp.int32)
    me = lon.astype(jnp.int32).reshape(1)

    def by_lon(value, move):
        return lax.ppermute(value, "lon", [(i, i ^ move) for i in range(lon_count)])

    hbm = pl.BlockSpec(memory_space=pltpu.HBM)
    plan, tile_labels = call(
        functools.partial(plan_kernel, store),
        [struct((lon_count, 16, 128), F32), struct((rows, cols), F32)],
        [
            pltpu.VMEM(requests.shape, jnp.int32),
            pltpu.VMEM((slots, rows), jnp.int32),
            pltpu.VMEM((slots, rows), jnp.int32),
            pltpu.SMEM(composite_weights.shape, F32),
            pltpu.VMEM(labels.shape, jnp.int32),
            pltpu.SemaphoreType.DMA((5,)),
        ],
        vmem_limit=63 * 1024 * 1024,
        in_specs=[hbm] * 5,
    )(requests, footprint.T, weight_index.T, composite_weights, labels)
    plan, patches = lax.optimization_barrier((plan, patches))
    mate_patches = by_lon(patches, 1)
    plans = lax.all_to_all(plan, "lon", split_axis=0, concat_axis=0, tiled=True)
    stored, edge = call(
        functools.partial(store_kernel, bands),
        [struct((2 * store, row_width), BF16), struct((6 * GROUP, 2 * store), BF16)],
        in_specs=[smem, vmem, vmem],
        cost_estimate=pl.CostEstimate(flops=10**9, bytes_accessed=10**7, transcendentals=0),
    )(me, patches, mate_patches)
    plans, stored, edge = lax.optimization_barrier((plans, stored, edge))
    moves = list(range(chips - 1, 0, -1))
    parts = []
    for some in (moves, [0]):
        parts += call(
            functools.partial(part_kernel, some),
            [struct((rows, row_width + 2 * rows), BF16 if move else F32) for move in some],
            [
                pltpu.VMEM((chips, 2 * store, 2 * rows), F32),
                pltpu.VMEM((2 * rows, 2 * store), F32),
                pltpu.VMEM((chips + 2, 6 * GROUP, 2 * rows), F32),
            ],
            in_specs=[smem, vmem, vmem, vmem],
            cost_estimate=pl.CostEstimate(flops=10**9, bytes_accessed=10**7, transcendentals=0),
        )(me, plans, stored, edge)
    parts = [by_lon(part, 2 * move) for move, part in zip(moves, parts)] + parts[-1:]
    main, strips, upper, lower = call(
        functools.partial(composite_kernel, bands),
        [
            struct((GROUP, rows * cols), BF16),
            struct((10 * GROUP, 128), BF16),
            struct((GROUP, 3 * cols + 128), BF16),
            struct((GROUP, 3 * cols + 128), BF16),
        ],
        [
            pltpu.VMEM((GROUP * rows, cols), F32),
            pltpu.VMEM((10 * GROUP, 128), F32),
            pltpu.VMEM((GROUP, 128), F32),
        ],
        in_specs=[smem] + [vmem] * (2 + chips),
    )(me, plans, tile_labels, *parts)
    below = lax.ppermute(upper, "lat", [(i + 1, i) for i in range(lat_count - 1)])
    above = lax.ppermute(lower, "lat", [(i, i + 1) for i in range(lat_count - 1)])

    one_main, one_strip, two_main, two_back, head_pad, head_turn = call(
        weights_kernel,
        [
            struct((feat, 9 * GROUP), BF16),
            struct((feat, 9 * GROUP), BF16),
            struct((3 * feat, 3 * feat), BF16),
            struct((3 * feat, 3 * feat), BF16),
            struct((GROUP, feat), BF16),
            struct((feat, GROUP), BF16),
        ],
        [pltpu.VMEM((9 * GROUP, feat), F32), pltpu.VMEM((128, 128), F32)],
    )(conv1_weight.transpose(0, 2, 1), conv2_weight, head_weight)

    ext = rows + 6
    step, outer_step = 16, 32
    band_rows, hidden_rows, rate = call(
        functools.partial(inner_kernel, rows, cols, lat_count, lon_count, step),
        [
            struct((3 * GROUP, ext * cols), BF16),
            struct((3 * feat, ext * cols), BF16),
            struct((feat, rows * cols), F32),
        ],
        [pltpu.VMEM((10 * GROUP, 128), F32)],
        in_specs=[smem] + [vmem] * 4,
        cost_estimate=pl.CostEstimate(flops=10**8, bytes_accessed=10**7, transcendentals=0),
    )(place, main, strips, one_main, one_strip)
    half = 3 * feat // 2
    sum_width = 3 * feat + 4 * GROUP
    skip, keep, send = call(
        functools.partial(outer_kernel, bands, classes, rows, cols, lat_count, lon_count, outer_step),
        [
            struct((feat, rows * cols), BF16),
            struct((half, sum_width), F32),
            struct((half, sum_width), F32),
        ],
        [
            pltpu.VMEM((3 * GROUP, ext * cols), BF16),
            pltpu.VMEM((10 * GROUP, 128), F32),
            pltpu.VMEM((3 * feat, ext * cols), BF16),
            pltpu.VMEM((feat, rows * cols), F32),
            pltpu.VMEM((3 * feat, ext * cols), BF16),
            pltpu.VMEM((feat, ext * cols), BF16),
            pltpu.VMEM((3 * feat, sum_width), F32),
        ],
        in_specs=[smem] + [vmem] * 12,
    )(
        place, strips, above, below, band_rows, hidden_rows, rate,
        one_main, one_strip, two_main, two_back, head_pad, head_turn,
    )

    row_id, lane_id = iota((half, sum_width), 0), iota((half, sum_width), 1)
    at_loss = lane_id == 3 * feat + 3 * GROUP
    at_loss, at_rest = at_loss & (row_id == feat), at_loss & (row_id == feat + GROUP)

    def sum_over(value, axis, moves):
        value = jnp.where(at_loss, value + jnp.roll(value, -GROUP, axis=0), value)
        rounded = lax.reduce_precision(value, 8, 7)
        rest = lax.reduce_precision(jnp.roll(value - rounded, GROUP, axis=0), 8, 7)
        rounded = jnp.where(at_rest, rest, rounded)
        sent = rounded.astype(BF16)
        size = lax.axis_size(axis)
        terms = [rounded]
        for move in moves:
            terms.append(lax.ppermute(sent, axis, [(i, i ^ move) for i in range(size)]).astype(F32))
        return tree_sum(terms)

    total = keep + by_lon(send, 1)
    total = sum_over(total, "lon", range(2, lon_count, 2))
    total = sum_over(total, "lat", range(1, lat_count))
    other = by_lon(total, 1)
    pixels = rows * cols * lat_count * lon_count
    grad_one, grad_two, grad_head, loss = call(
        functools.partial(finish_kernel, pixels),
        [
            struct((9, bands, feat), F32),
            struct((9, feat, feat), F32),
            struct((classes, feat), F32),
            struct((1, 1), F32),
        ],
        [pltpu.VMEM((3 * feat, sum_width), F32)],
        in_specs=[smem, vmem, vmem],
    )(me, total, other)
    return skip.reshape(feat, rows, cols), grad_one.transpose(0, 2, 1), grad_two, grad_head, loss.reshape(())


def solution(mesh):
    placed = (
        P(("lat", "lon"), None),
        P("lat", "lon"),
        P("lat", "lon"),
        P("lat", "lon"),
        P(),
        P("lat", "lon"),
        P(),
        P(),
        P(),
    )
    return jax.shard_map(
        body,
        mesh=mesh,
        in_specs=placed,
        out_specs=(P(None, "lat", "lon"), P(), P(), P(), P()),
        check_vma=False,
    )
```

```python
import functools

import jax
import jax.numpy as jnp
from jax import lax
from jax.experimental import pallas as pl
from jax.experimental.pallas import tpu as pltpu
from jax.sharding import PartitionSpec as P

BF16 = jnp.bfloat16
F32 = jnp.float32
GROUP = 16
VMEM_LIMIT = 28 * 1024 * 1024


def dot(left, right):
    return lax.dot_general(left, right, (((1,), (0,)), ((), ())), preferred_element_type=F32)


def dot_nt(left, right):
    return lax.dot_general(left, right, (((1,), (1,)), ((), ())), preferred_element_type=F32)


def iota(shape, dim):
    return lax.broadcasted_iota(jnp.int32, shape, dim)


def call(kernel, out_shape, scratch=(), vmem_limit=VMEM_LIMIT, **kwargs):
    return pl.pallas_call(
        kernel,
        out_shape=out_shape,
        scratch_shapes=list(scratch),
        compiler_params=pltpu.CompilerParams(vmem_limit_bytes=vmem_limit),
        **kwargs,
    )


def struct(shape, dtype):
    return jax.ShapeDtypeStruct(shape, dtype)


def plan_kernel(
    store, requests_hbm, footprint_hbm, weight_index_hbm, levels_hbm, labels_hbm, out, labels_out,
    requests, footprint, weight_index, levels, labels, sems,
):
    copies = [
        pltpu.make_async_copy(source, target, sems.at[i])
        for i, (source, target) in enumerate(
            (
                (footprint_hbm, footprint),
                (requests_hbm, requests),
                (weight_index_hbm, weight_index),
                (levels_hbm, levels),
                (labels_hbm, labels),
            )
        )
    ]
    for copy in copies:
        copy.start()
    for copy in copies:
        copy.wait()
    slots, rows = footprint.shape
    patch_cols = labels.shape[1]
    count = out.shape[0]
    bucket = requests.shape[1] // count
    foot = footprint[...]
    level_of = weight_index[...]
    weight = jnp.zeros((slots, rows), F32)
    for level in range(levels.shape[0]):
        weight = jnp.where(level_of == level, levels[level], weight)
    weight = jnp.where(foot >= 0, weight, 0.0)
    weight = weight / jnp.sum(weight, axis=0, keepdims=True)
    flat = jnp.concatenate([foot[slot : slot + 1] for slot in range(slots)], axis=1)
    owner = jnp.right_shift(flat, bucket.bit_length() - 1)
    place = jnp.bitwise_and(flat, bucket - 1)
    at_place = jnp.where(iota((bucket, slots * rows), 0) == place, 1.0, 0.0).astype(BF16)
    asked = requests[...].astype(F32)
    asked = jnp.concatenate([asked[:, i * bucket : (i + 1) * bucket] for i in range(count)], axis=0)
    offset = dot(asked.astype(BF16), at_place)
    offset = jnp.sum(jnp.where(iota(offset.shape, 0) == owner, offset, 0.0), axis=0, keepdims=True)
    entry = offset + (owner * store).astype(F32)
    entry = jnp.concatenate([entry[:, slot * rows : (slot + 1) * rows] for slot in range(slots)], axis=0)
    lane = iota((8, patch_cols), 1)
    side = iota((8, patch_cols), 0)
    pick = ((side == 0) & (lane == 0)) | ((side == 1) & (lane == patch_cols - 1))
    label = labels[...].astype(F32)
    labels_out[...] = label
    edges = dot_nt(jnp.where(pick, 1.0, 0.0).astype(BF16), label.astype(BF16))
    entries = jnp.concatenate([entry, edges], axis=1)
    weights = jnp.concatenate([weight, jnp.zeros_like(weight)], axis=1)
    for target in range(count):
        out[target, 0:slots, :] = entries
        out[target, slots : 2 * slots, :] = weights


def store_kernel(bands, me_ref, own, mate, stored, edge):
    store, row_width = own.shape
    patch_cols = row_width // bands
    core = me_ref[0] % 2
    stored[pl.ds(pl.multiple_of(core * store, 64), store), :] = own[...]
    stored[pl.ds(pl.multiple_of((1 - core) * store, 64), store), :] = mate[...]
    row_id = iota((6 * GROUP, patch_cols), 0)
    lane_id = iota((6 * GROUP, patch_cols), 1)
    column = row_id // GROUP
    column_lane = jnp.where(column < 3, column + (patch_cols - 3), column - 3)
    at_column = lane_id == column_lane
    total = jnp.zeros(edge.shape, F32)
    for band in range(bands):
        pick = jnp.where(at_column & (row_id % GROUP == band), 1.0, 0.0).astype(BF16)
        total = total + dot_nt(pick, stored[:, band * patch_cols : (band + 1) * patch_cols])
    edge[...] = total.astype(BF16)


def put_weights(plans, chip, first, target):
    held, lanes = target.shape
    rows = lanes // 2
    slots = plans.shape[1] // 2
    both = jnp.concatenate([plans[2 * chip, :, 0:rows], plans[2 * chip + 1, :, 0:rows]], axis=1)
    entries, weights = both[0:slots] - first, both[slots:]
    for start in range(0, held, 64):
        stored_row = (iota((64, lanes), 0) + start).astype(F32)
        total = jnp.zeros((64, lanes), F32)
        for slot in range(slots):
            total = total + jnp.where(entries[slot : slot + 1] == stored_row, weights[slot : slot + 1], 0.0)
        target[start : start + 64, :] = total


def high_low(value):
    high = value.astype(BF16)
    return high, (value - high.astype(F32)).astype(BF16)


END_LINES = 80


def ends_part_kernel(moves, bands, me_ref, plans, stored, edge, row_weights, *refs):
    smalls, (over, sides, product, lines) = refs[:-4], refs[-4:]
    chips = plans.shape[0] // 2
    _, rows, held = row_weights.shape
    cols = stored.shape[1] // bands
    me = me_ref[0]
    here, core = me // 2, me % 2
    first = (here * held).astype(F32)
    sides[0] = jnp.zeros(sides.shape[1:], F32)
    sides[chips + 1] = jnp.zeros(sides.shape[1:], F32)
    for chip in range(chips):
        put_weights(plans, chip, first, over.at[chip])
        high, low = high_low(over[chip])
        sides[chip + 1] = dot(edge[...], high) + dot(edge[...], low)
    ends = []
    for i, move in enumerate(moves):
        both = jnp.transpose(over[jnp.bitwise_xor(here, move)])
        weights = jnp.where(core == 0, both[0:rows], both[rows:])
        row_weights[i] = weights
        ends += [weights[0:3], weights[rows - 3 : rows]]
    high, low = high_low(jnp.concatenate(ends, axis=0))
    count = high.shape[0]
    both = dot(jnp.concatenate([high, low], axis=0), stored[...])
    product[...] = both[0:count] + both[count:]
    for i, (move, small) in enumerate(zip(moves, smalls, strict=True)):
        lines[...] = jnp.zeros_like(lines)
        for band in range(bands):
            lines[6 * band : 6 * band + 6, :] = product[6 * i : 6 * i + 6, band * cols : (band + 1) * cols]
        small[0:END_LINES, :] = lines[...].astype(small.dtype)
        chip = jnp.bitwise_xor(here, move)
        near, before, after = sides[chip + 1], sides[chip], sides[chip + 2]
        left = jnp.where(core == 1, near[0 : 3 * GROUP, 0:rows], before[0 : 3 * GROUP, rows:])
        right = jnp.where(core == 0, near[3 * GROUP :, rows:], after[3 * GROUP :, 0:rows])
        small[END_LINES:, :] = jnp.concatenate([left, right], axis=1).astype(small.dtype)


def part_kernel(indices, stored, row_weights, *outs):
    rows = outs[0].shape[0]
    row_width = stored.shape[1]
    for index, out in zip(indices, outs, strict=True):
        high, low = high_low(row_weights[index])
        both = jnp.concatenate([high, low], axis=0)
        for start in range(0, row_width, 512):
            stop = min(start + 512, row_width)
            product = dot(both, stored[:, start:stop])
            out[:, start:stop] = (product[:rows] + product[rows:]).astype(out.dtype)


def ends_kernel(bands, me_ref, plans, labels, *refs):
    count = plans.shape[0]
    rows, cols = labels.shape
    smalls, (upper, lower, total, bundle) = refs[:-4], refs[-4:]
    me = me_ref[0]
    value = smalls[0][...].astype(F32)
    for small in smalls[1:]:
        value = value + small[...].astype(F32)
    total[...] = value
    before = plans[jnp.maximum(me - 1, 0), 1:2, rows : 2 * rows]
    after = plans[jnp.minimum(me + 1, count - 1), 0:1, rows : 2 * rows]
    for target, start, end in ((upper, 0, 0), (lower, rows - 3, 3)):
        bundle[...] = jnp.zeros_like(bundle)
        for i in range(3):
            line = jnp.concatenate(
                [
                    total[pl.ds(end + i, bands, stride=6), :],
                    labels[start + i : start + i + 1, :],
                    jnp.zeros((GROUP - bands - 1, cols), F32),
                ],
                axis=0,
            )
            target[:, i * cols : (i + 1) * cols] = line.astype(BF16)
            for column, at in ((3, 0), (4, 1), (5, cols - 2), (6, cols - 1)):
                bundle[:, column * 3 + i : column * 3 + i + 1] = line[:, at : at + 1]
        for column in range(3):
            group = total[END_LINES + column * GROUP : END_LINES + (column + 1) * GROUP, :]
            bundle[:, column * 3 : column * 3 + 3] = group[:, start : start + 3]
            at = (column + 7) * 3
            bundle[:, at : at + 3] = group[:, rows + start : rows + start + 3]
        bundle[bands : bands + 1, 6:9] = before[:, start : start + 3]
        bundle[bands : bands + 1, 21:24] = after[:, start : start + 3]
        target[:, 3 * cols :] = bundle[...].astype(BF16)


def composite_kernel(bands, me_ref, plans, labels, *refs):
    count = plans.shape[0]
    tile_rows, patch_cols = labels.shape
    inputs, (main, strips, bank, side) = refs[:-4], refs[-4:]
    parts, smalls = inputs[: len(inputs) // 2], inputs[len(inputs) // 2 :]
    me = me_ref[0]
    for band in range(bands):
        columns = slice(band * patch_cols, (band + 1) * patch_cols)
        total = parts[0][:, columns].astype(F32)
        for part in parts[1:]:
            total = total + part[:, columns].astype(F32)
        bank[band * tile_rows : (band + 1) * tile_rows, :] = total
    bank[bands * tile_rows : (bands + 1) * tile_rows, :] = labels[...]
    bank[(bands + 1) * tile_rows : GROUP * tile_rows, :] = jnp.zeros(
        ((GROUP - bands - 1) * tile_rows, patch_cols), F32
    )
    for row in range(tile_rows):
        main[:, row * patch_cols : (row + 1) * patch_cols] = bank[
            pl.ds(row, GROUP, stride=tile_rows), :
        ].astype(BF16)

    far = smalls[0][END_LINES:, :].astype(F32)
    for small in smalls[1:]:
        far = far + small[END_LINES:, :].astype(F32)
    side[...] = jnp.zeros_like(side)
    side[0 : 3 * GROUP, 3 : 3 + tile_rows] = far[:, :tile_rows]
    side[7 * GROUP : 10 * GROUP, 3 : 3 + tile_rows] = far[:, tile_rows:]
    before = plans[jnp.maximum(me - 1, 0), 1:2, tile_rows : 2 * tile_rows]
    after = plans[jnp.minimum(me + 1, count - 1), 0:1, tile_rows : 2 * tile_rows]
    side[2 * GROUP + bands : 2 * GROUP + bands + 1, 3 : 3 + tile_rows] = before
    side[7 * GROUP + bands : 7 * GROUP + bands + 1, 3 : 3 + tile_rows] = after
    row_id = iota((4 * GROUP, patch_cols), 0)
    lane_id = iota((4 * GROUP, patch_cols), 1)
    near = jnp.zeros((4 * GROUP, tile_rows), F32)
    column = row_id // GROUP
    column_lane = jnp.where(column < 2, column, column + (patch_cols - 4))
    for band in range(bands):
        pick = (row_id % GROUP == band) & (lane_id == column_lane)
        tile = bank[band * tile_rows : (band + 1) * tile_rows, :].astype(BF16)
        near = near + dot_nt(jnp.where(pick, 1.0, 0.0).astype(BF16), tile)
    side[3 * GROUP : 7 * GROUP, 3 : 3 + tile_rows] = near
    strips[...] = side[...].astype(BF16)


def weights_kernel(conv1, conv2, head, one_main, one_strip, two_main, two_back, head_pad, head_turn, wide, tall):
    bands = conv1.shape[1]
    feat = conv2.shape[1]
    classes = head.shape[0]
    wide[...] = jnp.zeros_like(wide)
    for tap in range(9):
        wide[tap * GROUP : tap * GROUP + bands, :] = conv1[tap].astype(F32)
    one_main[...] = jnp.transpose(wide[...]).astype(BF16)
    for tap in range(9):
        wide[tap * GROUP : tap * GROUP + bands, :] = conv1[(tap % 3) * 3 + tap // 3].astype(F32)
    one_strip[...] = jnp.transpose(wide[...]).astype(BF16)
    for row in range(3):
        at = slice(row * feat, (row + 1) * feat)
        two_main[at, :] = jnp.concatenate([conv2[row * 3 + col] for col in range(3)], axis=1)
        turned = jnp.concatenate([conv2[8 - (row * 3 + col)].astype(F32) for col in range(3)], axis=0)
        two_back[at, :] = jnp.transpose(turned).astype(BF16)
    tall[...] = jnp.zeros_like(tall)
    tall[0:classes, 0:feat] = head[...].astype(F32)
    padded = tall[...]
    head_pad[...] = padded[0:GROUP, 0:feat].astype(BF16)
    head_turn[...] = jnp.transpose(padded)[0:feat, 0:GROUP].astype(BF16)


def sigmoid(value):
    return 0.5 * jnp.tanh(0.5 * value) + 0.5


def head_stage(pre, label, mask, head_pad, head_turn, classes):
    gate = sigmoid(pre)
    soft = pre * gate
    skip = soft.astype(BF16)
    logits = dot(head_pad, skip)
    rank = iota(logits.shape, 0)
    real = rank < classes
    total = jnp.sum(jnp.where(real, jnp.exp(logits), 0.0), axis=0, keepdims=True)
    log_total = jnp.log(total)
    chosen = rank == label
    error = jnp.where(real, jnp.exp(logits - log_total) - jnp.where(chosen, 1.0, 0.0), 0.0)
    error = error.astype(BF16)
    loss = log_total - jnp.sum(jnp.where(chosen, logits, 0.0), axis=0, keepdims=True)
    back = dot(head_turn, error)
    slope = back * (gate + soft * (1.0 - gate))
    if mask is not None:
        slope = jnp.where(mask, slope, 0.0)
    return skip, error, slope.astype(BF16), loss


def span(row, count, cols):
    return slice(row * cols, (row + count) * cols)


def put_shifted(target, value, row, count, left_side, right_side, size, cols):
    lane = iota((1, cols), 1)
    target[size : 2 * size, span(row, count, cols)] = value
    for i in range(count):
        tile = value[:, i * cols : (i + 1) * cols]
        turn = (128 - (row + i)) % 128
        left = pltpu.roll(left_side, turn, 1)
        right = pltpu.roll(right_side, (turn + cols - 1) % 128, 1)
        target[0:size, span(row + i, 1, cols)] = jnp.where(lane == 0, left, pltpu.roll(tile, 1, 1))
        target[2 * size : 3 * size, span(row + i, 1, cols)] = jnp.where(
            lane == cols - 1, right, pltpu.roll(tile, cols - 1, 1)
        )


def above_below(ref, row, count, cols):
    return jnp.concatenate([ref[:, span(row + u, count, cols)] for u in (-1, 0, 1)], axis=0)


def below_above(ref, row, count, cols):
    return jnp.concatenate([ref[:, span(row - u, count, cols)] for u in (-1, 0, 1)], axis=0)


def conv_rows(weight, ref, row, count, cols):
    feat = weight.shape[0] // 3
    near = dot(weight[...], ref[:, span(row - 1, count + 2, cols)])
    return (
        near[0:feat, span(0, count, cols)]
        + near[feat : 2 * feat, span(1, count, cols)]
        + near[2 * feat :, span(2, count, cols)]
    )


def turned_rows(value):
    return jnp.concatenate(
        [pltpu.roll(value, 1, 1), value, pltpu.roll(value, value.shape[1] - 1, 1)], axis=0
    ).astype(BF16)


def strip_inside(place, rows, lat_count, lon_count):
    lat, lon = place[0], place[1]
    lane_row = iota((1, 128), 1) - 3
    inside = (lat * rows + lane_row >= 0) & (lat * rows + lane_row < lat_count * rows)
    inside = inside & (lane_row < rows + 3)
    return inside, inside & (lon > 0), inside & (lon < lon_count - 1)


def strip_hidden(side, one_strip, insides, firsts):
    inside, left_inside, right_inside = insides
    taps = {}
    for first in firsts:
        for column in range(first, first + 3):
            if column not in taps:
                taps[column] = turned_rows(side[column * GROUP : (column + 1) * GROUP, :])
    near = jnp.concatenate(
        [jnp.concatenate([taps[first + i] for first in firsts], axis=1) for i in range(3)], axis=0
    )
    pre = dot(one_strip[...], near)
    soft = pre * sigmoid(pre)
    hidden = []
    for i, first in enumerate(firsts):
        mask = left_inside if first in (0, 1) else right_inside if first in (6, 7) else inside
        hidden.append(jnp.where(mask, soft[:, i * 128 : (i + 1) * 128], 0.0))
    return hidden


def hidden_chunk(one_main, band_rows, hidden_rows, rate, row, count, mask, sides, cols):
    pre = dot(one_main[...], above_below(band_rows, row, count, cols))
    gate = sigmoid(pre)
    soft = pre * gate
    if rate is not None:
        rate[:, span(row - 3, count, cols)] = gate + soft * (1.0 - gate)
    if mask is not None:
        soft = jnp.where(mask, soft, 0.0)
    put_shifted(hidden_rows, soft.astype(BF16), row, count, *sides, pre.shape[0], cols)


def label_rows(band_rows, bands, row, count, cols):
    return band_rows[GROUP + bands : GROUP + bands + 1, span(row, count, cols)].astype(F32).astype(jnp.int32)


def network_kernel(
    bands, classes, rows, cols, lat_count, lon_count, step,
    place, main, strips, above, below,
    one_main, one_strip, two_main, two_back, head_pad, head_turn,
    skip_out, keep_out, send_out,
    band_rows, side, hidden_rows, rate, slope_rows, slope_own, sums,
):
    feat = head_turn.shape[0]
    lat, lon = place[0], place[1]

    side[...] = strips[...].astype(F32)
    up_tail = above[:, 3 * cols :].astype(F32)
    down_tail = below[:, 3 * cols :].astype(F32)
    for column in range(10):
        at = slice(column * GROUP, (column + 1) * GROUP)
        side[at, 0:3] = up_tail[:, column * 3 : column * 3 + 3]
        side[at, 3 + rows : 6 + rows] = down_tail[:, column * 3 : column * 3 + 3]

    insides = strip_inside(place, rows, lat_count, lon_count)
    hidden_side = strip_hidden(side, one_strip, insides, (0, 1, 2, 5, 6, 7))
    hidden_taps = [turned_rows(value) for value in hidden_side]
    strip_pre = None
    for col in range(3):
        weight = jnp.concatenate(
            [two_main[u * feat : (u + 1) * feat, col * feat : (col + 1) * feat] for u in range(3)], axis=1
        )
        term = dot(weight, jnp.concatenate([hidden_taps[col], hidden_taps[3 + col]], axis=1))
        strip_pre = term if strip_pre is None else strip_pre + term

    band_sides = (
        side[2 * GROUP : 3 * GROUP, :].astype(BF16),
        side[7 * GROUP : 8 * GROUP, :].astype(BF16),
    )
    put_shifted(band_rows, above[:, 0 : 3 * cols], 0, 3, *band_sides, GROUP, cols)
    put_shifted(band_rows, below[:, 0 : 3 * cols], rows + 3, 3, *band_sides, GROUP, cols)
    put_shifted(band_rows, main[...], 3, rows, *band_sides, GROUP, cols)

    top_inside, bottom_inside = lat > 0, lat < lat_count - 1
    hidden_sides = (hidden_side[1].astype(BF16), hidden_side[4].astype(BF16))
    near = jnp.concatenate(
        [above_below(band_rows, 1, 2, cols), above_below(band_rows, rows + 3, 2, cols)], axis=1
    )
    pre = dot(one_main[...], near)
    soft = pre * sigmoid(pre)
    lane = iota((1, 4 * cols), 1)
    inside = ((lane >= 2 * cols) | top_inside) & ((lane < 2 * cols) | bottom_inside)
    soft = jnp.where(inside, soft, 0.0).astype(BF16)
    put_shifted(hidden_rows, soft[:, span(0, 2, cols)], 1, 2, *hidden_sides, feat, cols)
    put_shifted(hidden_rows, soft[:, span(2, 2, cols)], rows + 3, 2, *hidden_sides, feat, cols)
    for row in range(3, rows + 3, step):
        hidden_chunk(one_main, band_rows, hidden_rows, rate, row, step, None, hidden_sides, cols)

    pre = [conv_rows(two_main, hidden_rows, row, 1, cols) for row in (2, rows + 3)]
    label = [side[c * GROUP + bands : c * GROUP + bands + 1, :].astype(jnp.int32) for c in (2, 7)]
    label += [label_rows(band_rows, bands, row, 1, cols) for row in (2, rows + 3)]
    ones = jnp.ones((1, cols), jnp.int32)
    mask = [jnp.where(inside, 1, 0) for inside in insides[1:]]
    mask += [jnp.where(inside, ones, 0) for inside in (top_inside, bottom_inside)]
    slope = head_stage(
        jnp.concatenate([strip_pre] + pre, axis=1),
        jnp.concatenate(label, axis=1),
        jnp.concatenate(mask, axis=1) > 0,
        head_pad[...],
        head_turn[...],
        classes,
    )[2]
    slope_side = (slope[:, 0:128], slope[:, 128:256])
    put_shifted(slope_rows, slope[:, 256 : 256 + cols], 2, 1, *slope_side, feat, cols)
    put_shifted(slope_rows, slope[:, 256 + cols :], rows + 3, 1, *slope_side, feat, cols)

    for row in (1, rows + 3):
        slope_own[:, span(row, 2, cols)] = jnp.zeros((feat, 2 * cols), BF16)
    grad_head = jnp.zeros((feat, GROUP), F32)
    loss_sum = jnp.zeros((1, 1), F32)
    for row in range(3, rows + 3, step):
        pre = conv_rows(two_main, hidden_rows, row, step, cols)
        label = label_rows(band_rows, bands, row, step, cols)
        skip, error, slope, loss = head_stage(pre, label, None, head_pad[...], head_turn[...], classes)
        skip_out[:, span(row - 3, step, cols)] = skip
        slope_own[:, span(row, step, cols)] = slope
        grad_head = grad_head + dot_nt(skip, error)
        put_shifted(slope_rows, slope, row, step, *slope_side, feat, cols)
        loss_sum = loss_sum + jnp.sum(loss, axis=1, keepdims=True)

    def grad_of(product):
        total = None
        for row in range(2, rows + 4, 11):
            count = min(11, rows + 4 - row)
            term = product(below_above(slope_own, row, count, cols), span(row, count, cols))
            total = term if total is None else total + term
        return total

    sums[...] = jnp.zeros_like(sums)
    sums[:, 0 : 3 * feat] = grad_of(lambda slopes, at: dot_nt(slopes, hidden_rows[:, at]))
    for row in range(3, rows + 3, step):
        back = conv_rows(two_back, slope_rows, row, step, cols)
        slope_own[:, span(row, step, cols)] = (back * rate[:, span(row - 3, step, cols)]).astype(BF16)
    sums[:, 3 * feat : 3 * feat + 3 * GROUP] = grad_of(lambda slopes, at: dot_nt(slopes, band_rows[:, at]))
    at = 3 * feat + 3 * GROUP
    sums[0:feat, at : at + GROUP] = grad_head
    sums[feat : feat + 1, at : at + 1] = loss_sum
    half = 3 * feat // 2
    core = lon % 2
    keep_out[...] = sums[pl.ds(pl.multiple_of(core * half, 8), half), :]
    send_out[...] = sums[pl.ds(pl.multiple_of((1 - core) * half, 8), half), :]


def finish_kernel(pixels, me_ref, own, mate, grad_one, grad_two, grad_head, loss, sums):
    half = own.shape[0]
    feat = grad_two.shape[1]
    bands = grad_one.shape[1]
    classes = grad_head.shape[0]
    core = me_ref[0] % 2
    scale = 1.0 / pixels
    sums[pl.ds(pl.multiple_of(core * half, 8), half), :] = own[...] * scale
    sums[pl.ds(pl.multiple_of((1 - core) * half, 8), half), :] = mate[...] * scale
    at = 3 * feat
    turned = jnp.transpose(sums[:, at : at + 3 * GROUP + GROUP])
    for tap in range(9):
        u, v = tap // 3, tap % 3
        grad_two[tap] = sums[u * feat : (u + 1) * feat, v * feat : (v + 1) * feat]
        grad_one[tap] = turned[v * GROUP : v * GROUP + bands, u * feat : (u + 1) * feat]
    grad_head[...] = turned[3 * GROUP : 3 * GROUP + classes, 0:feat]
    loss_row = turned[3 * GROUP : 3 * GROUP + 1]
    loss[...] = loss_row[:, feat : feat + 1] + loss_row[:, feat + GROUP : feat + GROUP + 1]


def tree_sum(values):
    values = list(values)
    while len(values) > 1:
        values = [values[i] + values[i + 1] for i in range(0, len(values), 2)]
    return values[0]


def body(
    patches,
    requests,
    footprint,
    weight_index,
    composite_weights,
    labels,
    conv1_weight,
    conv2_weight,
    head_weight,
):
    lon_count = lax.axis_size("lon")
    lat_count = lax.axis_size("lat")
    chips = lon_count // 2
    rows, slots = footprint.shape
    cols = labels.shape[1]
    store, row_width = patches.shape
    bands = row_width // cols
    bucket = requests.shape[1] // lon_count
    feat = conv2_weight.shape[1]
    classes = head_weight.shape[0]
    vmem = pl.BlockSpec(memory_space=pltpu.VMEM)
    smem = pl.BlockSpec(memory_space=pltpu.SMEM)

    lon = lax.axis_index("lon")
    place = jnp.stack([lax.axis_index("lat"), lon]).astype(jnp.int32)
    me = lon.astype(jnp.int32).reshape(1)

    def by_lon(value, move):
        return lax.ppermute(value, "lon", [(i, i ^ move) for i in range(lon_count)])

    hbm = pl.BlockSpec(memory_space=pltpu.HBM)
    plan, tile_labels = call(
        functools.partial(plan_kernel, store),
        [struct((lon_count, 16, 128), F32), struct((rows, cols), F32)],
        [
            pltpu.VMEM(requests.shape, jnp.int32),
            pltpu.VMEM((slots, rows), jnp.int32),
            pltpu.VMEM((slots, rows), jnp.int32),
            pltpu.SMEM(composite_weights.shape, F32),
            pltpu.VMEM(labels.shape, jnp.int32),
            pltpu.SemaphoreType.DMA((5,)),
        ],
        vmem_limit=63 * 1024 * 1024,
        in_specs=[hbm] * 5,
    )(requests, footprint.T, weight_index.T, composite_weights, labels)
    plan, patches = lax.optimization_barrier((plan, patches))
    mate_patches = by_lon(patches, 1)
    plans = lax.all_to_all(plan, "lon", split_axis=0, concat_axis=0, tiled=True)
    stored, edge = call(
        functools.partial(store_kernel, bands),
        [struct((2 * store, row_width), BF16), struct((6 * GROUP, 2 * store), BF16)],
        in_specs=[smem, vmem, vmem],
        cost_estimate=pl.CostEstimate(flops=10**9, bytes_accessed=10**7, transcendentals=0),
    )(me, patches, mate_patches)
    plans, stored, edge = lax.optimization_barrier((plans, stored, edge))
    moves = list(range(chips - 1, -1, -1))
    cost = pl.CostEstimate(flops=10**9, bytes_accessed=10**7, transcendentals=0)
    row_weights, *smalls = call(
        functools.partial(ends_part_kernel, moves, bands),
        [struct((chips, rows, 2 * store), F32)]
        + [struct((END_LINES + 3 * GROUP, cols), BF16 if move else F32) for move in moves],
        [
            pltpu.VMEM((chips, 2 * store, 2 * rows), F32),
            pltpu.VMEM((chips + 2, 6 * GROUP, 2 * rows), F32),
            pltpu.VMEM((6 * chips, row_width), F32),
            pltpu.VMEM((END_LINES, cols), F32),
        ],
        in_specs=[smem, vmem, vmem, vmem],
        cost_estimate=cost,
    )(me, plans, stored, edge)
    smalls = [by_lon(small, 2 * move) if move else small for move, small in zip(moves, smalls)]
    parts = []
    for some in (moves[:-1], moves[-1:]):
        parts += call(
            functools.partial(part_kernel, [moves.index(move) for move in some]),
            [struct((rows, row_width), BF16 if move else F32) for move in some],
            in_specs=[vmem, vmem],
            cost_estimate=cost,
        )(stored, row_weights)
    parts = [by_lon(part, 2 * move) if move else part for move, part in zip(moves, parts)]
    upper, lower = call(
        functools.partial(ends_kernel, bands),
        [struct((GROUP, 3 * cols + 128), BF16)] * 2,
        [pltpu.VMEM((END_LINES + 3 * GROUP, cols), F32), pltpu.VMEM((GROUP, 128), F32)],
        in_specs=[smem] + [vmem] * (2 + chips),
        cost_estimate=pl.CostEstimate(flops=3 * 10**10, bytes_accessed=10**7, transcendentals=0),
    )(me, plans, tile_labels, *smalls)
    main, strips = call(
        functools.partial(composite_kernel, bands),
        [struct((GROUP, rows * cols), BF16), struct((10 * GROUP, 128), BF16)],
        [pltpu.VMEM((GROUP * rows, cols), F32), pltpu.VMEM((10 * GROUP, 128), F32)],
        in_specs=[smem] + [vmem] * (2 + 2 * chips),
        cost_estimate=cost,
    )(me, plans, tile_labels, *parts, *smalls)
    below = lax.ppermute(upper, "lat", [(i + 1, i) for i in range(lat_count - 1)])
    above = lax.ppermute(lower, "lat", [(i, i + 1) for i in range(lat_count - 1)])

    one_main, one_strip, two_main, two_back, head_pad, head_turn = call(
        weights_kernel,
        [
            struct((feat, 9 * GROUP), BF16),
            struct((feat, 9 * GROUP), BF16),
            struct((3 * feat, 3 * feat), BF16),
            struct((3 * feat, 3 * feat), BF16),
            struct((GROUP, feat), BF16),
            struct((feat, GROUP), BF16),
        ],
        [pltpu.VMEM((9 * GROUP, feat), F32), pltpu.VMEM((128, 128), F32)],
    )(conv1_weight.transpose(0, 2, 1), conv2_weight, head_weight)

    ext = rows + 6
    half = 3 * feat // 2
    sum_width = 3 * feat + 4 * GROUP
    skip, keep, send = call(
        functools.partial(network_kernel, bands, classes, rows, cols, lat_count, lon_count, 32),
        [
            struct((feat, rows * cols), BF16),
            struct((half, sum_width), F32),
            struct((half, sum_width), F32),
        ],
        [
            pltpu.VMEM((3 * GROUP, ext * cols), BF16),
            pltpu.VMEM((10 * GROUP, 128), F32),
            pltpu.VMEM((3 * feat, ext * cols), BF16),
            pltpu.VMEM((feat, rows * cols), F32),
            pltpu.VMEM((3 * feat, ext * cols), BF16),
            pltpu.VMEM((feat, ext * cols), BF16),
            pltpu.VMEM((3 * feat, sum_width), F32),
        ],
        in_specs=[smem] + [vmem] * 10,
    )(
        place, main, strips, above, below,
        one_main, one_strip, two_main, two_back, head_pad, head_turn,
    )

    row_id, lane_id = iota((half, sum_width), 0), iota((half, sum_width), 1)
    at_loss = lane_id == 3 * feat + 3 * GROUP
    at_loss, at_rest = at_loss & (row_id == feat), at_loss & (row_id == feat + GROUP)

    def sum_over(value, axis, moves):
        value = jnp.where(at_loss, value + jnp.roll(value, -GROUP, axis=0), value)
        rounded = lax.reduce_precision(value, 8, 7)
        rest = lax.reduce_precision(jnp.roll(value - rounded, GROUP, axis=0), 8, 7)
        rounded = jnp.where(at_rest, rest, rounded)
        sent = rounded.astype(BF16)
        size = lax.axis_size(axis)
        terms = [rounded]
        for move in moves:
            terms.append(lax.ppermute(sent, axis, [(i, i ^ move) for i in range(size)]).astype(F32))
        return tree_sum(terms)

    total = keep + by_lon(send, 1)
    total = sum_over(total, "lon", range(2, lon_count, 2))
    total = sum_over(total, "lat", range(1, lat_count))
    other = by_lon(total, 1)
    pixels = rows * cols * lat_count * lon_count
    grad_one, grad_two, grad_head, loss = call(
        functools.partial(finish_kernel, pixels),
        [
            struct((9, bands, feat), F32),
            struct((9, feat, feat), F32),
            struct((classes, feat), F32),
            struct((1, 1), F32),
        ],
        [pltpu.VMEM((3 * feat, sum_width), F32)],
        in_specs=[smem, vmem, vmem],
    )(me, total, other)
    return skip.reshape(feat, rows, cols), grad_one.transpose(0, 2, 1), grad_two, grad_head, loss.reshape(())


def solution(mesh):
    placed = (
        P(("lat", "lon"), None),
        P("lat", "lon"),
        P("lat", "lon"),
        P("lat", "lon"),
        P(),
        P("lat", "lon"),
        P(),
        P(),
        P(),
    )
    return jax.shard_map(
        body,
        mesh=mesh,
        in_specs=placed,
        out_specs=(P(None, "lat", "lon"), P(), P(), P(), P()),
        check_vma=False,
    )
```

```python
import functools

import jax
import jax.numpy as jnp
from jax import lax
from jax.experimental import pallas as pl
from jax.experimental.pallas import tpu as pltpu
from jax.sharding import PartitionSpec as P

BF16 = jnp.bfloat16
F32 = jnp.float32
GROUP = 16
VMEM_LIMIT = 28 * 1024 * 1024


def dot(left, right):
    return lax.dot_general(left, right, (((1,), (0,)), ((), ())), preferred_element_type=F32)


def dot_nt(left, right):
    return lax.dot_general(left, right, (((1,), (1,)), ((), ())), preferred_element_type=F32)


def iota(shape, dim):
    return lax.broadcasted_iota(jnp.int32, shape, dim)


def call(kernel, out_shape, scratch=(), vmem_limit=VMEM_LIMIT, **kwargs):
    return pl.pallas_call(
        kernel,
        out_shape=out_shape,
        scratch_shapes=list(scratch),
        compiler_params=pltpu.CompilerParams(vmem_limit_bytes=vmem_limit),
        **kwargs,
    )


def struct(shape, dtype):
    return jax.ShapeDtypeStruct(shape, dtype)


def plan_kernel(
    store, requests_hbm, footprint_hbm, weight_index_hbm, levels_hbm, labels_hbm, out, labels_out,
    requests, footprint, weight_index, levels, labels, sems,
):
    copies = [
        pltpu.make_async_copy(source, target, sems.at[i])
        for i, (source, target) in enumerate(
            (
                (footprint_hbm, footprint),
                (requests_hbm, requests),
                (weight_index_hbm, weight_index),
                (levels_hbm, levels),
                (labels_hbm, labels),
            )
        )
    ]
    for copy in copies:
        copy.start()
    for copy in copies:
        copy.wait()
    slots, rows = footprint.shape
    patch_cols = labels.shape[1]
    count = out.shape[0]
    bucket = requests.shape[1] // count
    foot = footprint[...]
    level_of = weight_index[...]
    weight = jnp.zeros((slots, rows), F32)
    for level in range(levels.shape[0]):
        weight = jnp.where(level_of == level, levels[level], weight)
    weight = jnp.where(foot >= 0, weight, 0.0)
    weight = weight / jnp.sum(weight, axis=0, keepdims=True)
    flat = jnp.concatenate([foot[slot : slot + 1] for slot in range(slots)], axis=1)
    owner = jnp.right_shift(flat, bucket.bit_length() - 1)
    place = jnp.bitwise_and(flat, bucket - 1)
    at_place = jnp.where(iota((bucket, slots * rows), 0) == place, 1.0, 0.0).astype(BF16)
    asked = requests[...].astype(F32)
    asked = jnp.concatenate([asked[:, i * bucket : (i + 1) * bucket] for i in range(count)], axis=0)
    offset = dot(asked.astype(BF16), at_place)
    offset = jnp.sum(jnp.where(iota(offset.shape, 0) == owner, offset, 0.0), axis=0, keepdims=True)
    entry = offset + (owner * store).astype(F32)
    entry = jnp.concatenate([entry[:, slot * rows : (slot + 1) * rows] for slot in range(slots)], axis=0)
    lane = iota((8, patch_cols), 1)
    side = iota((8, patch_cols), 0)
    pick = ((side == 0) & (lane == 0)) | ((side == 1) & (lane == patch_cols - 1))
    label = labels[...].astype(F32)
    labels_out[...] = label
    edges = dot_nt(jnp.where(pick, 1.0, 0.0).astype(BF16), label.astype(BF16))
    entries = jnp.concatenate([entry, edges], axis=1)
    weights = jnp.concatenate([weight, jnp.zeros_like(weight)], axis=1)
    for target in range(count):
        out[target, 0:slots, :] = entries
        out[target, slots : 2 * slots, :] = weights


def store_kernel(bands, me_ref, own, mate, stored, edge, sem):
    store, row_width = own.shape
    patch_cols = row_width // bands
    core = me_ref[0] % 2
    copy = pltpu.make_async_copy(own, stored.at[pl.ds(pl.multiple_of(core * store, 64), store)], sem)
    copy.start()
    stored[pl.ds(pl.multiple_of((1 - core) * store, 64), store), :] = mate[...]
    copy.wait()
    row_id = iota((6 * GROUP, patch_cols), 0)
    lane_id = iota((6 * GROUP, patch_cols), 1)
    column = row_id // GROUP
    column_lane = jnp.where(column < 3, column + (patch_cols - 3), column - 3)
    at_column = lane_id == column_lane
    total = jnp.zeros(edge.shape, F32)
    for band in range(bands):
        pick = jnp.where(at_column & (row_id % GROUP == band), 1.0, 0.0).astype(BF16)
        total = total + dot_nt(pick, stored[:, band * patch_cols : (band + 1) * patch_cols])
    edge[...] = total.astype(BF16)


def put_weights(plans, chip, first, target):
    held, lanes = target.shape
    rows = lanes // 2
    slots = plans.shape[1] // 2
    both = jnp.concatenate([plans[2 * chip, :, 0:rows], plans[2 * chip + 1, :, 0:rows]], axis=1)
    entries, weights = both[0:slots] - first, both[slots:]
    for start in range(0, held, 64):
        stored_row = (iota((64, lanes), 0) + start).astype(F32)
        total = jnp.zeros((64, lanes), F32)
        for slot in range(slots):
            total = total + jnp.where(entries[slot : slot + 1] == stored_row, weights[slot : slot + 1], 0.0)
        target[start : start + 64, :] = total


def high_low(value):
    high = value.astype(BF16)
    return high, (value - high.astype(F32)).astype(BF16)


END_LINES = 80


def ends_part_kernel(moves, bands, me_ref, plans, stored, edge, row_weights, *refs):
    smalls, (over, sides, product, lines) = refs[:-4], refs[-4:]
    chips = plans.shape[0] // 2
    _, rows, held = row_weights.shape
    cols = stored.shape[1] // bands
    me = me_ref[0]
    here, core = me // 2, me % 2
    first = (here * held).astype(F32)
    sides[0] = jnp.zeros(sides.shape[1:], F32)
    sides[chips + 1] = jnp.zeros(sides.shape[1:], F32)
    for chip in range(chips):
        put_weights(plans, chip, first, over.at[chip])
        high, low = high_low(over[chip])
        sides[chip + 1] = dot(edge[...], high) + dot(edge[...], low)
    ends = []
    for i, move in enumerate(moves):
        both = jnp.transpose(over[jnp.bitwise_xor(here, move)])
        weights = jnp.where(core == 0, both[0:rows], both[rows:])
        row_weights[i] = weights
        ends += [weights[0:3], weights[rows - 3 : rows]]
    high, low = high_low(jnp.concatenate(ends, axis=0))
    count = high.shape[0]
    both = dot(jnp.concatenate([high, low], axis=0), stored[...])
    product[...] = both[0:count] + both[count:]
    for i, (move, small) in enumerate(zip(moves, smalls, strict=True)):
        lines[...] = jnp.zeros_like(lines)
        for band in range(bands):
            lines[6 * band : 6 * band + 6, :] = product[6 * i : 6 * i + 6, band * cols : (band + 1) * cols]
        small[0:END_LINES, :] = lines[...].astype(small.dtype)
        chip = jnp.bitwise_xor(here, move)
        near, before, after = sides[chip + 1], sides[chip], sides[chip + 2]
        left = jnp.where(core == 1, near[0 : 3 * GROUP, 0:rows], before[0 : 3 * GROUP, rows:])
        right = jnp.where(core == 0, near[3 * GROUP :, rows:], after[3 * GROUP :, 0:rows])
        small[END_LINES:, :] = jnp.concatenate([left, right], axis=1).astype(small.dtype)


def part_kernel(indices, stored, row_weights, *outs):
    rows = outs[0].shape[0]
    row_width = stored.shape[1]
    for index, out in zip(indices, outs, strict=True):
        high, low = high_low(row_weights[index])
        both = jnp.concatenate([high, low], axis=0)
        for start in range(0, row_width, 512):
            stop = min(start + 512, row_width)
            product = dot(both, stored[:, start:stop])
            out[:, start:stop] = (product[:rows] + product[rows:]).astype(out.dtype)


def ends_kernel(bands, me_ref, plans, labels, *refs):
    count = plans.shape[0]
    rows, cols = labels.shape
    smalls, (upper, lower, total, bundle) = refs[:-4], refs[-4:]
    me = me_ref[0]
    value = smalls[0][...].astype(F32)
    for small in smalls[1:]:
        value = value + small[...].astype(F32)
    total[...] = value
    before = plans[jnp.maximum(me - 1, 0), 1:2, rows : 2 * rows]
    after = plans[jnp.minimum(me + 1, count - 1), 0:1, rows : 2 * rows]
    for target, start, end in ((upper, 0, 0), (lower, rows - 3, 3)):
        bundle[...] = jnp.zeros_like(bundle)
        for i in range(3):
            line = jnp.concatenate(
                [
                    total[pl.ds(end + i, bands, stride=6), :],
                    labels[start + i : start + i + 1, :],
                    jnp.zeros((GROUP - bands - 1, cols), F32),
                ],
                axis=0,
            )
            target[:, i * cols : (i + 1) * cols] = line.astype(BF16)
            for column, at in ((3, 0), (4, 1), (5, cols - 2), (6, cols - 1)):
                bundle[:, column * 3 + i : column * 3 + i + 1] = line[:, at : at + 1]
        for column in range(3):
            group = total[END_LINES + column * GROUP : END_LINES + (column + 1) * GROUP, :]
            bundle[:, column * 3 : column * 3 + 3] = group[:, start : start + 3]
            at = (column + 7) * 3
            bundle[:, at : at + 3] = group[:, rows + start : rows + start + 3]
        bundle[bands : bands + 1, 6:9] = before[:, start : start + 3]
        bundle[bands : bands + 1, 21:24] = after[:, start : start + 3]
        target[:, 3 * cols :] = bundle[...].astype(BF16)


def composite_kernel(bands, me_ref, plans, labels, *refs):
    count = plans.shape[0]
    tile_rows, patch_cols = labels.shape
    inputs, (main, strips, bank, side) = refs[:-4], refs[-4:]
    parts, smalls = inputs[: len(inputs) // 2], inputs[len(inputs) // 2 :]
    me = me_ref[0]
    for band in range(bands):
        columns = slice(band * patch_cols, (band + 1) * patch_cols)
        total = parts[0][:, columns].astype(F32)
        for part in parts[1:]:
            total = total + part[:, columns].astype(F32)
        bank[band * tile_rows : (band + 1) * tile_rows, :] = total
    bank[bands * tile_rows : (bands + 1) * tile_rows, :] = labels[...]
    bank[(bands + 1) * tile_rows : GROUP * tile_rows, :] = jnp.zeros(
        ((GROUP - bands - 1) * tile_rows, patch_cols), F32
    )
    for row in range(tile_rows):
        main[:, row * patch_cols : (row + 1) * patch_cols] = bank[
            pl.ds(row, GROUP, stride=tile_rows), :
        ].astype(BF16)

    far = smalls[0][END_LINES:, :].astype(F32)
    for small in smalls[1:]:
        far = far + small[END_LINES:, :].astype(F32)
    side[...] = jnp.zeros_like(side)
    side[0 : 3 * GROUP, 3 : 3 + tile_rows] = far[:, :tile_rows]
    side[7 * GROUP : 10 * GROUP, 3 : 3 + tile_rows] = far[:, tile_rows:]
    before = plans[jnp.maximum(me - 1, 0), 1:2, tile_rows : 2 * tile_rows]
    after = plans[jnp.minimum(me + 1, count - 1), 0:1, tile_rows : 2 * tile_rows]
    side[2 * GROUP + bands : 2 * GROUP + bands + 1, 3 : 3 + tile_rows] = before
    side[7 * GROUP + bands : 7 * GROUP + bands + 1, 3 : 3 + tile_rows] = after
    row_id = iota((4 * GROUP, patch_cols), 0)
    lane_id = iota((4 * GROUP, patch_cols), 1)
    near = jnp.zeros((4 * GROUP, tile_rows), F32)
    column = row_id // GROUP
    column_lane = jnp.where(column < 2, column, column + (patch_cols - 4))
    for band in range(bands):
        pick = (row_id % GROUP == band) & (lane_id == column_lane)
        tile = bank[band * tile_rows : (band + 1) * tile_rows, :].astype(BF16)
        near = near + dot_nt(jnp.where(pick, 1.0, 0.0).astype(BF16), tile)
    side[3 * GROUP : 7 * GROUP, 3 : 3 + tile_rows] = near
    strips[...] = side[...].astype(BF16)


def weights_kernel(
    conv1_hbm, conv2_hbm, head_hbm, one_main, one_strip, two_main, two_back, head_pad, head_turn,
    wide, tall, conv1, conv2, head, sems,
):
    copies = [
        pltpu.make_async_copy(source, target, sems.at[i])
        for i, (source, target) in enumerate(((conv1_hbm, conv1), (conv2_hbm, conv2), (head_hbm, head)))
    ]
    for copy in copies:
        copy.start()
    for copy in copies:
        copy.wait()
    bands = conv1.shape[1]
    feat = conv2.shape[1]
    classes = head.shape[0]
    wide[...] = jnp.zeros_like(wide)
    for tap in range(9):
        wide[tap * GROUP : tap * GROUP + bands, :] = conv1[tap].astype(F32)
    one_main[...] = jnp.transpose(wide[...]).astype(BF16)
    for tap in range(9):
        wide[tap * GROUP : tap * GROUP + bands, :] = conv1[(tap % 3) * 3 + tap // 3].astype(F32)
    one_strip[...] = jnp.transpose(wide[...]).astype(BF16)
    for row in range(3):
        at = slice(row * feat, (row + 1) * feat)
        two_main[at, :] = jnp.concatenate([conv2[row * 3 + col] for col in range(3)], axis=1)
        turned = jnp.concatenate([conv2[8 - (row * 3 + col)].astype(F32) for col in range(3)], axis=0)
        two_back[at, :] = jnp.transpose(turned).astype(BF16)
    tall[...] = jnp.zeros_like(tall)
    tall[0:classes, 0:feat] = head[...].astype(F32)
    padded = tall[...]
    head_pad[...] = padded[0:GROUP, 0:feat].astype(BF16)
    head_turn[...] = jnp.transpose(padded)[0:feat, 0:GROUP].astype(BF16)


def sigmoid(value):
    return 0.5 * jnp.tanh(0.5 * value) + 0.5


def head_stage(pre, label, mask, head_pad, head_turn, classes):
    gate = sigmoid(pre)
    soft = pre * gate
    skip = soft.astype(BF16)
    logits = dot(head_pad, skip)
    rank = iota(logits.shape, 0)
    real = rank < classes
    total = jnp.sum(jnp.where(real, jnp.exp(logits), 0.0), axis=0, keepdims=True)
    log_total = jnp.log(total)
    chosen = rank == label
    error = jnp.where(real, jnp.exp(logits - log_total) - jnp.where(chosen, 1.0, 0.0), 0.0)
    error = error.astype(BF16)
    loss = log_total - jnp.sum(jnp.where(chosen, logits, 0.0), axis=0, keepdims=True)
    back = dot(head_turn, error)
    slope = back * (gate + soft * (1.0 - gate))
    if mask is not None:
        slope = jnp.where(mask, slope, 0.0)
    return skip, error, slope.astype(BF16), loss


def span(row, count, cols):
    return slice(row * cols, (row + count) * cols)


def put_shifted(target, value, row, count, left_side, right_side, size, cols):
    lane = iota((1, cols), 1)
    target[size : 2 * size, span(row, count, cols)] = value
    for i in range(count):
        tile = value[:, i * cols : (i + 1) * cols]
        turn = (128 - (row + i)) % 128
        left = pltpu.roll(left_side, turn, 1)
        right = pltpu.roll(right_side, (turn + cols - 1) % 128, 1)
        target[0:size, span(row + i, 1, cols)] = jnp.where(lane == 0, left, pltpu.roll(tile, 1, 1))
        target[2 * size : 3 * size, span(row + i, 1, cols)] = jnp.where(
            lane == cols - 1, right, pltpu.roll(tile, cols - 1, 1)
        )


def above_below(ref, row, count, cols):
    return jnp.concatenate([ref[:, span(row + u, count, cols)] for u in (-1, 0, 1)], axis=0)


def below_above(ref, row, count, cols):
    return jnp.concatenate([ref[:, span(row - u, count, cols)] for u in (-1, 0, 1)], axis=0)


def conv_rows(weight, ref, row, count, cols):
    feat = weight.shape[0] // 3
    near = dot(weight[...], ref[:, span(row - 1, count + 2, cols)])
    return (
        near[0:feat, span(0, count, cols)]
        + near[feat : 2 * feat, span(1, count, cols)]
        + near[2 * feat :, span(2, count, cols)]
    )


def turned_rows(value):
    return jnp.concatenate(
        [pltpu.roll(value, 1, 1), value, pltpu.roll(value, value.shape[1] - 1, 1)], axis=0
    ).astype(BF16)


def strip_inside(place, rows, lat_count, lon_count):
    lat, lon = place[0], place[1]
    lane_row = iota((1, 128), 1) - 3
    inside = (lat * rows + lane_row >= 0) & (lat * rows + lane_row < lat_count * rows)
    inside = inside & (lane_row < rows + 3)
    return inside, inside & (lon > 0), inside & (lon < lon_count - 1)


def strip_hidden(side, one_strip, insides, firsts):
    inside, left_inside, right_inside = insides
    taps = {}
    for first in firsts:
        for column in range(first, first + 3):
            if column not in taps:
                taps[column] = turned_rows(side[column * GROUP : (column + 1) * GROUP, :])
    near = jnp.concatenate(
        [jnp.concatenate([taps[first + i] for first in firsts], axis=1) for i in range(3)], axis=0
    )
    pre = dot(one_strip[...], near)
    soft = pre * sigmoid(pre)
    hidden = []
    for i, first in enumerate(firsts):
        mask = left_inside if first in (0, 1) else right_inside if first in (6, 7) else inside
        hidden.append(jnp.where(mask, soft[:, i * 128 : (i + 1) * 128], 0.0))
    return hidden


def hidden_chunk(one_main, band_rows, hidden_rows, rate, row, count, mask, sides, cols):
    pre = dot(one_main[...], above_below(band_rows, row, count, cols))
    gate = sigmoid(pre)
    soft = pre * gate
    if rate is not None:
        rate[:, span(row - 3, count, cols)] = gate + soft * (1.0 - gate)
    if mask is not None:
        soft = jnp.where(mask, soft, 0.0)
    put_shifted(hidden_rows, soft.astype(BF16), row, count, *sides, pre.shape[0], cols)


def label_rows(band_rows, bands, row, count, cols):
    return band_rows[GROUP + bands : GROUP + bands + 1, span(row, count, cols)].astype(F32).astype(jnp.int32)


def network_kernel(
    bands, classes, rows, cols, lat_count, lon_count, step,
    place, main, strips, above, below,
    one_main, one_strip, two_main, two_back, head_pad, head_turn,
    skip_out, keep_out, send_out,
    band_rows, side, hidden_rows, rate, slope_rows, slope_own, sums,
):
    feat = head_turn.shape[0]
    lat, lon = place[0], place[1]

    side[...] = strips[...].astype(F32)
    up_tail = above[:, 3 * cols :].astype(F32)
    down_tail = below[:, 3 * cols :].astype(F32)
    for column in range(10):
        at = slice(column * GROUP, (column + 1) * GROUP)
        side[at, 0:3] = up_tail[:, column * 3 : column * 3 + 3]
        side[at, 3 + rows : 6 + rows] = down_tail[:, column * 3 : column * 3 + 3]

    insides = strip_inside(place, rows, lat_count, lon_count)
    hidden_side = strip_hidden(side, one_strip, insides, (0, 1, 2, 5, 6, 7))
    hidden_taps = [turned_rows(value) for value in hidden_side]
    strip_pre = None
    for col in range(3):
        weight = jnp.concatenate(
            [two_main[u * feat : (u + 1) * feat, col * feat : (col + 1) * feat] for u in range(3)], axis=1
        )
        term = dot(weight, jnp.concatenate([hidden_taps[col], hidden_taps[3 + col]], axis=1))
        strip_pre = term if strip_pre is None else strip_pre + term

    band_sides = (
        side[2 * GROUP : 3 * GROUP, :].astype(BF16),
        side[7 * GROUP : 8 * GROUP, :].astype(BF16),
    )
    put_shifted(band_rows, above[:, 0 : 3 * cols], 0, 3, *band_sides, GROUP, cols)
    put_shifted(band_rows, below[:, 0 : 3 * cols], rows + 3, 3, *band_sides, GROUP, cols)
    put_shifted(band_rows, main[...], 3, rows, *band_sides, GROUP, cols)

    top_inside, bottom_inside = lat > 0, lat < lat_count - 1
    hidden_sides = (hidden_side[1].astype(BF16), hidden_side[4].astype(BF16))
    near = jnp.concatenate(
        [above_below(band_rows, 1, 2, cols), above_below(band_rows, rows + 3, 2, cols)], axis=1
    )
    pre = dot(one_main[...], near)
    soft = pre * sigmoid(pre)
    lane = iota((1, 4 * cols), 1)
    inside = ((lane >= 2 * cols) | top_inside) & ((lane < 2 * cols) | bottom_inside)
    soft = jnp.where(inside, soft, 0.0).astype(BF16)
    put_shifted(hidden_rows, soft[:, span(0, 2, cols)], 1, 2, *hidden_sides, feat, cols)
    put_shifted(hidden_rows, soft[:, span(2, 2, cols)], rows + 3, 2, *hidden_sides, feat, cols)
    for row in range(3, rows + 3, step):
        hidden_chunk(one_main, band_rows, hidden_rows, rate, row, step, None, hidden_sides, cols)

    pre = [conv_rows(two_main, hidden_rows, row, 1, cols) for row in (2, rows + 3)]
    label = [side[c * GROUP + bands : c * GROUP + bands + 1, :].astype(jnp.int32) for c in (2, 7)]
    label += [label_rows(band_rows, bands, row, 1, cols) for row in (2, rows + 3)]
    ones = jnp.ones((1, cols), jnp.int32)
    mask = [jnp.where(inside, 1, 0) for inside in insides[1:]]
    mask += [jnp.where(inside, ones, 0) for inside in (top_inside, bottom_inside)]
    slope = head_stage(
        jnp.concatenate([strip_pre] + pre, axis=1),
        jnp.concatenate(label, axis=1),
        jnp.concatenate(mask, axis=1) > 0,
        head_pad[...],
        head_turn[...],
        classes,
    )[2]
    slope_side = (slope[:, 0:128], slope[:, 128:256])
    put_shifted(slope_rows, slope[:, 256 : 256 + cols], 2, 1, *slope_side, feat, cols)
    put_shifted(slope_rows, slope[:, 256 + cols :], rows + 3, 1, *slope_side, feat, cols)

    for row in (1, rows + 3):
        slope_own[:, span(row, 2, cols)] = jnp.zeros((feat, 2 * cols), BF16)
    grad_head = jnp.zeros((feat, GROUP), F32)
    loss_sum = jnp.zeros((1, 1), F32)
    for row in range(3, rows + 3, step):
        pre = conv_rows(two_main, hidden_rows, row, step, cols)
        label = label_rows(band_rows, bands, row, step, cols)
        skip, error, slope, loss = head_stage(pre, label, None, head_pad[...], head_turn[...], classes)
        skip_out[:, span(row - 3, step, cols)] = skip
        slope_own[:, span(row, step, cols)] = slope
        grad_head = grad_head + dot_nt(skip, error)
        put_shifted(slope_rows, slope, row, step, *slope_side, feat, cols)
        loss_sum = loss_sum + jnp.sum(loss, axis=1, keepdims=True)

    def grad_of(product):
        total = None
        for row in range(2, rows + 4, 11):
            count = min(11, rows + 4 - row)
            term = product(below_above(slope_own, row, count, cols), span(row, count, cols))
            total = term if total is None else total + term
        return total

    sums[...] = jnp.zeros_like(sums)
    sums[:, 0 : 3 * feat] = grad_of(lambda slopes, at: dot_nt(slopes, hidden_rows[:, at]))
    for row in range(3, rows + 3, step):
        back = conv_rows(two_back, slope_rows, row, step, cols)
        slope_own[:, span(row, step, cols)] = (back * rate[:, span(row - 3, step, cols)]).astype(BF16)
    sums[:, 3 * feat : 3 * feat + 3 * GROUP] = grad_of(lambda slopes, at: dot_nt(slopes, band_rows[:, at]))
    at = 3 * feat + 3 * GROUP
    sums[0:feat, at : at + GROUP] = grad_head
    sums[feat : feat + 1, at : at + 1] = loss_sum
    half = 3 * feat // 2
    core = lon % 2
    keep_out[...] = sums[pl.ds(pl.multiple_of(core * half, 8), half), :]
    send_out[...] = sums[pl.ds(pl.multiple_of((1 - core) * half, 8), half), :]


def finish_kernel(pixels, me_ref, own, mate, grad_one, grad_two, grad_head, loss, sums):
    half = own.shape[0]
    feat = grad_two.shape[1]
    bands = grad_one.shape[1]
    classes = grad_head.shape[0]
    core = me_ref[0] % 2
    scale = 1.0 / pixels
    sums[pl.ds(pl.multiple_of(core * half, 8), half), :] = own[...] * scale
    sums[pl.ds(pl.multiple_of((1 - core) * half, 8), half), :] = mate[...] * scale
    at = 3 * feat
    turned = jnp.transpose(sums[:, at : at + 3 * GROUP + GROUP])
    for tap in range(9):
        u, v = tap // 3, tap % 3
        grad_two[tap] = sums[u * feat : (u + 1) * feat, v * feat : (v + 1) * feat]
        grad_one[tap] = turned[v * GROUP : v * GROUP + bands, u * feat : (u + 1) * feat]
    grad_head[...] = turned[3 * GROUP : 3 * GROUP + classes, 0:feat]
    loss_row = turned[3 * GROUP : 3 * GROUP + 1]
    loss[...] = loss_row[:, feat : feat + 1] + loss_row[:, feat + GROUP : feat + GROUP + 1]


def tree_sum(values):
    values = list(values)
    while len(values) > 1:
        values = [values[i] + values[i + 1] for i in range(0, len(values), 2)]
    return values[0]


def body(
    patches,
    requests,
    footprint,
    weight_index,
    composite_weights,
    labels,
    conv1_weight,
    conv2_weight,
    head_weight,
):
    lon_count = lax.axis_size("lon")
    lat_count = lax.axis_size("lat")
    chips = lon_count // 2
    rows, slots = footprint.shape
    cols = labels.shape[1]
    store, row_width = patches.shape
    bands = row_width // cols
    bucket = requests.shape[1] // lon_count
    feat = conv2_weight.shape[1]
    classes = head_weight.shape[0]
    vmem = pl.BlockSpec(memory_space=pltpu.VMEM)
    smem = pl.BlockSpec(memory_space=pltpu.SMEM)

    lon = lax.axis_index("lon")
    place = jnp.stack([lax.axis_index("lat"), lon]).astype(jnp.int32)
    me = lon.astype(jnp.int32).reshape(1)

    def by_lon(value, move):
        return lax.ppermute(value, "lon", [(i, i ^ move) for i in range(lon_count)])

    hbm = pl.BlockSpec(memory_space=pltpu.HBM)
    in_hbm = lambda value: pltpu.with_memory_space_constraint(value, pltpu.HBM)
    plan, tile_labels = call(
        functools.partial(plan_kernel, store),
        [struct((lon_count, 16, 128), F32), struct((rows, cols), F32)],
        [
            pltpu.VMEM(requests.shape, jnp.int32),
            pltpu.VMEM((slots, rows), jnp.int32),
            pltpu.VMEM((slots, rows), jnp.int32),
            pltpu.SMEM(composite_weights.shape, F32),
            pltpu.VMEM(labels.shape, jnp.int32),
            pltpu.SemaphoreType.DMA((5,)),
        ],
        vmem_limit=63 * 1024 * 1024,
        in_specs=[hbm] * 5,
    )(requests, footprint.T, weight_index.T, composite_weights, labels)
    plan, patches = lax.optimization_barrier((plan, patches))
    mate_patches = by_lon(patches, 1)
    plans = lax.all_to_all(plan, "lon", split_axis=0, concat_axis=0, tiled=True)
    stored, edge = call(
        functools.partial(store_kernel, bands),
        [struct((2 * store, row_width), BF16), struct((6 * GROUP, 2 * store), BF16)],
        [pltpu.SemaphoreType.DMA],
        in_specs=[smem, hbm, vmem],
        cost_estimate=pl.CostEstimate(flops=10**9, bytes_accessed=10**7, transcendentals=0),
    )(me, in_hbm(patches), mate_patches)
    plans, stored, edge = lax.optimization_barrier((plans, stored, edge))
    moves = list(range(chips - 1, -1, -1))
    cost = pl.CostEstimate(flops=10**9, bytes_accessed=10**7, transcendentals=0)
    row_weights, *smalls = call(
        functools.partial(ends_part_kernel, moves, bands),
        [struct((chips, rows, 2 * store), F32)]
        + [struct((END_LINES + 3 * GROUP, cols), BF16 if move else F32) for move in moves],
        [
            pltpu.VMEM((chips, 2 * store, 2 * rows), F32),
            pltpu.VMEM((chips + 2, 6 * GROUP, 2 * rows), F32),
            pltpu.VMEM((6 * chips, row_width), F32),
            pltpu.VMEM((END_LINES, cols), F32),
        ],
        in_specs=[smem, vmem, vmem, vmem],
        cost_estimate=cost,
    )(me, plans, stored, edge)
    smalls = [by_lon(small, 2 * move) if move else small for move, small in zip(moves, smalls)]
    parts = []
    for some in (moves[:-1], moves[-1:]):
        if len(some) == 1:
            row_weights, *smalls = lax.optimization_barrier((row_weights, *smalls))
        parts += call(
            functools.partial(part_kernel, [moves.index(move) for move in some]),
            [struct((rows, row_width), BF16 if move else F32) for move in some],
            in_specs=[vmem, vmem],
            cost_estimate=cost,
        )(stored, row_weights)
    parts = [by_lon(part, 2 * move) if move else part for move, part in zip(moves, parts)]
    upper, lower = call(
        functools.partial(ends_kernel, bands),
        [struct((GROUP, 3 * cols + 128), BF16)] * 2,
        [pltpu.VMEM((END_LINES + 3 * GROUP, cols), F32), pltpu.VMEM((GROUP, 128), F32)],
        in_specs=[smem] + [vmem] * (2 + chips),
        cost_estimate=pl.CostEstimate(flops=3 * 10**10, bytes_accessed=10**7, transcendentals=0),
    )(me, plans, tile_labels, *smalls)
    main, strips = call(
        functools.partial(composite_kernel, bands),
        [struct((GROUP, rows * cols), BF16), struct((10 * GROUP, 128), BF16)],
        [pltpu.VMEM((GROUP * rows, cols), F32), pltpu.VMEM((10 * GROUP, 128), F32)],
        in_specs=[smem] + [vmem] * (2 + 2 * chips),
        cost_estimate=cost,
    )(me, plans, tile_labels, *parts, *smalls)
    below = lax.ppermute(upper, "lat", [(i + 1, i) for i in range(lat_count - 1)])
    above = lax.ppermute(lower, "lat", [(i, i + 1) for i in range(lat_count - 1)])

    one_main, one_strip, two_main, two_back, head_pad, head_turn = call(
        weights_kernel,
        [
            struct((feat, 9 * GROUP), BF16),
            struct((feat, 9 * GROUP), BF16),
            struct((3 * feat, 3 * feat), BF16),
            struct((3 * feat, 3 * feat), BF16),
            struct((GROUP, feat), BF16),
            struct((feat, GROUP), BF16),
        ],
        [
            pltpu.VMEM((9 * GROUP, feat), F32),
            pltpu.VMEM((128, 128), F32),
            pltpu.VMEM((9, bands, feat), BF16),
            pltpu.VMEM(conv2_weight.shape, BF16),
            pltpu.VMEM(head_weight.shape, BF16),
            pltpu.SemaphoreType.DMA((3,)),
        ],
        in_specs=[hbm] * 3,
    )(*[in_hbm(value) for value in (conv1_weight.transpose(0, 2, 1), conv2_weight, head_weight)])

    ext = rows + 6
    half = 3 * feat // 2
    sum_width = 3 * feat + 4 * GROUP
    skip, keep, send = call(
        functools.partial(network_kernel, bands, classes, rows, cols, lat_count, lon_count, 32),
        [
            struct((feat, rows * cols), BF16),
            struct((half, sum_width), F32),
            struct((half, sum_width), F32),
        ],
        [
            pltpu.VMEM((3 * GROUP, ext * cols), BF16),
            pltpu.VMEM((10 * GROUP, 128), F32),
            pltpu.VMEM((3 * feat, ext * cols), BF16),
            pltpu.VMEM((feat, rows * cols), F32),
            pltpu.VMEM((3 * feat, ext * cols), BF16),
            pltpu.VMEM((feat, ext * cols), BF16),
            pltpu.VMEM((3 * feat, sum_width), F32),
        ],
        in_specs=[smem] + [vmem] * 10,
    )(
        place, main, strips, above, below,
        one_main, one_strip, two_main, two_back, head_pad, head_turn,
    )

    row_id, lane_id = iota((half, sum_width), 0), iota((half, sum_width), 1)
    at_loss = lane_id == 3 * feat + 3 * GROUP
    at_loss, at_rest = at_loss & (row_id == feat), at_loss & (row_id == feat + GROUP)

    def sum_over(value, axis, moves):
        value = jnp.where(at_loss, value + jnp.roll(value, -GROUP, axis=0), value)
        rounded = lax.reduce_precision(value, 8, 7)
        rest = lax.reduce_precision(jnp.roll(value - rounded, GROUP, axis=0), 8, 7)
        rounded = jnp.where(at_rest, rest, rounded)
        sent = rounded.astype(BF16)
        size = lax.axis_size(axis)
        terms = [rounded]
        for move in moves:
            terms.append(lax.ppermute(sent, axis, [(i, i ^ move) for i in range(size)]).astype(F32))
        return tree_sum(terms)

    total = keep + by_lon(send, 1)
    total = sum_over(total, "lon", range(2, lon_count, 2))
    total = sum_over(total, "lat", range(1, lat_count))
    other = by_lon(total, 1)
    pixels = rows * cols * lat_count * lon_count
    grad_one, grad_two, grad_head, loss = call(
        functools.partial(finish_kernel, pixels),
        [
            struct((9, bands, feat), F32),
            struct((9, feat, feat), F32),
            struct((classes, feat), F32),
            struct((1, 1), F32),
        ],
        [pltpu.VMEM((3 * feat, sum_width), F32)],
        in_specs=[smem, vmem, vmem],
    )(me, total, other)
    return skip.reshape(feat, rows, cols), grad_one.transpose(0, 2, 1), grad_two, grad_head, loss.reshape(())


def solution(mesh):
    placed = (
        P(("lat", "lon"), None),
        P("lat", "lon"),
        P("lat", "lon"),
        P("lat", "lon"),
        P(),
        P("lat", "lon"),
        P(),
        P(),
        P(),
    )
    return jax.shard_map(
        body,
        mesh=mesh,
        in_specs=placed,
        out_specs=(P(None, "lat", "lon"), P(), P(), P(), P()),
        check_vma=False,
    )
```

```python
import functools

import jax
import jax.numpy as jnp
from jax import lax
from jax.experimental import pallas as pl
from jax.experimental.pallas import tpu as pltpu
from jax.sharding import PartitionSpec as P

BF16 = jnp.bfloat16
F32 = jnp.float32
GROUP = 16
VMEM_LIMIT = 28 * 1024 * 1024


def dot(left, right):
    return lax.dot_general(left, right, (((1,), (0,)), ((), ())), preferred_element_type=F32)


def dot_nt(left, right):
    return lax.dot_general(left, right, (((1,), (1,)), ((), ())), preferred_element_type=F32)


def iota(shape, dim):
    return lax.broadcasted_iota(jnp.int32, shape, dim)


def call(kernel, out_shape, scratch=(), vmem_limit=VMEM_LIMIT, **kwargs):
    return pl.pallas_call(
        kernel,
        out_shape=out_shape,
        scratch_shapes=list(scratch),
        compiler_params=pltpu.CompilerParams(vmem_limit_bytes=vmem_limit),
        **kwargs,
    )


def struct(shape, dtype):
    return jax.ShapeDtypeStruct(shape, dtype)


def plan_kernel(
    store, requests_hbm, footprint_hbm, weight_index_hbm, levels_hbm, labels_hbm, out, labels_out,
    requests, footprint, weight_index, levels, labels, sems,
):
    copies = [
        pltpu.make_async_copy(source, target, sems.at[i])
        for i, (source, target) in enumerate(
            (
                (footprint_hbm, footprint),
                (requests_hbm, requests),
                (weight_index_hbm, weight_index),
                (levels_hbm, levels),
                (labels_hbm, labels),
            )
        )
    ]
    for copy in copies:
        copy.start()
    for copy in copies:
        copy.wait()
    slots, rows = footprint.shape
    patch_cols = labels.shape[1]
    count = out.shape[0]
    bucket = requests.shape[1] // count
    foot = footprint[...]
    level_of = weight_index[...]
    weight = jnp.zeros((slots, rows), F32)
    for level in range(levels.shape[0]):
        weight = jnp.where(level_of == level, levels[level], weight)
    weight = jnp.where(foot >= 0, weight, 0.0)
    weight = weight / jnp.sum(weight, axis=0, keepdims=True)
    flat = jnp.concatenate([foot[slot : slot + 1] for slot in range(slots)], axis=1)
    owner = jnp.right_shift(flat, bucket.bit_length() - 1)
    place = jnp.bitwise_and(flat, bucket - 1)
    at_place = jnp.where(iota((bucket, slots * rows), 0) == place, 1.0, 0.0).astype(BF16)
    asked = requests[...].astype(F32)
    asked = jnp.concatenate([asked[:, i * bucket : (i + 1) * bucket] for i in range(count)], axis=0)
    offset = dot(asked.astype(BF16), at_place)
    offset = jnp.sum(jnp.where(iota(offset.shape, 0) == owner, offset, 0.0), axis=0, keepdims=True)
    entry = offset + (owner * store).astype(F32)
    entry = jnp.concatenate([entry[:, slot * rows : (slot + 1) * rows] for slot in range(slots)], axis=0)
    lane = iota((8, patch_cols), 1)
    side = iota((8, patch_cols), 0)
    pick = ((side == 0) & (lane == 0)) | ((side == 1) & (lane == patch_cols - 1))
    label = labels[...].astype(F32)
    labels_out[...] = label
    edges = dot_nt(jnp.where(pick, 1.0, 0.0).astype(BF16), label.astype(BF16))
    entries = jnp.concatenate([entry, edges], axis=1)
    weights = jnp.concatenate([weight, jnp.zeros_like(weight)], axis=1)
    for target in range(count):
        out[target, 0:slots, :] = entries
        out[target, slots : 2 * slots, :] = weights


def store_kernel(bands, me_ref, own, mate, stored, edge, sem):
    store, row_width = own.shape
    patch_cols = row_width // bands
    core = me_ref[0] % 2
    copy = pltpu.make_async_copy(own, stored.at[pl.ds(pl.multiple_of(core * store, 64), store)], sem)
    copy.start()
    stored[pl.ds(pl.multiple_of((1 - core) * store, 64), store), :] = mate[...]
    copy.wait()
    row_id = iota((6 * GROUP, patch_cols), 0)
    lane_id = iota((6 * GROUP, patch_cols), 1)
    column = row_id // GROUP
    column_lane = jnp.where(column < 3, column + (patch_cols - 3), column - 3)
    at_column = lane_id == column_lane
    total = jnp.zeros(edge.shape, F32)
    for band in range(bands):
        pick = jnp.where(at_column & (row_id % GROUP == band), 1.0, 0.0).astype(BF16)
        total = total + dot_nt(pick, stored[:, band * patch_cols : (band + 1) * patch_cols])
    edge[...] = total.astype(BF16)


def put_weights(plans, chip, first, target):
    held, lanes = target.shape
    rows = lanes // 2
    slots = plans.shape[1] // 2
    both = jnp.concatenate([plans[2 * chip, :, 0:rows], plans[2 * chip + 1, :, 0:rows]], axis=1)
    entries, weights = both[0:slots] - first, both[slots:]
    for start in range(0, held, 64):
        stored_row = (iota((64, lanes), 0) + start).astype(F32)
        total = jnp.zeros((64, lanes), F32)
        for slot in range(slots):
            total = total + jnp.where(entries[slot : slot + 1] == stored_row, weights[slot : slot + 1], 0.0)
        target[start : start + 64, :] = total


def high_low(value):
    high = value.astype(BF16)
    return high, (value - high.astype(F32)).astype(BF16)


ENDS = 8


def ends_part_kernel(moves, bands, me_ref, plans, stored, edge, row_weights, *refs):
    smalls, (over, sides, product, lines) = refs[:-4], refs[-4:]
    chips = plans.shape[0] // 2
    _, rows, held = row_weights.shape
    cols = stored.shape[1] // bands
    me = me_ref[0]
    here, core = me // 2, me % 2
    first = (here * held).astype(F32)
    sides[0] = jnp.zeros(sides.shape[1:], F32)
    sides[chips + 1] = jnp.zeros(sides.shape[1:], F32)
    for chip in range(chips):
        put_weights(plans, chip, first, over.at[chip])
        high, low = high_low(over[chip])
        sides[chip + 1] = dot(edge[...], high) + dot(edge[...], low)
    ends = []
    for i, move in enumerate(moves):
        both = jnp.transpose(over[jnp.bitwise_xor(here, move)])
        weights = jnp.where(core == 0, both[0:rows], both[rows:])
        row_weights[i] = weights
        ends += [weights[0:ENDS], weights[rows - ENDS : rows]]
    high, low = high_low(jnp.concatenate(ends, axis=0))
    count = high.shape[0]
    both = dot(jnp.concatenate([high, low], axis=0), stored[...])
    product[...] = both[0:count] + both[count:]
    for i, (move, small) in enumerate(zip(moves, smalls, strict=True)):
        pair = slice(2 * ENDS * i, 2 * ENDS * (i + 1))
        for band in range(bands):
            lines[2 * ENDS * band : 2 * ENDS * (band + 1), :] = product[pair, band * cols : (band + 1) * cols]
        small[0 : lines.shape[0], :] = lines[...].astype(small.dtype)
        chip = jnp.bitwise_xor(here, move)
        near, before, after = sides[chip + 1], sides[chip], sides[chip + 2]
        left = jnp.where(core == 1, near[0 : 3 * GROUP, 0:rows], before[0 : 3 * GROUP, rows:])
        right = jnp.where(core == 0, near[3 * GROUP :, rows:], after[3 * GROUP :, 0:rows])
        small[lines.shape[0] :, :] = jnp.concatenate([left, right], axis=1).astype(small.dtype)


def part_kernel(indices, stored, row_weights, *outs):
    rows = outs[0].shape[0]
    row_width = stored.shape[1]
    for index, out in zip(indices, outs, strict=True):
        high, low = high_low(row_weights[index][ENDS : ENDS + rows])
        both = jnp.concatenate([high, low], axis=0)
        for start in range(0, row_width, 512):
            stop = min(start + 512, row_width)
            product = dot(both, stored[:, start:stop])
            out[:, start:stop] = (product[:rows] + product[rows:]).astype(out.dtype)


def ends_kernel(bands, me_ref, plans, labels, *refs):
    count = plans.shape[0]
    rows, cols = labels.shape
    smalls, (upper, lower, total, bundle) = refs[:-4], refs[-4:]
    me = me_ref[0]
    value = smalls[0][...].astype(F32)
    for small in smalls[1:]:
        value = value + small[...].astype(F32)
    total[...] = value
    before = plans[jnp.maximum(me - 1, 0), 1:2, rows : 2 * rows]
    after = plans[jnp.minimum(me + 1, count - 1), 0:1, rows : 2 * rows]
    lines = 2 * ENDS * bands
    for target, start, end in ((upper, 0, 0), (lower, rows - 3, 2 * ENDS - 3)):
        bundle[...] = jnp.zeros_like(bundle)
        for i in range(3):
            line = jnp.concatenate(
                [
                    total[pl.ds(end + i, bands, stride=2 * ENDS), :],
                    labels[start + i : start + i + 1, :],
                    jnp.zeros((GROUP - bands - 1, cols), F32),
                ],
                axis=0,
            )
            target[:, i * cols : (i + 1) * cols] = line.astype(BF16)
            for column, at in ((3, 0), (4, 1), (5, cols - 2), (6, cols - 1)):
                bundle[:, column * 3 + i : column * 3 + i + 1] = line[:, at : at + 1]
        for column in range(3):
            group = total[lines + column * GROUP : lines + (column + 1) * GROUP, :]
            bundle[:, column * 3 : column * 3 + 3] = group[:, start : start + 3]
            at = (column + 7) * 3
            bundle[:, at : at + 3] = group[:, rows + start : rows + start + 3]
        bundle[bands : bands + 1, 6:9] = before[:, start : start + 3]
        bundle[bands : bands + 1, 21:24] = after[:, start : start + 3]
        target[:, 3 * cols :] = bundle[...].astype(BF16)


def composite_kernel(bands, me_ref, plans, labels, *refs):
    count = plans.shape[0]
    tile_rows, patch_cols = labels.shape
    inputs, (main, strips, bank, side) = refs[:-4], refs[-4:]
    parts, smalls = inputs[: len(inputs) // 2], inputs[len(inputs) // 2 :]
    me = me_ref[0]
    small_sum = smalls[0][...].astype(F32)
    for small in smalls[1:]:
        small_sum = small_sum + small[...].astype(F32)
    for band in range(bands):
        columns = slice(band * patch_cols, (band + 1) * patch_cols)
        total = parts[0][:, columns].astype(F32)
        for part in parts[1:]:
            total = total + part[:, columns].astype(F32)
        ends = small_sum[2 * ENDS * band : 2 * ENDS * (band + 1)]
        total = jnp.concatenate([ends[0:ENDS], total, ends[ENDS:]], axis=0)
        bank[band * tile_rows : (band + 1) * tile_rows, :] = total
    bank[bands * tile_rows : (bands + 1) * tile_rows, :] = labels[...]
    bank[(bands + 1) * tile_rows : GROUP * tile_rows, :] = jnp.zeros(
        ((GROUP - bands - 1) * tile_rows, patch_cols), F32
    )
    for row in range(tile_rows):
        main[:, row * patch_cols : (row + 1) * patch_cols] = bank[
            pl.ds(row, GROUP, stride=tile_rows), :
        ].astype(BF16)

    far = small_sum[2 * ENDS * bands :]
    side[...] = jnp.zeros_like(side)
    side[0 : 3 * GROUP, 3 : 3 + tile_rows] = far[:, :tile_rows]
    side[7 * GROUP : 10 * GROUP, 3 : 3 + tile_rows] = far[:, tile_rows:]
    before = plans[jnp.maximum(me - 1, 0), 1:2, tile_rows : 2 * tile_rows]
    after = plans[jnp.minimum(me + 1, count - 1), 0:1, tile_rows : 2 * tile_rows]
    side[2 * GROUP + bands : 2 * GROUP + bands + 1, 3 : 3 + tile_rows] = before
    side[7 * GROUP + bands : 7 * GROUP + bands + 1, 3 : 3 + tile_rows] = after
    row_id = iota((4 * GROUP, patch_cols), 0)
    lane_id = iota((4 * GROUP, patch_cols), 1)
    near = jnp.zeros((4 * GROUP, tile_rows), F32)
    column = row_id // GROUP
    column_lane = jnp.where(column < 2, column, column + (patch_cols - 4))
    for band in range(bands):
        pick = (row_id % GROUP == band) & (lane_id == column_lane)
        tile = bank[band * tile_rows : (band + 1) * tile_rows, :].astype(BF16)
        near = near + dot_nt(jnp.where(pick, 1.0, 0.0).astype(BF16), tile)
    side[3 * GROUP : 7 * GROUP, 3 : 3 + tile_rows] = near
    strips[...] = side[...].astype(BF16)


def weights_kernel(
    conv1_hbm, conv2_hbm, head_hbm, one_main, one_strip, two_main, two_back, head_pad, head_turn,
    wide, tall, conv1, conv2, head, sems,
):
    copies = [
        pltpu.make_async_copy(source, target, sems.at[i])
        for i, (source, target) in enumerate(((conv1_hbm, conv1), (conv2_hbm, conv2), (head_hbm, head)))
    ]
    for copy in copies:
        copy.start()
    for copy in copies:
        copy.wait()
    bands = conv1.shape[1]
    feat = conv2.shape[1]
    classes = head.shape[0]
    wide[...] = jnp.zeros_like(wide)
    for tap in range(9):
        wide[tap * GROUP : tap * GROUP + bands, :] = conv1[tap].astype(F32)
    one_main[...] = jnp.transpose(wide[...]).astype(BF16)
    for tap in range(9):
        wide[tap * GROUP : tap * GROUP + bands, :] = conv1[(tap % 3) * 3 + tap // 3].astype(F32)
    one_strip[...] = jnp.transpose(wide[...]).astype(BF16)
    for row in range(3):
        at = slice(row * feat, (row + 1) * feat)
        two_main[at, :] = jnp.concatenate([conv2[row * 3 + col] for col in range(3)], axis=1)
        turned = jnp.concatenate([conv2[8 - (row * 3 + col)].astype(F32) for col in range(3)], axis=0)
        two_back[at, :] = jnp.transpose(turned).astype(BF16)
    tall[...] = jnp.zeros_like(tall)
    tall[0:classes, 0:feat] = head[...].astype(F32)
    padded = tall[...]
    head_pad[...] = padded[0:GROUP, 0:feat].astype(BF16)
    head_turn[...] = jnp.transpose(padded)[0:feat, 0:GROUP].astype(BF16)


def sigmoid(value):
    return 0.5 * jnp.tanh(0.5 * value) + 0.5


def head_stage(pre, label, mask, head_pad, head_turn, classes):
    gate = sigmoid(pre)
    soft = pre * gate
    skip = soft.astype(BF16)
    logits = dot(head_pad, skip)
    rank = iota(logits.shape, 0)
    real = rank < classes
    total = jnp.sum(jnp.where(real, jnp.exp(logits), 0.0), axis=0, keepdims=True)
    log_total = jnp.log(total)
    chosen = rank == label
    error = jnp.where(real, jnp.exp(logits - log_total) - jnp.where(chosen, 1.0, 0.0), 0.0)
    error = error.astype(BF16)
    loss = log_total - jnp.sum(jnp.where(chosen, logits, 0.0), axis=0, keepdims=True)
    back = dot(head_turn, error)
    slope = back * (gate + soft * (1.0 - gate))
    if mask is not None:
        slope = jnp.where(mask, slope, 0.0)
    return skip, error, slope.astype(BF16), loss


def span(row, count, cols):
    return slice(row * cols, (row + count) * cols)


def put_shifted(target, value, row, count, left_side, right_side, size, cols):
    lane = iota((1, cols), 1)
    target[size : 2 * size, span(row, count, cols)] = value
    for i in range(count):
        tile = value[:, i * cols : (i + 1) * cols]
        turn = (128 - (row + i)) % 128
        left = pltpu.roll(left_side, turn, 1)
        right = pltpu.roll(right_side, (turn + cols - 1) % 128, 1)
        target[0:size, span(row + i, 1, cols)] = jnp.where(lane == 0, left, pltpu.roll(tile, 1, 1))
        target[2 * size : 3 * size, span(row + i, 1, cols)] = jnp.where(
            lane == cols - 1, right, pltpu.roll(tile, cols - 1, 1)
        )


def above_below(ref, row, count, cols):
    return jnp.concatenate([ref[:, span(row + u, count, cols)] for u in (-1, 0, 1)], axis=0)


def below_above(ref, row, count, cols):
    return jnp.concatenate([ref[:, span(row - u, count, cols)] for u in (-1, 0, 1)], axis=0)


def conv_rows(weight, ref, row, count, cols):
    feat = weight.shape[0] // 3
    near = dot(weight[...], ref[:, span(row - 1, count + 2, cols)])
    return (
        near[0:feat, span(0, count, cols)]
        + near[feat : 2 * feat, span(1, count, cols)]
        + near[2 * feat :, span(2, count, cols)]
    )


def turned_rows(value):
    return jnp.concatenate(
        [pltpu.roll(value, 1, 1), value, pltpu.roll(value, value.shape[1] - 1, 1)], axis=0
    ).astype(BF16)


def strip_inside(place, rows, lat_count, lon_count):
    lat, lon = place[0], place[1]
    lane_row = iota((1, 128), 1) - 3
    inside = (lat * rows + lane_row >= 0) & (lat * rows + lane_row < lat_count * rows)
    inside = inside & (lane_row < rows + 3)
    return inside, inside & (lon > 0), inside & (lon < lon_count - 1)


def strip_hidden(side, one_strip, insides, firsts):
    inside, left_inside, right_inside = insides
    taps = {}
    for first in firsts:
        for column in range(first, first + 3):
            if column not in taps:
                taps[column] = turned_rows(side[column * GROUP : (column + 1) * GROUP, :])
    near = jnp.concatenate(
        [jnp.concatenate([taps[first + i] for first in firsts], axis=1) for i in range(3)], axis=0
    )
    pre = dot(one_strip[...], near)
    soft = pre * sigmoid(pre)
    hidden = []
    for i, first in enumerate(firsts):
        mask = left_inside if first in (0, 1) else right_inside if first in (6, 7) else inside
        hidden.append(jnp.where(mask, soft[:, i * 128 : (i + 1) * 128], 0.0))
    return hidden


def hidden_chunk(one_main, band_rows, hidden_rows, rate, row, count, mask, sides, cols):
    pre = dot(one_main[...], above_below(band_rows, row, count, cols))
    gate = sigmoid(pre)
    soft = pre * gate
    if rate is not None:
        rate[:, span(row - 3, count, cols)] = gate + soft * (1.0 - gate)
    if mask is not None:
        soft = jnp.where(mask, soft, 0.0)
    put_shifted(hidden_rows, soft.astype(BF16), row, count, *sides, pre.shape[0], cols)


def label_rows(band_rows, bands, row, count, cols):
    return band_rows[GROUP + bands : GROUP + bands + 1, span(row, count, cols)].astype(F32).astype(jnp.int32)


def network_kernel(
    bands, classes, rows, cols, lat_count, lon_count, step,
    place, main, strips, above, below,
    one_main, one_strip, two_main, two_back, head_pad, head_turn,
    skip_out, keep_out, send_out,
    band_rows, side, hidden_rows, rate, slope_rows, slope_own, sums,
):
    feat = head_turn.shape[0]
    lat, lon = place[0], place[1]

    side[...] = strips[...].astype(F32)
    up_tail = above[:, 3 * cols :].astype(F32)
    down_tail = below[:, 3 * cols :].astype(F32)
    for column in range(10):
        at = slice(column * GROUP, (column + 1) * GROUP)
        side[at, 0:3] = up_tail[:, column * 3 : column * 3 + 3]
        side[at, 3 + rows : 6 + rows] = down_tail[:, column * 3 : column * 3 + 3]

    insides = strip_inside(place, rows, lat_count, lon_count)
    hidden_side = strip_hidden(side, one_strip, insides, (0, 1, 2, 5, 6, 7))
    hidden_taps = [turned_rows(value) for value in hidden_side]
    strip_pre = None
    for col in range(3):
        weight = jnp.concatenate(
            [two_main[u * feat : (u + 1) * feat, col * feat : (col + 1) * feat] for u in range(3)], axis=1
        )
        term = dot(weight, jnp.concatenate([hidden_taps[col], hidden_taps[3 + col]], axis=1))
        strip_pre = term if strip_pre is None else strip_pre + term

    band_sides = (
        side[2 * GROUP : 3 * GROUP, :].astype(BF16),
        side[7 * GROUP : 8 * GROUP, :].astype(BF16),
    )
    put_shifted(band_rows, above[:, 0 : 3 * cols], 0, 3, *band_sides, GROUP, cols)
    put_shifted(band_rows, below[:, 0 : 3 * cols], rows + 3, 3, *band_sides, GROUP, cols)
    put_shifted(band_rows, main[...], 3, rows, *band_sides, GROUP, cols)

    top_inside, bottom_inside = lat > 0, lat < lat_count - 1
    hidden_sides = (hidden_side[1].astype(BF16), hidden_side[4].astype(BF16))
    near = jnp.concatenate(
        [above_below(band_rows, 1, 2, cols), above_below(band_rows, rows + 3, 2, cols)], axis=1
    )
    pre = dot(one_main[...], near)
    soft = pre * sigmoid(pre)
    lane = iota((1, 4 * cols), 1)
    inside = ((lane >= 2 * cols) | top_inside) & ((lane < 2 * cols) | bottom_inside)
    soft = jnp.where(inside, soft, 0.0).astype(BF16)
    put_shifted(hidden_rows, soft[:, span(0, 2, cols)], 1, 2, *hidden_sides, feat, cols)
    put_shifted(hidden_rows, soft[:, span(2, 2, cols)], rows + 3, 2, *hidden_sides, feat, cols)
    for row in range(3, rows + 3, step):
        hidden_chunk(one_main, band_rows, hidden_rows, rate, row, step, None, hidden_sides, cols)

    pre = [conv_rows(two_main, hidden_rows, row, 1, cols) for row in (2, rows + 3)]
    label = [side[c * GROUP + bands : c * GROUP + bands + 1, :].astype(jnp.int32) for c in (2, 7)]
    label += [label_rows(band_rows, bands, row, 1, cols) for row in (2, rows + 3)]
    ones = jnp.ones((1, cols), jnp.int32)
    mask = [jnp.where(inside, 1, 0) for inside in insides[1:]]
    mask += [jnp.where(inside, ones, 0) for inside in (top_inside, bottom_inside)]
    slope = head_stage(
        jnp.concatenate([strip_pre] + pre, axis=1),
        jnp.concatenate(label, axis=1),
        jnp.concatenate(mask, axis=1) > 0,
        head_pad[...],
        head_turn[...],
        classes,
    )[2]
    slope_side = (slope[:, 0:128], slope[:, 128:256])
    put_shifted(slope_rows, slope[:, 256 : 256 + cols], 2, 1, *slope_side, feat, cols)
    put_shifted(slope_rows, slope[:, 256 + cols :], rows + 3, 1, *slope_side, feat, cols)

    for row in (1, rows + 3):
        slope_own[:, span(row, 2, cols)] = jnp.zeros((feat, 2 * cols), BF16)
    grad_head = jnp.zeros((feat, GROUP), F32)
    loss_sum = jnp.zeros((1, 1), F32)
    for row in range(3, rows + 3, step):
        pre = conv_rows(two_main, hidden_rows, row, step, cols)
        label = label_rows(band_rows, bands, row, step, cols)
        skip, error, slope, loss = head_stage(pre, label, None, head_pad[...], head_turn[...], classes)
        skip_out[:, span(row - 3, step, cols)] = skip
        slope_own[:, span(row, step, cols)] = slope
        grad_head = grad_head + dot_nt(skip, error)
        put_shifted(slope_rows, slope, row, step, *slope_side, feat, cols)
        loss_sum = loss_sum + jnp.sum(loss, axis=1, keepdims=True)

    def grad_of(product):
        total = None
        for row in range(2, rows + 4, 11):
            count = min(11, rows + 4 - row)
            term = product(below_above(slope_own, row, count, cols), span(row, count, cols))
            total = term if total is None else total + term
        return total

    sums[...] = jnp.zeros_like(sums)
    sums[:, 0 : 3 * feat] = grad_of(lambda slopes, at: dot_nt(slopes, hidden_rows[:, at]))
    for row in range(3, rows + 3, step):
        back = conv_rows(two_back, slope_rows, row, step, cols)
        slope_own[:, span(row, step, cols)] = (back * rate[:, span(row - 3, step, cols)]).astype(BF16)
    sums[:, 3 * feat : 3 * feat + 3 * GROUP] = grad_of(lambda slopes, at: dot_nt(slopes, band_rows[:, at]))
    at = 3 * feat + 3 * GROUP
    sums[0:feat, at : at + GROUP] = grad_head
    sums[feat : feat + 1, at : at + 1] = loss_sum
    half = 3 * feat // 2
    core = lon % 2
    keep_out[...] = sums[pl.ds(pl.multiple_of(core * half, 8), half), :]
    send_out[...] = sums[pl.ds(pl.multiple_of((1 - core) * half, 8), half), :]


def finish_kernel(pixels, me_ref, own, mate, grad_one, grad_two, grad_head, loss, sums):
    half = own.shape[0]
    feat = grad_two.shape[1]
    bands = grad_one.shape[1]
    classes = grad_head.shape[0]
    core = me_ref[0] % 2
    scale = 1.0 / pixels
    sums[pl.ds(pl.multiple_of(core * half, 8), half), :] = own[...] * scale
    sums[pl.ds(pl.multiple_of((1 - core) * half, 8), half), :] = mate[...] * scale
    at = 3 * feat
    turned = jnp.transpose(sums[:, at : at + 3 * GROUP + GROUP])
    for tap in range(9):
        u, v = tap // 3, tap % 3
        grad_two[tap] = sums[u * feat : (u + 1) * feat, v * feat : (v + 1) * feat]
        grad_one[tap] = turned[v * GROUP : v * GROUP + bands, u * feat : (u + 1) * feat]
    grad_head[...] = turned[3 * GROUP : 3 * GROUP + classes, 0:feat]
    loss_row = turned[3 * GROUP : 3 * GROUP + 1]
    loss[...] = loss_row[:, feat : feat + 1] + loss_row[:, feat + GROUP : feat + GROUP + 1]


def tree_sum(values):
    values = list(values)
    while len(values) > 1:
        values = [values[i] + values[i + 1] for i in range(0, len(values), 2)]
    return values[0]


def body(
    patches,
    requests,
    footprint,
    weight_index,
    composite_weights,
    labels,
    conv1_weight,
    conv2_weight,
    head_weight,
):
    lon_count = lax.axis_size("lon")
    lat_count = lax.axis_size("lat")
    chips = lon_count // 2
    rows, slots = footprint.shape
    cols = labels.shape[1]
    store, row_width = patches.shape
    bands = row_width // cols
    bucket = requests.shape[1] // lon_count
    feat = conv2_weight.shape[1]
    classes = head_weight.shape[0]
    vmem = pl.BlockSpec(memory_space=pltpu.VMEM)
    smem = pl.BlockSpec(memory_space=pltpu.SMEM)

    lon = lax.axis_index("lon")
    place = jnp.stack([lax.axis_index("lat"), lon]).astype(jnp.int32)
    me = lon.astype(jnp.int32).reshape(1)

    def by_lon(value, move):
        return lax.ppermute(value, "lon", [(i, i ^ move) for i in range(lon_count)])

    hbm = pl.BlockSpec(memory_space=pltpu.HBM)
    in_hbm = lambda value: pltpu.with_memory_space_constraint(value, pltpu.HBM)
    plan, tile_labels = call(
        functools.partial(plan_kernel, store),
        [struct((lon_count, 16, 128), F32), struct((rows, cols), F32)],
        [
            pltpu.VMEM(requests.shape, jnp.int32),
            pltpu.VMEM((slots, rows), jnp.int32),
            pltpu.VMEM((slots, rows), jnp.int32),
            pltpu.SMEM(composite_weights.shape, F32),
            pltpu.VMEM(labels.shape, jnp.int32),
            pltpu.SemaphoreType.DMA((5,)),
        ],
        vmem_limit=63 * 1024 * 1024,
        in_specs=[hbm] * 5,
    )(requests, footprint.T, weight_index.T, composite_weights, labels)
    plan, patches = lax.optimization_barrier((plan, patches))
    mate_patches = by_lon(patches, 1)
    plans = lax.all_to_all(plan, "lon", split_axis=0, concat_axis=0, tiled=True)
    stored, edge = call(
        functools.partial(store_kernel, bands),
        [struct((2 * store, row_width), BF16), struct((6 * GROUP, 2 * store), BF16)],
        [pltpu.SemaphoreType.DMA],
        in_specs=[smem, hbm, vmem],
        cost_estimate=pl.CostEstimate(flops=10**9, bytes_accessed=10**7, transcendentals=0),
    )(me, in_hbm(patches), mate_patches)
    plans, stored, edge = lax.optimization_barrier((plans, stored, edge))
    moves = list(range(chips - 1, -1, -1))
    small_lines = 2 * ENDS * bands + 3 * GROUP
    cost = pl.CostEstimate(flops=10**9, bytes_accessed=10**7, transcendentals=0)
    row_weights, *smalls = call(
        functools.partial(ends_part_kernel, moves, bands),
        [struct((chips, rows, 2 * store), F32)]
        + [struct((small_lines, cols), BF16 if move else F32) for move in moves],
        [
            pltpu.VMEM((chips, 2 * store, 2 * rows), F32),
            pltpu.VMEM((chips + 2, 6 * GROUP, 2 * rows), F32),
            pltpu.VMEM((2 * ENDS * chips, row_width), F32),
            pltpu.VMEM((2 * ENDS * bands, cols), F32),
        ],
        in_specs=[smem, vmem, vmem, vmem],
        cost_estimate=cost,
    )(me, plans, stored, edge)
    smalls = [by_lon(small, 2 * move) if move else small for move, small in zip(moves, smalls)]
    parts = []
    for some in (moves[:-1], moves[-1:]):
        if len(some) == 1:
            row_weights, *smalls = lax.optimization_barrier((row_weights, *smalls))
        parts += call(
            functools.partial(part_kernel, [moves.index(move) for move in some]),
            [struct((rows - 2 * ENDS, row_width), BF16 if move else F32) for move in some],
            in_specs=[vmem, vmem],
            cost_estimate=cost,
        )(stored, row_weights)
    parts = [by_lon(part, 2 * move) if move else part for move, part in zip(moves, parts)]
    upper, lower = call(
        functools.partial(ends_kernel, bands),
        [struct((GROUP, 3 * cols + 128), BF16)] * 2,
        [pltpu.VMEM((small_lines, cols), F32), pltpu.VMEM((GROUP, 128), F32)],
        in_specs=[smem] + [vmem] * (2 + chips),
        cost_estimate=pl.CostEstimate(flops=3 * 10**10, bytes_accessed=10**7, transcendentals=0),
    )(me, plans, tile_labels, *smalls)
    main, strips = call(
        functools.partial(composite_kernel, bands),
        [struct((GROUP, rows * cols), BF16), struct((10 * GROUP, 128), BF16)],
        [pltpu.VMEM((GROUP * rows, cols), F32), pltpu.VMEM((10 * GROUP, 128), F32)],
        in_specs=[smem] + [vmem] * (2 + 2 * chips),
        cost_estimate=cost,
    )(me, plans, tile_labels, *parts, *smalls)
    below = lax.ppermute(upper, "lat", [(i + 1, i) for i in range(lat_count - 1)])
    above = lax.ppermute(lower, "lat", [(i, i + 1) for i in range(lat_count - 1)])

    one_main, one_strip, two_main, two_back, head_pad, head_turn = call(
        weights_kernel,
        [
            struct((feat, 9 * GROUP), BF16),
            struct((feat, 9 * GROUP), BF16),
            struct((3 * feat, 3 * feat), BF16),
            struct((3 * feat, 3 * feat), BF16),
            struct((GROUP, feat), BF16),
            struct((feat, GROUP), BF16),
        ],
        [
            pltpu.VMEM((9 * GROUP, feat), F32),
            pltpu.VMEM((128, 128), F32),
            pltpu.VMEM((9, bands, feat), BF16),
            pltpu.VMEM(conv2_weight.shape, BF16),
            pltpu.VMEM(head_weight.shape, BF16),
            pltpu.SemaphoreType.DMA((3,)),
        ],
        in_specs=[hbm] * 3,
    )(*[in_hbm(value) for value in (conv1_weight.transpose(0, 2, 1), conv2_weight, head_weight)])

    ext = rows + 6
    half = 3 * feat // 2
    sum_width = 3 * feat + 4 * GROUP
    skip, keep, send = call(
        functools.partial(network_kernel, bands, classes, rows, cols, lat_count, lon_count, 32),
        [
            struct((feat, rows * cols), BF16),
            struct((half, sum_width), F32),
            struct((half, sum_width), F32),
        ],
        [
            pltpu.VMEM((3 * GROUP, ext * cols), BF16),
            pltpu.VMEM((10 * GROUP, 128), F32),
            pltpu.VMEM((3 * feat, ext * cols), BF16),
            pltpu.VMEM((feat, rows * cols), F32),
            pltpu.VMEM((3 * feat, ext * cols), BF16),
            pltpu.VMEM((feat, ext * cols), BF16),
            pltpu.VMEM((3 * feat, sum_width), F32),
        ],
        in_specs=[smem] + [vmem] * 10,
    )(
        place, main, strips, above, below,
        one_main, one_strip, two_main, two_back, head_pad, head_turn,
    )

    row_id, lane_id = iota((half, sum_width), 0), iota((half, sum_width), 1)
    at_loss = lane_id == 3 * feat + 3 * GROUP
    at_loss, at_rest = at_loss & (row_id == feat), at_loss & (row_id == feat + GROUP)

    def sum_over(value, axis, moves):
        value = jnp.where(at_loss, value + jnp.roll(value, -GROUP, axis=0), value)
        rounded = lax.reduce_precision(value, 8, 7)
        rest = lax.reduce_precision(jnp.roll(value - rounded, GROUP, axis=0), 8, 7)
        rounded = jnp.where(at_rest, rest, rounded)
        sent = rounded.astype(BF16)
        size = lax.axis_size(axis)
        terms = [rounded]
        for move in moves:
            terms.append(lax.ppermute(sent, axis, [(i, i ^ move) for i in range(size)]).astype(F32))
        return tree_sum(terms)

    total = keep + by_lon(send, 1)
    total = sum_over(total, "lon", range(2, lon_count, 2))
    total = sum_over(total, "lat", range(1, lat_count))
    other = by_lon(total, 1)
    pixels = rows * cols * lat_count * lon_count
    grad_one, grad_two, grad_head, loss = call(
        functools.partial(finish_kernel, pixels),
        [
            struct((9, bands, feat), F32),
            struct((9, feat, feat), F32),
            struct((classes, feat), F32),
            struct((1, 1), F32),
        ],
        [pltpu.VMEM((3 * feat, sum_width), F32)],
        in_specs=[smem, vmem, vmem],
    )(me, total, other)
    return skip.reshape(feat, rows, cols), grad_one.transpose(0, 2, 1), grad_two, grad_head, loss.reshape(())


def solution(mesh):
    placed = (
        P(("lat", "lon"), None),
        P("lat", "lon"),
        P("lat", "lon"),
        P("lat", "lon"),
        P(),
        P("lat", "lon"),
        P(),
        P(),
        P(),
    )
    return jax.shard_map(
        body,
        mesh=mesh,
        in_specs=placed,
        out_specs=(P(None, "lat", "lon"), P(), P(), P(), P()),
        check_vma=False,
    )
```

```python
import functools

import jax
import jax.numpy as jnp
from jax import lax
from jax.experimental import pallas as pl
from jax.experimental.pallas import tpu as pltpu
from jax.sharding import PartitionSpec as P

BF16 = jnp.bfloat16
F32 = jnp.float32
GROUP = 16
VMEM_LIMIT = 28 * 1024 * 1024


def dot(left, right):
    return lax.dot_general(left, right, (((1,), (0,)), ((), ())), preferred_element_type=F32)


def dot_nt(left, right):
    return lax.dot_general(left, right, (((1,), (1,)), ((), ())), preferred_element_type=F32)


def iota(shape, dim):
    return lax.broadcasted_iota(jnp.int32, shape, dim)


def call(kernel, out_shape, scratch=(), vmem_limit=VMEM_LIMIT, **kwargs):
    return pl.pallas_call(
        kernel,
        out_shape=out_shape,
        scratch_shapes=list(scratch),
        compiler_params=pltpu.CompilerParams(vmem_limit_bytes=vmem_limit),
        **kwargs,
    )


def struct(shape, dtype):
    return jax.ShapeDtypeStruct(shape, dtype)


def plan_kernel(
    store, requests_hbm, footprint_hbm, weight_index_hbm, levels_hbm, labels_hbm, out, labels_out,
    requests, footprint, weight_index, levels, labels, sems,
):
    copies = [
        pltpu.make_async_copy(source, target, sems.at[i])
        for i, (source, target) in enumerate(
            (
                (footprint_hbm, footprint),
                (requests_hbm, requests),
                (weight_index_hbm, weight_index),
                (levels_hbm, levels),
                (labels_hbm, labels),
            )
        )
    ]
    for copy in copies:
        copy.start()
    for copy in copies:
        copy.wait()
    slots, rows = footprint.shape
    patch_cols = labels.shape[1]
    count = out.shape[0]
    bucket = requests.shape[1] // count
    foot = footprint[...]
    level_of = weight_index[...]
    weight = jnp.zeros((slots, rows), F32)
    for level in range(levels.shape[0]):
        weight = jnp.where(level_of == level, levels[level], weight)
    weight = jnp.where(foot >= 0, weight, 0.0)
    weight = weight / jnp.sum(weight, axis=0, keepdims=True)
    flat = jnp.concatenate([foot[slot : slot + 1] for slot in range(slots)], axis=1)
    owner = jnp.right_shift(flat, bucket.bit_length() - 1)
    place = jnp.bitwise_and(flat, bucket - 1)
    at_place = jnp.where(iota((bucket, slots * rows), 0) == place, 1.0, 0.0).astype(BF16)
    asked = requests[...].astype(F32)
    asked = jnp.concatenate([asked[:, i * bucket : (i + 1) * bucket] for i in range(count)], axis=0)
    offset = dot(asked.astype(BF16), at_place)
    offset = jnp.sum(jnp.where(iota(offset.shape, 0) == owner, offset, 0.0), axis=0, keepdims=True)
    entry = offset + (owner * store).astype(F32)
    entry = jnp.concatenate([entry[:, slot * rows : (slot + 1) * rows] for slot in range(slots)], axis=0)
    lane = iota((8, patch_cols), 1)
    side = iota((8, patch_cols), 0)
    pick = ((side == 0) & (lane == 0)) | ((side == 1) & (lane == patch_cols - 1))
    label = labels[...].astype(F32)
    labels_out[...] = label
    edges = dot_nt(jnp.where(pick, 1.0, 0.0).astype(BF16), label.astype(BF16))
    entries = jnp.concatenate([entry, edges], axis=1)
    weights = jnp.concatenate([weight, jnp.zeros_like(weight)], axis=1)
    for target in range(count):
        out[target, 0:slots, :] = entries
        out[target, slots : 2 * slots, :] = weights


def store_kernel(bands, me_ref, own, mate, stored, edge, sem):
    store, row_width = own.shape
    patch_cols = row_width // bands
    core = me_ref[0] % 2
    copy = pltpu.make_async_copy(own, stored.at[pl.ds(pl.multiple_of(core * store, 64), store)], sem)
    copy.start()
    stored[pl.ds(pl.multiple_of((1 - core) * store, 64), store), :] = mate[...]
    copy.wait()
    row_id = iota((6 * GROUP, patch_cols), 0)
    lane_id = iota((6 * GROUP, patch_cols), 1)
    column = row_id // GROUP
    column_lane = jnp.where(column < 3, column + (patch_cols - 3), column - 3)
    at_column = lane_id == column_lane
    total = jnp.zeros(edge.shape, F32)
    for band in range(bands):
        pick = jnp.where(at_column & (row_id % GROUP == band), 1.0, 0.0).astype(BF16)
        total = total + dot_nt(pick, stored[:, band * patch_cols : (band + 1) * patch_cols])
    edge[...] = total.astype(BF16)


def put_weights(plans, chip, first, target):
    held, lanes = target.shape
    rows = lanes // 2
    slots = plans.shape[1] // 2
    both = jnp.concatenate([plans[2 * chip, :, 0:rows], plans[2 * chip + 1, :, 0:rows]], axis=1)
    entries, weights = both[0:slots] - first, both[slots:]
    for start in range(0, held, 64):
        stored_row = (iota((64, lanes), 0) + start).astype(F32)
        total = jnp.zeros((64, lanes), F32)
        for slot in range(slots):
            total = total + jnp.where(entries[slot : slot + 1] == stored_row, weights[slot : slot + 1], 0.0)
        target[start : start + 64, :] = total


def high_low(value):
    high = value.astype(BF16)
    return high, (value - high.astype(F32)).astype(BF16)


ENDS = 8


def ends_part_kernel(moves, bands, me_ref, plans, stored, edge, row_weights, *refs):
    smalls, (over, sides, product, lines) = refs[:-4], refs[-4:]
    chips = plans.shape[0] // 2
    _, rows, held = row_weights.shape
    cols = stored.shape[1] // bands
    me = me_ref[0]
    here, core = me // 2, me % 2
    first = (here * held).astype(F32)
    sides[0] = jnp.zeros(sides.shape[1:], F32)
    sides[chips + 1] = jnp.zeros(sides.shape[1:], F32)
    for chip in range(chips):
        put_weights(plans, chip, first, over.at[chip])
        high, low = high_low(over[chip])
        sides[chip + 1] = dot(edge[...], high) + dot(edge[...], low)
    ends = []
    for i, move in enumerate(moves):
        both = jnp.transpose(over[jnp.bitwise_xor(here, move)])
        weights = jnp.where(core == 0, both[0:rows], both[rows:])
        row_weights[i] = weights
        ends += [weights[0:ENDS], weights[rows - ENDS : rows]]
    high, low = high_low(jnp.concatenate(ends, axis=0))
    count = high.shape[0]
    both = dot(jnp.concatenate([high, low], axis=0), stored[...])
    product[...] = both[0:count] + both[count:]
    for i, (move, small) in enumerate(zip(moves, smalls, strict=True)):
        pair = slice(2 * ENDS * i, 2 * ENDS * (i + 1))
        for band in range(bands):
            lines[2 * ENDS * band : 2 * ENDS * (band + 1), :] = product[pair, band * cols : (band + 1) * cols]
        small[0 : lines.shape[0], :] = lines[...].astype(small.dtype)
        chip = jnp.bitwise_xor(here, move)
        near, before, after = sides[chip + 1], sides[chip], sides[chip + 2]
        left = jnp.where(core == 1, near[0 : 3 * GROUP, 0:rows], before[0 : 3 * GROUP, rows:])
        right = jnp.where(core == 0, near[3 * GROUP :, rows:], after[3 * GROUP :, 0:rows])
        small[lines.shape[0] :, :] = jnp.concatenate([left, right], axis=1).astype(small.dtype)


def part_kernel(indices, stored, row_weights, *outs):
    rows = outs[0].shape[0]
    row_width = stored.shape[1]
    for index, out in zip(indices, outs, strict=True):
        high, low = high_low(row_weights[index][ENDS : ENDS + rows])
        both = jnp.concatenate([high, low], axis=0)
        for start in range(0, row_width, 512):
            stop = min(start + 512, row_width)
            product = dot(both, stored[:, start:stop])
            out[:, start:stop] = (product[:rows] + product[rows:]).astype(out.dtype)


def ends_kernel(bands, me_ref, plans, labels, *refs):
    count = plans.shape[0]
    rows, cols = labels.shape
    smalls, (upper, lower, total, bundle) = refs[:-4], refs[-4:]
    me = me_ref[0]
    value = smalls[0][...].astype(F32)
    for small in smalls[1:]:
        value = value + small[...].astype(F32)
    total[...] = value
    before = plans[jnp.maximum(me - 1, 0), 1:2, rows : 2 * rows]
    after = plans[jnp.minimum(me + 1, count - 1), 0:1, rows : 2 * rows]
    lines = 2 * ENDS * bands
    for target, start, end in ((upper, 0, 0), (lower, rows - 3, 2 * ENDS - 3)):
        bundle[...] = jnp.zeros_like(bundle)
        for i in range(3):
            line = jnp.concatenate(
                [
                    total[pl.ds(end + i, bands, stride=2 * ENDS), :],
                    labels[start + i : start + i + 1, :],
                    jnp.zeros((GROUP - bands - 1, cols), F32),
                ],
                axis=0,
            )
            target[:, i * cols : (i + 1) * cols] = line.astype(BF16)
            for column, at in ((3, 0), (4, 1), (5, cols - 2), (6, cols - 1)):
                bundle[:, column * 3 + i : column * 3 + i + 1] = line[:, at : at + 1]
        for column in range(3):
            group = total[lines + column * GROUP : lines + (column + 1) * GROUP, :]
            bundle[:, column * 3 : column * 3 + 3] = group[:, start : start + 3]
            at = (column + 7) * 3
            bundle[:, at : at + 3] = group[:, rows + start : rows + start + 3]
        bundle[bands : bands + 1, 6:9] = before[:, start : start + 3]
        bundle[bands : bands + 1, 21:24] = after[:, start : start + 3]
        target[:, 3 * cols :] = bundle[...].astype(BF16)


def composite_kernel(bands, me_ref, plans, labels, *refs):
    count = plans.shape[0]
    tile_rows, patch_cols = labels.shape
    inputs, (main, strips, bank, side) = refs[:-4], refs[-4:]
    parts, smalls = inputs[: len(inputs) // 2], inputs[len(inputs) // 2 :]
    me = me_ref[0]
    small_sum = smalls[0][...].astype(F32)
    for small in smalls[1:]:
        small_sum = small_sum + small[...].astype(F32)
    for band in range(bands):
        columns = slice(band * patch_cols, (band + 1) * patch_cols)
        total = parts[0][:, columns].astype(F32)
        for part in parts[1:]:
            total = total + part[:, columns].astype(F32)
        ends = small_sum[2 * ENDS * band : 2 * ENDS * (band + 1)]
        total = jnp.concatenate([ends[0:ENDS], total, ends[ENDS:]], axis=0)
        bank[band * tile_rows : (band + 1) * tile_rows, :] = total
    bank[bands * tile_rows : (bands + 1) * tile_rows, :] = labels[...]
    bank[(bands + 1) * tile_rows : GROUP * tile_rows, :] = jnp.zeros(
        ((GROUP - bands - 1) * tile_rows, patch_cols), F32
    )
    for row in range(tile_rows):
        main[:, row * patch_cols : (row + 1) * patch_cols] = bank[
            pl.ds(row, GROUP, stride=tile_rows), :
        ].astype(BF16)

    far = small_sum[2 * ENDS * bands :]
    side[...] = jnp.zeros_like(side)
    side[0 : 3 * GROUP, 3 : 3 + tile_rows] = far[:, :tile_rows]
    side[7 * GROUP : 10 * GROUP, 3 : 3 + tile_rows] = far[:, tile_rows:]
    before = plans[jnp.maximum(me - 1, 0), 1:2, tile_rows : 2 * tile_rows]
    after = plans[jnp.minimum(me + 1, count - 1), 0:1, tile_rows : 2 * tile_rows]
    side[2 * GROUP + bands : 2 * GROUP + bands + 1, 3 : 3 + tile_rows] = before
    side[7 * GROUP + bands : 7 * GROUP + bands + 1, 3 : 3 + tile_rows] = after
    row_id = iota((4 * GROUP, patch_cols), 0)
    lane_id = iota((4 * GROUP, patch_cols), 1)
    near = jnp.zeros((4 * GROUP, tile_rows), F32)
    column = row_id // GROUP
    column_lane = jnp.where(column < 2, column, column + (patch_cols - 4))
    for band in range(bands):
        pick = (row_id % GROUP == band) & (lane_id == column_lane)
        tile = bank[band * tile_rows : (band + 1) * tile_rows, :].astype(BF16)
        near = near + dot_nt(jnp.where(pick, 1.0, 0.0).astype(BF16), tile)
    side[3 * GROUP : 7 * GROUP, 3 : 3 + tile_rows] = near
    strips[...] = side[...].astype(BF16)


def weights_kernel(
    conv1_hbm, conv2_hbm, head_hbm, one_main, one_strip, two_main, two_back, head_pad, head_turn,
    wide, tall, conv1, conv2, head, sems,
):
    copies = [
        pltpu.make_async_copy(source, target, sems.at[i])
        for i, (source, target) in enumerate(((conv1_hbm, conv1), (conv2_hbm, conv2), (head_hbm, head)))
    ]
    for copy in copies:
        copy.start()
    for copy in copies:
        copy.wait()
    bands = conv1.shape[1]
    feat = conv2.shape[1]
    classes = head.shape[0]
    wide[...] = jnp.zeros_like(wide)
    for tap in range(9):
        wide[tap * GROUP : tap * GROUP + bands, :] = conv1[tap].astype(F32)
    one_main[...] = jnp.transpose(wide[...]).astype(BF16)
    for tap in range(9):
        wide[tap * GROUP : tap * GROUP + bands, :] = conv1[(tap % 3) * 3 + tap // 3].astype(F32)
    one_strip[...] = jnp.transpose(wide[...]).astype(BF16)
    for row in range(3):
        at = slice(row * feat, (row + 1) * feat)
        two_main[at, :] = jnp.concatenate([conv2[row * 3 + col] for col in range(3)], axis=1)
        turned = jnp.concatenate([conv2[8 - (row * 3 + col)].astype(F32) for col in range(3)], axis=0)
        two_back[at, :] = jnp.transpose(turned).astype(BF16)
    tall[...] = jnp.zeros_like(tall)
    tall[0:classes, 0:feat] = head[...].astype(F32)
    padded = tall[...]
    head_pad[...] = padded[0:GROUP, 0:feat].astype(BF16)
    head_turn[...] = jnp.transpose(padded)[0:feat, 0:GROUP].astype(BF16)


def sigmoid(value):
    return 0.5 * jnp.tanh(0.5 * value) + 0.5


def head_stage(pre, label, mask, head_pad, head_turn, classes):
    gate = sigmoid(pre)
    soft = pre * gate
    skip = soft.astype(BF16)
    logits = dot(head_pad, skip)
    rank = iota(logits.shape, 0)
    real = rank < classes
    total = jnp.sum(jnp.where(real, jnp.exp(logits), 0.0), axis=0, keepdims=True)
    log_total = jnp.log(total)
    chosen = rank == label
    error = jnp.where(real, jnp.exp(logits - log_total) - jnp.where(chosen, 1.0, 0.0), 0.0)
    error = error.astype(BF16)
    loss = log_total - jnp.sum(jnp.where(chosen, logits, 0.0), axis=0, keepdims=True)
    back = dot(head_turn, error)
    slope = back * (gate + soft * (1.0 - gate))
    if mask is not None:
        slope = jnp.where(mask, slope, 0.0)
    return skip, error, slope.astype(BF16), loss


def span(row, count, cols):
    return slice(row * cols, (row + count) * cols)


def put_shifted(target, value, row, count, left_side, right_side, size, cols):
    lane = iota((1, cols), 1)
    target[size : 2 * size, span(row, count, cols)] = value
    for i in range(count):
        tile = value[:, i * cols : (i + 1) * cols]
        turn = (128 - (row + i)) % 128
        left = pltpu.roll(left_side, turn, 1)
        right = pltpu.roll(right_side, (turn + cols - 1) % 128, 1)
        target[0:size, span(row + i, 1, cols)] = jnp.where(lane == 0, left, pltpu.roll(tile, 1, 1))
        target[2 * size : 3 * size, span(row + i, 1, cols)] = jnp.where(
            lane == cols - 1, right, pltpu.roll(tile, cols - 1, 1)
        )


def above_below(ref, row, count, cols):
    return jnp.concatenate([ref[:, span(row + u, count, cols)] for u in (-1, 0, 1)], axis=0)


def below_above(ref, row, count, cols):
    return jnp.concatenate([ref[:, span(row - u, count, cols)] for u in (-1, 0, 1)], axis=0)


def conv_rows(weight, ref, row, count, cols):
    feat = weight.shape[0] // 3
    near = dot(weight[...], ref[:, span(row - 1, count + 2, cols)])
    return (
        near[0:feat, span(0, count, cols)]
        + near[feat : 2 * feat, span(1, count, cols)]
        + near[2 * feat :, span(2, count, cols)]
    )


def turned_rows(value):
    return jnp.concatenate(
        [pltpu.roll(value, 1, 1), value, pltpu.roll(value, value.shape[1] - 1, 1)], axis=0
    ).astype(BF16)


def strip_inside(place, rows, lat_count, lon_count):
    lat, lon = place[0], place[1]
    lane_row = iota((1, 128), 1) - 3
    inside = (lat * rows + lane_row >= 0) & (lat * rows + lane_row < lat_count * rows)
    inside = inside & (lane_row < rows + 3)
    return inside, inside & (lon > 0), inside & (lon < lon_count - 1)


def strip_hidden(side, one_strip, insides, firsts):
    inside, left_inside, right_inside = insides
    taps = {}
    for first in firsts:
        for column in range(first, first + 3):
            if column not in taps:
                taps[column] = turned_rows(side[column * GROUP : (column + 1) * GROUP, :])
    near = jnp.concatenate(
        [jnp.concatenate([taps[first + i] for first in firsts], axis=1) for i in range(3)], axis=0
    )
    pre = dot(one_strip[...], near)
    soft = pre * sigmoid(pre)
    hidden = []
    for i, first in enumerate(firsts):
        mask = left_inside if first in (0, 1) else right_inside if first in (6, 7) else inside
        hidden.append(jnp.where(mask, soft[:, i * 128 : (i + 1) * 128], 0.0))
    return hidden


def hidden_chunk(one_main, band_rows, hidden_rows, rate, row, count, mask, sides, cols):
    pre = dot(one_main[...], above_below(band_rows, row, count, cols))
    gate = sigmoid(pre)
    soft = pre * gate
    if rate is not None:
        rate[:, span(row - 3, count, cols)] = gate + soft * (1.0 - gate)
    if mask is not None:
        soft = jnp.where(mask, soft, 0.0)
    put_shifted(hidden_rows, soft.astype(BF16), row, count, *sides, pre.shape[0], cols)


def label_rows(band_rows, bands, row, count, cols):
    return band_rows[GROUP + bands : GROUP + bands + 1, span(row, count, cols)].astype(F32).astype(jnp.int32)


def network_kernel(
    bands, classes, rows, cols, lat_count, lon_count, step,
    place, main, strips, above, below,
    one_main, one_strip, two_main, two_back, head_pad, head_turn,
    skip_out, keep_out, send_out,
    band_rows, side, hidden_rows, rate, slope_rows, slope_own, sums,
):
    feat = head_turn.shape[0]
    lat, lon = place[0], place[1]

    side[...] = strips[...].astype(F32)
    up_tail = above[:, 3 * cols :].astype(F32)
    down_tail = below[:, 3 * cols :].astype(F32)
    for column in range(10):
        at = slice(column * GROUP, (column + 1) * GROUP)
        side[at, 0:3] = up_tail[:, column * 3 : column * 3 + 3]
        side[at, 3 + rows : 6 + rows] = down_tail[:, column * 3 : column * 3 + 3]

    insides = strip_inside(place, rows, lat_count, lon_count)
    hidden_side = strip_hidden(side, one_strip, insides, (0, 1, 2, 5, 6, 7))
    hidden_taps = [turned_rows(value) for value in hidden_side]
    strip_pre = None
    for col in range(3):
        weight = jnp.concatenate(
            [two_main[u * feat : (u + 1) * feat, col * feat : (col + 1) * feat] for u in range(3)], axis=1
        )
        term = dot(weight, jnp.concatenate([hidden_taps[col], hidden_taps[3 + col]], axis=1))
        strip_pre = term if strip_pre is None else strip_pre + term

    band_sides = (
        side[2 * GROUP : 3 * GROUP, :].astype(BF16),
        side[7 * GROUP : 8 * GROUP, :].astype(BF16),
    )
    put_shifted(band_rows, above[:, 0 : 3 * cols], 0, 3, *band_sides, GROUP, cols)
    put_shifted(band_rows, below[:, 0 : 3 * cols], rows + 3, 3, *band_sides, GROUP, cols)
    put_shifted(band_rows, main[...], 3, rows, *band_sides, GROUP, cols)

    top_inside, bottom_inside = lat > 0, lat < lat_count - 1
    hidden_sides = (hidden_side[1].astype(BF16), hidden_side[4].astype(BF16))
    near = jnp.concatenate(
        [above_below(band_rows, 1, 2, cols), above_below(band_rows, rows + 3, 2, cols)], axis=1
    )
    pre = dot(one_main[...], near)
    soft = pre * sigmoid(pre)
    lane = iota((1, 4 * cols), 1)
    inside = ((lane >= 2 * cols) | top_inside) & ((lane < 2 * cols) | bottom_inside)
    soft = jnp.where(inside, soft, 0.0).astype(BF16)
    put_shifted(hidden_rows, soft[:, span(0, 2, cols)], 1, 2, *hidden_sides, feat, cols)
    put_shifted(hidden_rows, soft[:, span(2, 2, cols)], rows + 3, 2, *hidden_sides, feat, cols)
    for row in range(3, rows + 3, step):
        hidden_chunk(one_main, band_rows, hidden_rows, rate, row, step, None, hidden_sides, cols)

    pre = [conv_rows(two_main, hidden_rows, row, 1, cols) for row in (2, rows + 3)]
    label = [side[c * GROUP + bands : c * GROUP + bands + 1, :].astype(jnp.int32) for c in (2, 7)]
    label += [label_rows(band_rows, bands, row, 1, cols) for row in (2, rows + 3)]
    ones = jnp.ones((1, cols), jnp.int32)
    mask = [jnp.where(inside, 1, 0) for inside in insides[1:]]
    mask += [jnp.where(inside, ones, 0) for inside in (top_inside, bottom_inside)]
    slope = head_stage(
        jnp.concatenate([strip_pre] + pre, axis=1),
        jnp.concatenate(label, axis=1),
        jnp.concatenate(mask, axis=1) > 0,
        head_pad[...],
        head_turn[...],
        classes,
    )[2]
    slope_side = (slope[:, 0:128], slope[:, 128:256])
    put_shifted(slope_rows, slope[:, 256 : 256 + cols], 2, 1, *slope_side, feat, cols)
    put_shifted(slope_rows, slope[:, 256 + cols :], rows + 3, 1, *slope_side, feat, cols)

    for row in (1, rows + 3):
        slope_own[:, span(row, 2, cols)] = jnp.zeros((feat, 2 * cols), BF16)
    grad_head = jnp.zeros((feat, GROUP), F32)
    loss_sum = jnp.zeros((1, 1), F32)
    for row in range(3, rows + 3, step):
        pre = conv_rows(two_main, hidden_rows, row, step, cols)
        label = label_rows(band_rows, bands, row, step, cols)
        skip, error, slope, loss = head_stage(pre, label, None, head_pad[...], head_turn[...], classes)
        skip_out[:, span(row - 3, step, cols)] = skip
        slope_own[:, span(row, step, cols)] = slope
        grad_head = grad_head + dot_nt(skip, error)
        put_shifted(slope_rows, slope, row, step, *slope_side, feat, cols)
        loss_sum = loss_sum + jnp.sum(loss, axis=1, keepdims=True)

    def grad_of(product):
        total = None
        for row in range(2, rows + 4, 11):
            count = min(11, rows + 4 - row)
            term = product(below_above(slope_own, row, count, cols), span(row, count, cols))
            total = term if total is None else total + term
        return total

    sums[...] = jnp.zeros_like(sums)
    sums[:, 0 : 3 * feat] = grad_of(lambda slopes, at: dot_nt(slopes, hidden_rows[:, at]))
    for row in range(3, rows + 3, step):
        back = conv_rows(two_back, slope_rows, row, step, cols)
        slope_own[:, span(row, step, cols)] = (back * rate[:, span(row - 3, step, cols)]).astype(BF16)
    sums[:, 3 * feat : 3 * feat + 3 * GROUP] = grad_of(lambda slopes, at: dot_nt(slopes, band_rows[:, at]))
    at = 3 * feat + 3 * GROUP
    sums[0:feat, at : at + GROUP] = grad_head
    sums[feat : feat + 1, at : at + 1] = loss_sum
    half = 3 * feat // 2
    core = lon % 2
    keep_out[...] = sums[pl.ds(pl.multiple_of(core * half, 8), half), :]
    send_out[...] = sums[pl.ds(pl.multiple_of((1 - core) * half, 8), half), :]


def finish_kernel(pixels, me_ref, own, mate, grad_one, grad_two, grad_head, loss, sums):
    half = own.shape[0]
    feat = grad_two.shape[1]
    bands = grad_one.shape[1]
    classes = grad_head.shape[0]
    core = me_ref[0] % 2
    scale = 1.0 / pixels
    sums[pl.ds(pl.multiple_of(core * half, 8), half), :] = own[...] * scale
    sums[pl.ds(pl.multiple_of((1 - core) * half, 8), half), :] = mate[...] * scale
    at = 3 * feat
    turned = jnp.transpose(sums[:, at : at + 3 * GROUP + GROUP])
    for tap in range(9):
        u, v = tap // 3, tap % 3
        grad_two[tap] = sums[u * feat : (u + 1) * feat, v * feat : (v + 1) * feat]
        grad_one[tap] = turned[v * GROUP : v * GROUP + bands, u * feat : (u + 1) * feat]
    grad_head[...] = turned[3 * GROUP : 3 * GROUP + classes, 0:feat]
    loss_row = turned[3 * GROUP : 3 * GROUP + 1]
    loss[...] = loss_row[:, feat : feat + 1] + loss_row[:, feat + GROUP : feat + GROUP + 1]


def tree_sum(values):
    values = list(values)
    while len(values) > 1:
        values = [values[i] + values[i + 1] for i in range(0, len(values), 2)]
    return values[0]


def body(
    patches,
    requests,
    footprint,
    weight_index,
    composite_weights,
    labels,
    conv1_weight,
    conv2_weight,
    head_weight,
):
    lon_count = lax.axis_size("lon")
    lat_count = lax.axis_size("lat")
    chips = lon_count // 2
    rows, slots = footprint.shape
    cols = labels.shape[1]
    store, row_width = patches.shape
    bands = row_width // cols
    bucket = requests.shape[1] // lon_count
    feat = conv2_weight.shape[1]
    classes = head_weight.shape[0]
    vmem = pl.BlockSpec(memory_space=pltpu.VMEM)
    smem = pl.BlockSpec(memory_space=pltpu.SMEM)

    lon = lax.axis_index("lon")
    place = jnp.stack([lax.axis_index("lat"), lon]).astype(jnp.int32)
    me = lon.astype(jnp.int32).reshape(1)

    def by_lon(value, move):
        return lax.ppermute(value, "lon", [(i, i ^ move) for i in range(lon_count)])

    hbm = pl.BlockSpec(memory_space=pltpu.HBM)
    in_hbm = lambda value: pltpu.with_memory_space_constraint(value, pltpu.HBM)
    plan, tile_labels = call(
        functools.partial(plan_kernel, store),
        [struct((lon_count, 16, 128), F32), struct((rows, cols), F32)],
        [
            pltpu.VMEM(requests.shape, jnp.int32),
            pltpu.VMEM((slots, rows), jnp.int32),
            pltpu.VMEM((slots, rows), jnp.int32),
            pltpu.SMEM(composite_weights.shape, F32),
            pltpu.VMEM(labels.shape, jnp.int32),
            pltpu.SemaphoreType.DMA((5,)),
        ],
        vmem_limit=63 * 1024 * 1024,
        in_specs=[hbm] * 5,
    )(requests, footprint.T, weight_index.T, composite_weights, labels)
    plan, patches = lax.optimization_barrier((plan, patches))
    mate_patches = by_lon(patches, 1)
    plans = lax.all_to_all(plan, "lon", split_axis=0, concat_axis=0, tiled=True)
    stored, edge = call(
        functools.partial(store_kernel, bands),
        [struct((2 * store, row_width), BF16), struct((6 * GROUP, 2 * store), BF16)],
        [pltpu.SemaphoreType.DMA],
        in_specs=[smem, hbm, vmem],
        cost_estimate=pl.CostEstimate(flops=10**9, bytes_accessed=10**7, transcendentals=0),
    )(me, in_hbm(patches), mate_patches)
    plans, stored, edge = lax.optimization_barrier((plans, stored, edge))
    moves = list(range(chips - 1, -1, -1))
    small_lines = 2 * ENDS * bands + 3 * GROUP
    cost = pl.CostEstimate(flops=10**9, bytes_accessed=10**7, transcendentals=0)
    row_weights, *smalls = call(
        functools.partial(ends_part_kernel, moves, bands),
        [struct((chips, rows, 2 * store), F32)]
        + [struct((small_lines, cols), BF16 if move else F32) for move in moves],
        [
            pltpu.VMEM((chips, 2 * store, 2 * rows), F32),
            pltpu.VMEM((chips + 2, 6 * GROUP, 2 * rows), F32),
            pltpu.VMEM((2 * ENDS * chips, row_width), F32),
            pltpu.VMEM((2 * ENDS * bands, cols), F32),
        ],
        in_specs=[smem, vmem, vmem, vmem],
        cost_estimate=cost,
    )(me, plans, stored, edge)
    smalls = [by_lon(small, 2 * move) if move else small for move, small in zip(moves, smalls)]
    parts = []
    for some in (moves[:-1], moves[-1:]):
        if len(some) == 1:
            row_weights, *smalls = lax.optimization_barrier((row_weights, *smalls))
        parts += call(
            functools.partial(part_kernel, [moves.index(move) for move in some]),
            [struct((rows - 2 * ENDS, row_width), BF16 if move else F32) for move in some],
            in_specs=[vmem, vmem],
            cost_estimate=cost,
        )(stored, row_weights)
    parts = [by_lon(part, 2 * move) if move else part for move, part in zip(moves, parts)]
    upper, lower = call(
        functools.partial(ends_kernel, bands),
        [struct((GROUP, 3 * cols + 128), BF16)] * 2,
        [pltpu.VMEM((small_lines, cols), F32), pltpu.VMEM((GROUP, 128), F32)],
        in_specs=[smem] + [vmem] * (2 + chips),
        cost_estimate=pl.CostEstimate(flops=3 * 10**10, bytes_accessed=10**7, transcendentals=0),
    )(me, plans, tile_labels, *smalls)
    main, strips = call(
        functools.partial(composite_kernel, bands),
        [struct((GROUP, rows * cols), BF16), struct((10 * GROUP, 128), BF16)],
        [pltpu.VMEM(((GROUP + 1) * rows, cols), F32), pltpu.VMEM((10 * GROUP, 128), F32)],
        in_specs=[smem] + [vmem] * (2 + 2 * chips),
        cost_estimate=cost,
    )(me, plans, tile_labels, *parts, *smalls)
    below = lax.ppermute(upper, "lat", [(i + 1, i) for i in range(lat_count - 1)])
    above = lax.ppermute(lower, "lat", [(i, i + 1) for i in range(lat_count - 1)])

    one_main, one_strip, two_main, two_back, head_pad, head_turn = call(
        weights_kernel,
        [
            struct((feat, 9 * GROUP), BF16),
            struct((feat, 9 * GROUP), BF16),
            struct((3 * feat, 3 * feat), BF16),
            struct((3 * feat, 3 * feat), BF16),
            struct((GROUP, feat), BF16),
            struct((feat, GROUP), BF16),
        ],
        [
            pltpu.VMEM((9 * GROUP, feat), F32),
            pltpu.VMEM((128, 128), F32),
            pltpu.VMEM((9, bands, feat), BF16),
            pltpu.VMEM(conv2_weight.shape, BF16),
            pltpu.VMEM(head_weight.shape, BF16),
            pltpu.SemaphoreType.DMA((3,)),
        ],
        in_specs=[hbm] * 3,
    )(*[in_hbm(value) for value in (conv1_weight.transpose(0, 2, 1), conv2_weight, head_weight)])

    ext = rows + 6
    half = 3 * feat // 2
    sum_width = 3 * feat + 4 * GROUP
    skip, keep, send = call(
        functools.partial(network_kernel, bands, classes, rows, cols, lat_count, lon_count, 32),
        [
            struct((feat, rows * cols), BF16),
            struct((half, sum_width), F32),
            struct((half, sum_width), F32),
        ],
        [
            pltpu.VMEM((3 * GROUP, ext * cols), BF16),
            pltpu.VMEM((10 * GROUP, 128), F32),
            pltpu.VMEM((3 * feat, ext * cols), BF16),
            pltpu.VMEM((feat, rows * cols), F32),
            pltpu.VMEM((3 * feat, ext * cols), BF16),
            pltpu.VMEM((feat, ext * cols), BF16),
            pltpu.VMEM((3 * feat, sum_width), F32),
        ],
        in_specs=[smem] + [vmem] * 10,
    )(
        place, main, strips, above, below,
        one_main, one_strip, two_main, two_back, head_pad, head_turn,
    )

    last = sum_width - 128
    row_id, lane_id = iota((2 * GROUP, 128), 0), iota((2 * GROUP, 128), 1)
    at_loss = lane_id == 3 * feat + 3 * GROUP - last
    at_loss, at_rest = at_loss & (row_id == 0), at_loss & (row_id == GROUP)

    def sum_over(value, axis, moves):
        tile = value[feat : feat + 2 * GROUP, last:]
        tile = jnp.where(at_loss, tile + jnp.roll(tile, GROUP, axis=0), tile)
        rest = jnp.roll(tile - lax.reduce_precision(tile, 8, 7), GROUP, axis=0)
        tile = jnp.where(at_rest, rest, tile)
        rounded = lax.reduce_precision(lax.dynamic_update_slice(value, tile, (feat, last)), 8, 7)
        sent = rounded.astype(BF16)
        size = lax.axis_size(axis)
        terms = [rounded]
        for move in moves:
            terms.append(lax.ppermute(sent, axis, [(i, i ^ move) for i in range(size)]).astype(F32))
        return tree_sum(terms)

    total = keep + by_lon(send, 1)
    total = sum_over(total, "lon", range(2, lon_count, 2))
    total = sum_over(total, "lat", range(1, lat_count))
    other = by_lon(total, 1)
    pixels = rows * cols * lat_count * lon_count
    grad_one, grad_two, grad_head, loss = call(
        functools.partial(finish_kernel, pixels),
        [
            struct((9, bands, feat), F32),
            struct((9, feat, feat), F32),
            struct((classes, feat), F32),
            struct((1, 1), F32),
        ],
        [pltpu.VMEM((3 * feat, sum_width), F32)],
        in_specs=[smem, vmem, vmem],
    )(me, total, other)
    return skip.reshape(feat, rows, cols), grad_one.transpose(0, 2, 1), grad_two, grad_head, loss.reshape(())


def solution(mesh):
    placed = (
        P(("lat", "lon"), None),
        P("lat", "lon"),
        P("lat", "lon"),
        P("lat", "lon"),
        P(),
        P("lat", "lon"),
        P(),
        P(),
        P(),
    )
    return jax.shard_map(
        body,
        mesh=mesh,
        in_specs=placed,
        out_specs=(P(None, "lat", "lon"), P(), P(), P(), P()),
        check_vma=False,
    )
```

```python
import functools

import jax
import jax.numpy as jnp
from jax import lax
from jax.experimental import pallas as pl
from jax.experimental.pallas import tpu as pltpu
from jax.sharding import PartitionSpec as P

BF16 = jnp.bfloat16
F32 = jnp.float32
GROUP = 16
VMEM_LIMIT = 28 * 1024 * 1024


def dot(left, right):
    return lax.dot_general(left, right, (((1,), (0,)), ((), ())), preferred_element_type=F32)


def dot_nt(left, right):
    return lax.dot_general(left, right, (((1,), (1,)), ((), ())), preferred_element_type=F32)


def iota(shape, dim):
    return lax.broadcasted_iota(jnp.int32, shape, dim)


def call(kernel, out_shape, scratch=(), vmem_limit=VMEM_LIMIT, **kwargs):
    return pl.pallas_call(
        kernel,
        out_shape=out_shape,
        scratch_shapes=list(scratch),
        compiler_params=pltpu.CompilerParams(vmem_limit_bytes=vmem_limit),
        **kwargs,
    )


def struct(shape, dtype):
    return jax.ShapeDtypeStruct(shape, dtype)


def plan_kernel(
    store, requests_hbm, footprint_hbm, weight_index_hbm, levels_hbm, labels_hbm, out, labels_out,
    requests, footprint, weight_index, levels, labels, sems,
):
    copies = [
        pltpu.make_async_copy(source, target, sems.at[i])
        for i, (source, target) in enumerate(
            (
                (footprint_hbm, footprint),
                (requests_hbm, requests),
                (weight_index_hbm, weight_index),
                (levels_hbm, levels),
                (labels_hbm, labels),
            )
        )
    ]
    for copy in copies:
        copy.start()
    for copy in copies:
        copy.wait()
    slots, rows = footprint.shape
    patch_cols = labels.shape[1]
    count = out.shape[0]
    bucket = requests.shape[1] // count
    foot = footprint[...]
    level_of = weight_index[...]
    weight = jnp.zeros((slots, rows), F32)
    for level in range(levels.shape[0]):
        weight = jnp.where(level_of == level, levels[level], weight)
    weight = jnp.where(foot >= 0, weight, 0.0)
    weight = weight / jnp.sum(weight, axis=0, keepdims=True)
    flat = jnp.concatenate([foot[slot : slot + 1] for slot in range(slots)], axis=1)
    owner = jnp.right_shift(flat, bucket.bit_length() - 1)
    place = jnp.bitwise_and(flat, bucket - 1)
    at_place = jnp.where(iota((bucket, slots * rows), 0) == place, 1.0, 0.0).astype(BF16)
    asked = requests[...].astype(F32)
    asked = jnp.concatenate([asked[:, i * bucket : (i + 1) * bucket] for i in range(count)], axis=0)
    offset = dot(asked.astype(BF16), at_place)
    offset = jnp.sum(jnp.where(iota(offset.shape, 0) == owner, offset, 0.0), axis=0, keepdims=True)
    entry = offset + (owner * store).astype(F32)
    entry = jnp.concatenate([entry[:, slot * rows : (slot + 1) * rows] for slot in range(slots)], axis=0)
    lane = iota((8, patch_cols), 1)
    side = iota((8, patch_cols), 0)
    pick = ((side == 0) & (lane == 0)) | ((side == 1) & (lane == patch_cols - 1))
    label = labels[...].astype(F32)
    labels_out[...] = label
    edges = dot_nt(jnp.where(pick, 1.0, 0.0).astype(BF16), label.astype(BF16))
    entries = jnp.concatenate([entry, edges], axis=1)
    weights = jnp.concatenate([weight, jnp.zeros_like(weight)], axis=1)
    for target in range(count):
        out[target, 0:slots, :] = entries
        out[target, slots : 2 * slots, :] = weights


def store_kernel(bands, me_ref, own, mate, stored, edge, sem):
    store, row_width = own.shape
    patch_cols = row_width // bands
    core = me_ref[0] % 2
    copy = pltpu.make_async_copy(own, stored.at[pl.ds(pl.multiple_of(core * store, 64), store)], sem)
    copy.start()
    stored[pl.ds(pl.multiple_of((1 - core) * store, 64), store), :] = mate[...]
    copy.wait()
    row_id = iota((6 * GROUP, patch_cols), 0)
    lane_id = iota((6 * GROUP, patch_cols), 1)
    column = row_id // GROUP
    column_lane = jnp.where(column < 3, column + (patch_cols - 3), column - 3)
    at_column = lane_id == column_lane
    total = jnp.zeros(edge.shape, F32)
    for band in range(bands):
        pick = jnp.where(at_column & (row_id % GROUP == band), 1.0, 0.0).astype(BF16)
        total = total + dot_nt(pick, stored[:, band * patch_cols : (band + 1) * patch_cols])
    edge[...] = total.astype(BF16)


def put_weights(plans, chip, first, target):
    held, lanes = target.shape
    rows = lanes // 2
    slots = plans.shape[1] // 2
    both = jnp.concatenate([plans[2 * chip, :, 0:rows], plans[2 * chip + 1, :, 0:rows]], axis=1)
    entries, weights = both[0:slots] - first, both[slots:]
    for start in range(0, held, 64):
        stored_row = (iota((64, lanes), 0) + start).astype(F32)
        total = jnp.zeros((64, lanes), F32)
        for slot in range(slots):
            total = total + jnp.where(entries[slot : slot + 1] == stored_row, weights[slot : slot + 1], 0.0)
        target[start : start + 64, :] = total


def high_low(value):
    high = value.astype(BF16)
    return high, (value - high.astype(F32)).astype(BF16)


ENDS = 8


def ends_part_kernel(moves, bands, me_ref, plans, stored, edge, row_weights, *refs):
    smalls, (over, sides, product, lines) = refs[:-4], refs[-4:]
    chips = plans.shape[0] // 2
    _, rows, held = row_weights.shape
    cols = stored.shape[1] // bands
    me = me_ref[0]
    here, core = me // 2, me % 2
    first = (here * held).astype(F32)
    sides[0] = jnp.zeros(sides.shape[1:], F32)
    sides[chips + 1] = jnp.zeros(sides.shape[1:], F32)
    for chip in range(chips):
        put_weights(plans, chip, first, over.at[chip])
        high, low = high_low(over[chip])
        sides[chip + 1] = dot(edge[...], high) + dot(edge[...], low)
    ends = []
    for i, move in enumerate(moves):
        both = jnp.transpose(over[jnp.bitwise_xor(here, move)])
        weights = jnp.where(core == 0, both[0:rows], both[rows:])
        row_weights[i] = weights
        ends += [weights[0:ENDS], weights[rows - ENDS : rows]]
    high, low = high_low(jnp.concatenate(ends, axis=0))
    count = high.shape[0]
    both = dot(jnp.concatenate([high, low], axis=0), stored[...])
    product[...] = both[0:count] + both[count:]
    for i, (move, small) in enumerate(zip(moves, smalls, strict=True)):
        pair = slice(2 * ENDS * i, 2 * ENDS * (i + 1))
        for band in range(bands):
            lines[2 * ENDS * band : 2 * ENDS * (band + 1), :] = product[pair, band * cols : (band + 1) * cols]
        small[0 : lines.shape[0], :] = lines[...].astype(small.dtype)
        chip = jnp.bitwise_xor(here, move)
        near, before, after = sides[chip + 1], sides[chip], sides[chip + 2]
        left = jnp.where(core == 1, near[0 : 3 * GROUP, 0:rows], before[0 : 3 * GROUP, rows:])
        right = jnp.where(core == 0, near[3 * GROUP :, rows:], after[3 * GROUP :, 0:rows])
        small[lines.shape[0] :, :] = jnp.concatenate([left, right], axis=1).astype(small.dtype)


def part_kernel(indices, stored, row_weights, *outs):
    rows = outs[0].shape[0]
    row_width = stored.shape[1]
    for index, out in zip(indices, outs, strict=True):
        high, low = high_low(row_weights[index][ENDS : ENDS + rows])
        both = jnp.concatenate([high, low], axis=0)
        for start in range(0, row_width, 512):
            stop = min(start + 512, row_width)
            product = dot(both, stored[:, start:stop])
            out[:, start:stop] = (product[:rows] + product[rows:]).astype(out.dtype)


def ends_kernel(bands, me_ref, plans, labels, *refs):
    count = plans.shape[0]
    rows, cols = labels.shape
    smalls, (upper, lower, total, bundle) = refs[:-4], refs[-4:]
    me = me_ref[0]
    value = smalls[0][...].astype(F32)
    for small in smalls[1:]:
        value = value + small[...].astype(F32)
    total[...] = value
    before = plans[jnp.maximum(me - 1, 0), 1:2, rows : 2 * rows]
    after = plans[jnp.minimum(me + 1, count - 1), 0:1, rows : 2 * rows]
    lines = 2 * ENDS * bands
    for target, start, end in ((upper, 0, 0), (lower, rows - 3, 2 * ENDS - 3)):
        bundle[...] = jnp.zeros_like(bundle)
        for i in range(3):
            line = jnp.concatenate(
                [
                    total[pl.ds(end + i, bands, stride=2 * ENDS), :],
                    labels[start + i : start + i + 1, :],
                    jnp.zeros((GROUP - bands - 1, cols), F32),
                ],
                axis=0,
            )
            target[:, i * cols : (i + 1) * cols] = line.astype(BF16)
            for column, at in ((3, 0), (4, 1), (5, cols - 2), (6, cols - 1)):
                bundle[:, column * 3 + i : column * 3 + i + 1] = line[:, at : at + 1]
        for column in range(3):
            group = total[lines + column * GROUP : lines + (column + 1) * GROUP, :]
            bundle[:, column * 3 : column * 3 + 3] = group[:, start : start + 3]
            at = (column + 7) * 3
            bundle[:, at : at + 3] = group[:, rows + start : rows + start + 3]
        bundle[bands : bands + 1, 6:9] = before[:, start : start + 3]
        bundle[bands : bands + 1, 21:24] = after[:, start : start + 3]
        target[:, 3 * cols :] = bundle[...].astype(BF16)


def composite_kernel(bands, me_ref, plans, labels, *refs):
    count = plans.shape[0]
    tile_rows, patch_cols = labels.shape
    inputs, (main, strips, bank, side) = refs[:-4], refs[-4:]
    parts, smalls = inputs[: len(inputs) // 2], inputs[len(inputs) // 2 :]
    me = me_ref[0]
    small_sum = smalls[0][...].astype(F32)
    for small in smalls[1:]:
        small_sum = small_sum + small[...].astype(F32)
    for band in range(bands):
        columns = slice(band * patch_cols, (band + 1) * patch_cols)
        total = parts[0][:, columns].astype(F32)
        for part in parts[1:]:
            total = total + part[:, columns].astype(F32)
        ends = small_sum[2 * ENDS * band : 2 * ENDS * (band + 1)]
        total = jnp.concatenate([ends[0:ENDS], total, ends[ENDS:]], axis=0)
        bank[band * tile_rows : (band + 1) * tile_rows, :] = total
    bank[bands * tile_rows : (bands + 1) * tile_rows, :] = labels[...]
    bank[(bands + 1) * tile_rows : GROUP * tile_rows, :] = jnp.zeros(
        ((GROUP - bands - 1) * tile_rows, patch_cols), F32
    )
    for row in range(tile_rows):
        main[:, row * patch_cols : (row + 1) * patch_cols] = bank[
            pl.ds(row, GROUP, stride=tile_rows), :
        ].astype(BF16)

    far = small_sum[2 * ENDS * bands :]
    side[...] = jnp.zeros_like(side)
    side[0 : 3 * GROUP, 3 : 3 + tile_rows] = far[:, :tile_rows]
    side[7 * GROUP : 10 * GROUP, 3 : 3 + tile_rows] = far[:, tile_rows:]
    before = plans[jnp.maximum(me - 1, 0), 1:2, tile_rows : 2 * tile_rows]
    after = plans[jnp.minimum(me + 1, count - 1), 0:1, tile_rows : 2 * tile_rows]
    side[2 * GROUP + bands : 2 * GROUP + bands + 1, 3 : 3 + tile_rows] = before
    side[7 * GROUP + bands : 7 * GROUP + bands + 1, 3 : 3 + tile_rows] = after
    row_id = iota((4 * GROUP, patch_cols), 0)
    lane_id = iota((4 * GROUP, patch_cols), 1)
    near = jnp.zeros((4 * GROUP, tile_rows), F32)
    column = row_id // GROUP
    column_lane = jnp.where(column < 2, column, column + (patch_cols - 4))
    for band in range(bands):
        pick = (row_id % GROUP == band) & (lane_id == column_lane)
        tile = bank[band * tile_rows : (band + 1) * tile_rows, :].astype(BF16)
        near = near + dot_nt(jnp.where(pick, 1.0, 0.0).astype(BF16), tile)
    side[3 * GROUP : 7 * GROUP, 3 : 3 + tile_rows] = near
    strips[...] = side[...].astype(BF16)


def weights_kernel(
    conv1, conv2_hbm, head, one_main, one_strip, two_main, two_back, head_pad, head_turn,
    wide, tall, conv2, sem,
):
    copy = pltpu.make_async_copy(conv2_hbm, conv2, sem)
    copy.start()
    copy.wait()
    bands = conv1.shape[1]
    feat = conv2.shape[1]
    classes = head.shape[0]
    wide[...] = jnp.zeros_like(wide)
    for tap in range(9):
        wide[tap * GROUP : tap * GROUP + bands, :] = conv1[tap].astype(F32)
    one_main[...] = jnp.transpose(wide[...]).astype(BF16)
    for tap in range(9):
        wide[tap * GROUP : tap * GROUP + bands, :] = conv1[(tap % 3) * 3 + tap // 3].astype(F32)
    one_strip[...] = jnp.transpose(wide[...]).astype(BF16)
    for row in range(3):
        at = slice(row * feat, (row + 1) * feat)
        two_main[at, :] = jnp.concatenate([conv2[row * 3 + col] for col in range(3)], axis=1)
        turned = jnp.concatenate([conv2[8 - (row * 3 + col)].astype(F32) for col in range(3)], axis=0)
        two_back[at, :] = jnp.transpose(turned).astype(BF16)
    tall[...] = jnp.zeros_like(tall)
    tall[0:classes, 0:feat] = head[...].astype(F32)
    padded = tall[...]
    head_pad[...] = padded[0:GROUP, 0:feat].astype(BF16)
    head_turn[...] = jnp.transpose(padded)[0:feat, 0:GROUP].astype(BF16)


def sigmoid(value):
    return 0.5 * jnp.tanh(0.5 * value) + 0.5


def head_stage(pre, label, mask, head_pad, head_turn, classes):
    gate = sigmoid(pre)
    soft = pre * gate
    skip = soft.astype(BF16)
    logits = dot(head_pad, skip)
    rank = iota(logits.shape, 0)
    real = rank < classes
    total = jnp.sum(jnp.where(real, jnp.exp(logits), 0.0), axis=0, keepdims=True)
    log_total = jnp.log(total)
    chosen = rank == label
    error = jnp.where(real, jnp.exp(logits - log_total) - jnp.where(chosen, 1.0, 0.0), 0.0)
    error = error.astype(BF16)
    loss = log_total - jnp.sum(jnp.where(chosen, logits, 0.0), axis=0, keepdims=True)
    back = dot(head_turn, error)
    slope = back * (gate + soft * (1.0 - gate))
    if mask is not None:
        slope = jnp.where(mask, slope, 0.0)
    return skip, error, slope.astype(BF16), loss


def span(row, count, cols):
    return slice(row * cols, (row + count) * cols)


def put_shifted(target, value, row, count, left_side, right_side, size, cols):
    lane = iota((1, cols), 1)
    target[size : 2 * size, span(row, count, cols)] = value
    for i in range(count):
        tile = value[:, i * cols : (i + 1) * cols]
        turn = (128 - (row + i)) % 128
        left = pltpu.roll(left_side, turn, 1)
        right = pltpu.roll(right_side, (turn + cols - 1) % 128, 1)
        target[0:size, span(row + i, 1, cols)] = jnp.where(lane == 0, left, pltpu.roll(tile, 1, 1))
        target[2 * size : 3 * size, span(row + i, 1, cols)] = jnp.where(
            lane == cols - 1, right, pltpu.roll(tile, cols - 1, 1)
        )


def above_below(ref, row, count, cols):
    return jnp.concatenate([ref[:, span(row + u, count, cols)] for u in (-1, 0, 1)], axis=0)


def below_above(ref, row, count, cols):
    return jnp.concatenate([ref[:, span(row - u, count, cols)] for u in (-1, 0, 1)], axis=0)


def conv_rows(weight, ref, row, count, cols):
    feat = weight.shape[0] // 3
    near = dot(weight[...], ref[:, span(row - 1, count + 2, cols)])
    return (
        near[0:feat, span(0, count, cols)]
        + near[feat : 2 * feat, span(1, count, cols)]
        + near[2 * feat :, span(2, count, cols)]
    )


def turned_rows(value):
    return jnp.concatenate(
        [pltpu.roll(value, 1, 1), value, pltpu.roll(value, value.shape[1] - 1, 1)], axis=0
    ).astype(BF16)


def strip_inside(place, rows, lat_count, lon_count):
    lat, lon = place[0], place[1]
    lane_row = iota((1, 128), 1) - 3
    inside = (lat * rows + lane_row >= 0) & (lat * rows + lane_row < lat_count * rows)
    inside = inside & (lane_row < rows + 3)
    return inside, inside & (lon > 0), inside & (lon < lon_count - 1)


def strip_hidden(side, one_strip, insides, firsts):
    inside, left_inside, right_inside = insides
    taps = {}
    for first in firsts:
        for column in range(first, first + 3):
            if column not in taps:
                taps[column] = turned_rows(side[column * GROUP : (column + 1) * GROUP, :])
    near = jnp.concatenate(
        [jnp.concatenate([taps[first + i] for first in firsts], axis=1) for i in range(3)], axis=0
    )
    pre = dot(one_strip[...], near)
    soft = pre * sigmoid(pre)
    hidden = []
    for i, first in enumerate(firsts):
        mask = left_inside if first in (0, 1) else right_inside if first in (6, 7) else inside
        hidden.append(jnp.where(mask, soft[:, i * 128 : (i + 1) * 128], 0.0))
    return hidden


def hidden_chunk(one_main, band_rows, hidden_rows, rate, row, count, mask, sides, cols):
    pre = dot(one_main[...], above_below(band_rows, row, count, cols))
    gate = sigmoid(pre)
    soft = pre * gate
    if rate is not None:
        rate[:, span(row - 3, count, cols)] = gate + soft * (1.0 - gate)
    if mask is not None:
        soft = jnp.where(mask, soft, 0.0)
    put_shifted(hidden_rows, soft.astype(BF16), row, count, *sides, pre.shape[0], cols)


def label_rows(band_rows, bands, row, count, cols):
    return band_rows[GROUP + bands : GROUP + bands + 1, span(row, count, cols)].astype(F32).astype(jnp.int32)


def network_kernel(
    bands, classes, rows, cols, lat_count, lon_count, step,
    place, main, strips, above, below,
    one_main, one_strip, two_main, two_back, head_pad, head_turn,
    skip_out, keep_out, send_out,
    band_rows, side, hidden_rows, rate, slope_rows, slope_own, sums,
):
    feat = head_turn.shape[0]
    lat, lon = place[0], place[1]

    side[...] = strips[...].astype(F32)
    up_tail = above[:, 3 * cols :].astype(F32)
    down_tail = below[:, 3 * cols :].astype(F32)
    for column in range(10):
        at = slice(column * GROUP, (column + 1) * GROUP)
        side[at, 0:3] = up_tail[:, column * 3 : column * 3 + 3]
        side[at, 3 + rows : 6 + rows] = down_tail[:, column * 3 : column * 3 + 3]

    insides = strip_inside(place, rows, lat_count, lon_count)
    hidden_side = strip_hidden(side, one_strip, insides, (0, 1, 2, 5, 6, 7))
    hidden_taps = [turned_rows(value) for value in hidden_side]
    strip_pre = None
    for col in range(3):
        weight = jnp.concatenate(
            [two_main[u * feat : (u + 1) * feat, col * feat : (col + 1) * feat] for u in range(3)], axis=1
        )
        term = dot(weight, jnp.concatenate([hidden_taps[col], hidden_taps[3 + col]], axis=1))
        strip_pre = term if strip_pre is None else strip_pre + term

    band_sides = (
        side[2 * GROUP : 3 * GROUP, :].astype(BF16),
        side[7 * GROUP : 8 * GROUP, :].astype(BF16),
    )
    put_shifted(band_rows, above[:, 0 : 3 * cols], 0, 3, *band_sides, GROUP, cols)
    put_shifted(band_rows, below[:, 0 : 3 * cols], rows + 3, 3, *band_sides, GROUP, cols)
    put_shifted(band_rows, main[...], 3, rows, *band_sides, GROUP, cols)

    top_inside, bottom_inside = lat > 0, lat < lat_count - 1
    hidden_sides = (hidden_side[1].astype(BF16), hidden_side[4].astype(BF16))
    near = jnp.concatenate(
        [above_below(band_rows, 1, 2, cols), above_below(band_rows, rows + 3, 2, cols)], axis=1
    )
    pre = dot(one_main[...], near)
    soft = pre * sigmoid(pre)
    lane = iota((1, 4 * cols), 1)
    inside = ((lane >= 2 * cols) | top_inside) & ((lane < 2 * cols) | bottom_inside)
    soft = jnp.where(inside, soft, 0.0).astype(BF16)
    put_shifted(hidden_rows, soft[:, span(0, 2, cols)], 1, 2, *hidden_sides, feat, cols)
    put_shifted(hidden_rows, soft[:, span(2, 2, cols)], rows + 3, 2, *hidden_sides, feat, cols)
    for row in range(3, rows + 3, step):
        hidden_chunk(one_main, band_rows, hidden_rows, rate, row, step, None, hidden_sides, cols)

    pre = [conv_rows(two_main, hidden_rows, row, 1, cols) for row in (2, rows + 3)]
    label = [side[c * GROUP + bands : c * GROUP + bands + 1, :].astype(jnp.int32) for c in (2, 7)]
    label += [label_rows(band_rows, bands, row, 1, cols) for row in (2, rows + 3)]
    ones = jnp.ones((1, cols), jnp.int32)
    mask = [jnp.where(inside, 1, 0) for inside in insides[1:]]
    mask += [jnp.where(inside, ones, 0) for inside in (top_inside, bottom_inside)]
    slope = head_stage(
        jnp.concatenate([strip_pre] + pre, axis=1),
        jnp.concatenate(label, axis=1),
        jnp.concatenate(mask, axis=1) > 0,
        head_pad[...],
        head_turn[...],
        classes,
    )[2]
    slope_side = (slope[:, 0:128], slope[:, 128:256])
    put_shifted(slope_rows, slope[:, 256 : 256 + cols], 2, 1, *slope_side, feat, cols)
    put_shifted(slope_rows, slope[:, 256 + cols :], rows + 3, 1, *slope_side, feat, cols)

    for row in (1, rows + 3):
        slope_own[:, span(row, 2, cols)] = jnp.zeros((feat, 2 * cols), BF16)
    grad_head = jnp.zeros((feat, GROUP), F32)
    loss_sum = jnp.zeros((1, 1), F32)
    for row in range(3, rows + 3, step):
        pre = conv_rows(two_main, hidden_rows, row, step, cols)
        label = label_rows(band_rows, bands, row, step, cols)
        skip, error, slope, loss = head_stage(pre, label, None, head_pad[...], head_turn[...], classes)
        skip_out[:, span(row - 3, step, cols)] = skip
        slope_own[:, span(row, step, cols)] = slope
        grad_head = grad_head + dot_nt(skip, error)
        put_shifted(slope_rows, slope, row, step, *slope_side, feat, cols)
        loss_sum = loss_sum + jnp.sum(loss, axis=1, keepdims=True)

    def grad_of(product):
        total = None
        for row in range(2, rows + 4, 11):
            count = min(11, rows + 4 - row)
            term = product(below_above(slope_own, row, count, cols), span(row, count, cols))
            total = term if total is None else total + term
        return total

    sums[...] = jnp.zeros_like(sums)
    sums[:, 0 : 3 * feat] = grad_of(lambda slopes, at: dot_nt(slopes, hidden_rows[:, at]))
    for row in range(3, rows + 3, step):
        back = conv_rows(two_back, slope_rows, row, step, cols)
        slope_own[:, span(row, step, cols)] = (back * rate[:, span(row - 3, step, cols)]).astype(BF16)
    sums[:, 3 * feat : 3 * feat + 3 * GROUP] = grad_of(lambda slopes, at: dot_nt(slopes, band_rows[:, at]))
    at = 3 * feat + 3 * GROUP
    sums[0:feat, at : at + GROUP] = grad_head
    sums[feat : feat + 1, at : at + 1] = loss_sum
    half = 3 * feat // 2
    core = lon % 2
    keep_out[...] = sums[pl.ds(pl.multiple_of(core * half, 8), half), :]
    send_out[...] = sums[pl.ds(pl.multiple_of((1 - core) * half, 8), half), :]


def finish_kernel(pixels, me_ref, own, mate, grad_one, grad_two, grad_head, loss, sums):
    half = own.shape[0]
    feat = grad_two.shape[1]
    bands = grad_one.shape[1]
    classes = grad_head.shape[0]
    core = me_ref[0] % 2
    scale = 1.0 / pixels
    sums[pl.ds(pl.multiple_of(core * half, 8), half), :] = own[...] * scale
    sums[pl.ds(pl.multiple_of((1 - core) * half, 8), half), :] = mate[...] * scale
    at = 3 * feat
    turned = jnp.transpose(sums[:, at : at + 3 * GROUP + GROUP])
    for tap in range(9):
        u, v = tap // 3, tap % 3
        grad_two[tap] = sums[u * feat : (u + 1) * feat, v * feat : (v + 1) * feat]
        grad_one[tap] = turned[v * GROUP : v * GROUP + bands, u * feat : (u + 1) * feat]
    grad_head[...] = turned[3 * GROUP : 3 * GROUP + classes, 0:feat]
    loss_row = turned[3 * GROUP : 3 * GROUP + 1]
    loss[...] = loss_row[:, feat : feat + 1] + loss_row[:, feat + GROUP : feat + GROUP + 1]


def tree_sum(values):
    values = list(values)
    while len(values) > 1:
        values = [values[i] + values[i + 1] for i in range(0, len(values), 2)]
    return values[0]


def body(
    patches,
    requests,
    footprint,
    weight_index,
    composite_weights,
    labels,
    conv1_weight,
    conv2_weight,
    head_weight,
):
    lon_count = lax.axis_size("lon")
    lat_count = lax.axis_size("lat")
    chips = lon_count // 2
    rows, slots = footprint.shape
    cols = labels.shape[1]
    store, row_width = patches.shape
    bands = row_width // cols
    bucket = requests.shape[1] // lon_count
    feat = conv2_weight.shape[1]
    classes = head_weight.shape[0]
    vmem = pl.BlockSpec(memory_space=pltpu.VMEM)
    smem = pl.BlockSpec(memory_space=pltpu.SMEM)

    lon = lax.axis_index("lon")
    place = jnp.stack([lax.axis_index("lat"), lon]).astype(jnp.int32)
    me = lon.astype(jnp.int32).reshape(1)

    def by_lon(value, move):
        return lax.ppermute(value, "lon", [(i, i ^ move) for i in range(lon_count)])

    hbm = pl.BlockSpec(memory_space=pltpu.HBM)
    in_hbm = lambda value: pltpu.with_memory_space_constraint(value, pltpu.HBM)
    plan, tile_labels = call(
        functools.partial(plan_kernel, store),
        [struct((lon_count, 16, 128), F32), struct((rows, cols), F32)],
        [
            pltpu.VMEM(requests.shape, jnp.int32),
            pltpu.VMEM((slots, rows), jnp.int32),
            pltpu.VMEM((slots, rows), jnp.int32),
            pltpu.SMEM(composite_weights.shape, F32),
            pltpu.VMEM(labels.shape, jnp.int32),
            pltpu.SemaphoreType.DMA((5,)),
        ],
        vmem_limit=63 * 1024 * 1024,
        in_specs=[hbm] * 5,
    )(requests, footprint.T, weight_index.T, composite_weights, labels)
    plan, patches = lax.optimization_barrier((plan, patches))
    mate_patches = by_lon(patches, 1)
    plans = lax.all_to_all(plan, "lon", split_axis=0, concat_axis=0, tiled=True)
    stored, edge = call(
        functools.partial(store_kernel, bands),
        [struct((2 * store, row_width), BF16), struct((6 * GROUP, 2 * store), BF16)],
        [pltpu.SemaphoreType.DMA],
        in_specs=[smem, hbm, vmem],
        cost_estimate=pl.CostEstimate(flops=10**9, bytes_accessed=10**7, transcendentals=0),
    )(me, in_hbm(patches), mate_patches)
    plans, stored, edge = lax.optimization_barrier((plans, stored, edge))
    moves = list(range(chips - 1, -1, -1))
    small_lines = 2 * ENDS * bands + 3 * GROUP
    cost = pl.CostEstimate(flops=10**9, bytes_accessed=10**7, transcendentals=0)
    row_weights, *smalls = call(
        functools.partial(ends_part_kernel, moves, bands),
        [struct((chips, rows, 2 * store), F32)]
        + [struct((small_lines, cols), BF16 if move else F32) for move in moves],
        [
            pltpu.VMEM((chips, 2 * store, 2 * rows), F32),
            pltpu.VMEM((chips + 2, 6 * GROUP, 2 * rows), F32),
            pltpu.VMEM((2 * ENDS * chips, row_width), F32),
            pltpu.VMEM((2 * ENDS * bands, cols), F32),
        ],
        in_specs=[smem, vmem, vmem, vmem],
        cost_estimate=cost,
    )(me, plans, stored, edge)
    smalls = [by_lon(small, 2 * move) if move else small for move, small in zip(moves, smalls)]
    parts = []
    for some in (moves[:-1], moves[-1:]):
        if len(some) == 1:
            row_weights, *smalls = lax.optimization_barrier((row_weights, *smalls))
        parts += call(
            functools.partial(part_kernel, [moves.index(move) for move in some]),
            [struct((rows - 2 * ENDS, row_width), BF16 if move else F32) for move in some],
            in_specs=[vmem, vmem],
            cost_estimate=cost,
        )(stored, row_weights)
    parts = [by_lon(part, 2 * move) if move else part for move, part in zip(moves, parts)]
    upper, lower = call(
        functools.partial(ends_kernel, bands),
        [struct((GROUP, 3 * cols + 128), BF16)] * 2,
        [pltpu.VMEM((small_lines, cols), F32), pltpu.VMEM((GROUP, 128), F32)],
        in_specs=[smem] + [vmem] * (2 + chips),
        cost_estimate=pl.CostEstimate(flops=3 * 10**10, bytes_accessed=10**7, transcendentals=0),
    )(me, plans, tile_labels, *smalls)
    main, strips = call(
        functools.partial(composite_kernel, bands),
        [struct((GROUP, rows * cols), BF16), struct((10 * GROUP, 128), BF16)],
        [pltpu.VMEM(((GROUP + 1) * rows, cols), F32), pltpu.VMEM((10 * GROUP, 128), F32)],
        in_specs=[smem] + [vmem] * (2 + 2 * chips),
        cost_estimate=cost,
    )(me, plans, tile_labels, *parts, *smalls)
    below = lax.ppermute(upper, "lat", [(i + 1, i) for i in range(lat_count - 1)])
    above = lax.ppermute(lower, "lat", [(i, i + 1) for i in range(lat_count - 1)])

    one_main, one_strip, two_main, two_back, head_pad, head_turn = call(
        weights_kernel,
        [
            struct((feat, 9 * GROUP), BF16),
            struct((feat, 9 * GROUP), BF16),
            struct((3 * feat, 3 * feat), BF16),
            struct((3 * feat, 3 * feat), BF16),
            struct((GROUP, feat), BF16),
            struct((feat, GROUP), BF16),
        ],
        [
            pltpu.VMEM((9 * GROUP, feat), F32),
            pltpu.VMEM((128, 128), F32),
            pltpu.VMEM(conv2_weight.shape, BF16),
            pltpu.SemaphoreType.DMA,
        ],
        in_specs=[vmem, hbm, vmem],
    )(conv1_weight.transpose(0, 2, 1), in_hbm(conv2_weight), head_weight)

    ext = rows + 6
    half = 3 * feat // 2
    sum_width = 3 * feat + 4 * GROUP
    skip, keep, send = call(
        functools.partial(network_kernel, bands, classes, rows, cols, lat_count, lon_count, 32),
        [
            struct((feat, rows * cols), BF16),
            struct((half, sum_width), F32),
            struct((half, sum_width), F32),
        ],
        [
            pltpu.VMEM((3 * GROUP, ext * cols), BF16),
            pltpu.VMEM((10 * GROUP, 128), F32),
            pltpu.VMEM((3 * feat, ext * cols), BF16),
            pltpu.VMEM((feat, rows * cols), F32),
            pltpu.VMEM((3 * feat, ext * cols), BF16),
            pltpu.VMEM((feat, ext * cols), BF16),
            pltpu.VMEM((3 * feat, sum_width), F32),
        ],
        in_specs=[smem] + [vmem] * 10,
    )(
        place, main, strips, above, below,
        one_main, one_strip, two_main, two_back, head_pad, head_turn,
    )

    last = sum_width - 128
    row_id, lane_id = iota((2 * GROUP, 128), 0), iota((2 * GROUP, 128), 1)
    at_loss = lane_id == 3 * feat + 3 * GROUP - last
    at_loss, at_rest = at_loss & (row_id == 0), at_loss & (row_id == GROUP)

    def sum_over(value, axis, moves):
        tile = value[feat : feat + 2 * GROUP, last:]
        tile = jnp.where(at_loss, tile + jnp.roll(tile, GROUP, axis=0), tile)
        rest = jnp.roll(tile - lax.reduce_precision(tile, 8, 7), GROUP, axis=0)
        tile = jnp.where(at_rest, rest, tile)
        rounded = lax.reduce_precision(lax.dynamic_update_slice(value, tile, (feat, last)), 8, 7)
        sent = rounded.astype(BF16)
        size = lax.axis_size(axis)
        terms = [rounded]
        for move in moves:
            terms.append(lax.ppermute(sent, axis, [(i, i ^ move) for i in range(size)]).astype(F32))
        return tree_sum(terms)

    total = keep + by_lon(send, 1)
    total = sum_over(total, "lon", range(2, lon_count, 2))
    total = sum_over(total, "lat", range(1, lat_count))
    other = by_lon(total, 1)
    pixels = rows * cols * lat_count * lon_count
    grad_one, grad_two, grad_head, loss = call(
        functools.partial(finish_kernel, pixels),
        [
            struct((9, bands, feat), F32),
            struct((9, feat, feat), F32),
            struct((classes, feat), F32),
            struct((1, 1), F32),
        ],
        [pltpu.VMEM((3 * feat, sum_width), F32)],
        in_specs=[smem, vmem, vmem],
    )(me, total, other)
    return skip.reshape(feat, rows, cols), grad_one.transpose(0, 2, 1), grad_two, grad_head, loss.reshape(())


def solution(mesh):
    placed = (
        P(("lat", "lon"), None),
        P("lat", "lon"),
        P("lat", "lon"),
        P("lat", "lon"),
        P(),
        P("lat", "lon"),
        P(),
        P(),
        P(),
    )
    return jax.shard_map(
        body,
        mesh=mesh,
        in_specs=placed,
        out_specs=(P(None, "lat", "lon"), P(), P(), P(), P()),
        check_vma=False,
    )
```
